256 devices in a mesh: lon: 32 (over x, y, z_lo), lat: 4 (over z_hi), grp: 2 (over core).
Axes of the slice: x: 4, y: 4, z: 8 (z_hi: 4, z_lo: 2; z = z_hi * 2 + z_lo), core: 2. Of those that a mesh axis runs over, the one named last changes fastest.
Arguments:
- thermal_anomaly: float32 [12, 512, 2048], P(None, ('lon', 'grp'), 'lat'), may hold values from -6 to 6
- saltiness_anomaly: float32 [12, 512, 2048], P(None, ('lon', 'grp'), 'lat'), may hold values from -6 to 6
- zonal_flow_speed: float32 [12, 512, 2048], P(None, ('lon', 'grp'), 'lat'), may hold values from -3 to 3
- meridional_flow_speed: float32 [12, 512, 2048], P(None, ('lon', 'grp'), 'lat'), may hold values from -3 to 3
- water_indicator: int32 [512, 2048], P(('lon', 'grp'), 'lat'), may hold values from 0 to 1
- kernel_factors: float32 [64, 3, 3, 48], replicated, may hold values from -0.3125 to 0.3125
- hidden_pointwise_factors: float32 [64, 64], replicated, may hold values from -0.75 to 0.75
- final_pointwise_factors: float32 [48, 64], replicated, may hold values from -0.75 to 0.75
Outputs:
- temperature_out: float32 [12, 512, 2048], P(None, ('lon', 'grp'), 'lat')
- salinity_out: float32 [12, 512, 2048], P(None, ('lon', 'grp'), 'lat')
- conv_out: float32 [64, 3, 3, 48], replicated
- mix_out: float32 [64, 64], replicated
- out_out: float32 [48, 64], replicated
The draws below stay inside these ranges and needn't reach their ends.
All inputs are finite; a program needn't handle non-finite values.
Results may differ from the reference program's by a relative error of at most 0.0003.
Values sent between devices are 32-bit elements; how exact they have to be, the bound alone decides.
No kernel may reach another device: no remote copies, remote signals or barrier semaphores. Data moves between devices by JAX's collectives and lax.ppermute only.
A program may use at most 64 MiB of HBM per device.

```python
import jax
import jax.numpy as jnp
from jax import lax

VERTICAL_COUNT = 12
HID = 64
CIN = 48
COUT = 48
PARALLEL_COUNT = 512
MERIDIAN_COUNT = 2048


def draw_water_indicator(key, part):
    key = jax.random.fold_in(key, 7)
    drawn = jax.random.randint(key, (PARALLEL_COUNT, MERIDIAN_COUNT), 0, 100)
    longitude = jnp.arange(PARALLEL_COUNT, dtype=jnp.int32)[:, None]
    threshold = 30 + 60 * longitude // PARALLEL_COUNT
    return (drawn < threshold).astype(jnp.int32)


def block_levels(own_key, extent, shards, least, largest):
    factor_of = 1.0
    for axis_at, blocks in shards:
        steps = jax.random.uniform(jax.random.fold_in(jax.random.fold_in(own_key, 6), axis_at), (blocks,), jnp.float32, least / len(shards), largest / len(shards))
        factor_of = factor_of * jnp.repeat(jnp.exp(steps), extent[axis_at] // blocks).reshape((-1,) + (1,) * (len(extent) - 1 - axis_at))
    return factor_of


def normal_values(rng, extent, deviation, reach, shards=(), kind=jnp.bfloat16):
    entries = deviation * jax.random.normal(rng, extent, jnp.float32)
    if shards:
        entries = entries * block_levels(rng, extent, shards, -0.22, 0.18)
    return jnp.clip(entries, -reach, reach).astype(kind)


def setup_inputs(seed: int = 0) -> dict:
    seeds = jax.random.split(jax.random.key(seed), 9)
    return {
        "thermal_anomaly": normal_values(seeds[0], (VERTICAL_COUNT, PARALLEL_COUNT, MERIDIAN_COUNT), 1.0, 6.0, ((1, 64), (2, 4)), jnp.float32),
        "saltiness_anomaly": normal_values(seeds[1], (VERTICAL_COUNT, PARALLEL_COUNT, MERIDIAN_COUNT), 1.0, 6.0, ((1, 64), (2, 4)), jnp.float32),
        "zonal_flow_speed": normal_values(seeds[2], (VERTICAL_COUNT, PARALLEL_COUNT, MERIDIAN_COUNT), 0.6, 3.0, ((1, 64), (2, 4)), jnp.float32),
        "meridional_flow_speed": normal_values(seeds[3], (VERTICAL_COUNT, PARALLEL_COUNT, MERIDIAN_COUNT), 0.6, 3.0, ((1, 64), (2, 4)), jnp.float32),
        "water_indicator": draw_water_indicator(jax.random.fold_in(seeds[8], 71), 0),
        "kernel_factors": normal_values(seeds[5], (HID, 3, 3, CIN), (9 * CIN) ** -0.5, 0.3125, (), jnp.float32),
        "hidden_pointwise_factors": normal_values(seeds[6], (HID, HID), HID ** -0.5, 0.75, (), jnp.float32),
        "final_pointwise_factors": normal_values(seeds[7], (COUT, HID), HID ** -0.5, 0.75, (), jnp.float32),
    }


time_step = 0.2
diffusivity = 0.5
learn_rate = 200.0
highest = lax.Precision.HIGHEST


def attach_halo(field, width):
    wrapped = jnp.concatenate([field[..., -width:, :], field, field[..., :width, :]], axis=-2)
    zeros = jnp.zeros(wrapped.shape[:-1] + (width,), wrapped.dtype)
    return jnp.concatenate([zeros, wrapped, zeros], axis=-1)


def average_to_blocks(field):
    array_extent = field.shape
    return field.reshape(array_extent[:-2] + (array_extent[-2] // 4, 4, array_extent[-1] // 4, 4)).mean(axis=(-3, -1))


def upsample_blocks(field):
    return jnp.repeat(jnp.repeat(field, 4, axis=-2), 4, axis=-1)


def scalar_step_update(tracer, haloed_scalar, padded_eastward, padded_northward, padded_land_mask, forcing):
    west_side = haloed_scalar[..., :-1, 1:-1]
    east_side = haloed_scalar[..., 1:, 1:-1]
    east_flux = padded_land_mask[:-1, 1:-1] * padded_land_mask[1:, 1:-1] * (
        0.25 * (padded_eastward[..., :-1, 1:-1] + padded_eastward[..., 1:, 1:-1]) * (west_side + east_side)
        - diffusivity * (east_side - west_side))
    south_side = haloed_scalar[..., 1:-1, :-1]
    north_side = haloed_scalar[..., 1:-1, 1:]
    north_flux = padded_land_mask[1:-1, :-1] * padded_land_mask[1:-1, 1:] * (
        0.25 * (padded_northward[..., 1:-1, :-1] + padded_northward[..., 1:-1, 1:]) * (south_side + north_side)
        - diffusivity * (north_side - south_side))
    tendency = forcing - (east_flux[..., 1:, :] - east_flux[..., :-1, :]) - (north_flux[..., 1:] - north_flux[..., :-1])
    return tracer + time_step * padded_land_mask[1:-1, 1:-1] * tendency


def patches(padded, rows, columns):
    pieces = [padded[:, offset_x:offset_x + rows, offset_y:offset_y + columns]
              for offset_x in range(3) for offset_y in range(3)]
    return jnp.stack(pieces, 0).reshape(9 * padded.shape[0], rows * columns)


def network(present_kernel_result, present_hidden_result, present_final_result, patch_rows):
    flat_conv = present_kernel_result.reshape(present_kernel_result.shape[0], -1)
    hidden_one = jnp.tanh(jnp.dot(flat_conv, patch_rows, precision=highest))
    hidden_two = jnp.tanh(jnp.dot(present_hidden_result, hidden_one, precision=highest))
    predicted = jnp.dot(present_final_result, hidden_two, precision=highest)
    return hidden_one, hidden_two, predicted


def subgrid_closure_term(haloed_prediction, vertical_slabs):
    parallel_divergence = haloed_prediction[:, 2:, 1:-1] - haloed_prediction[:, :-2, 1:-1]
    meridional_divergence = haloed_prediction[:, 1:-1, 2:] - haloed_prediction[:, 1:-1, :-2]
    thermal_source_term = -0.5 * (parallel_divergence[:vertical_slabs] + meridional_divergence[vertical_slabs:2 * vertical_slabs])
    salinity_source_term = -0.5 * (parallel_divergence[2 * vertical_slabs:3 * vertical_slabs] + meridional_divergence[3 * vertical_slabs:])
    return thermal_source_term, salinity_source_term


def reference(thermal_anomaly, saltiness_anomaly, zonal_flow_speed, meridional_flow_speed, water_indicator, kernel_factors, hidden_pointwise_factors, final_pointwise_factors):
    vertical_slabs = thermal_anomaly.shape[0]
    mask_field = water_indicator.astype(jnp.float32)
    padded_land_mask = attach_halo(mask_field, 1)
    ocean_weight = average_to_blocks(mask_field)
    ocean_area = jnp.sum(ocean_weight)
    blocky_zonal_flow = average_to_blocks(zonal_flow_speed)
    blocky_meridional_flow = average_to_blocks(meridional_flow_speed)
    rows, columns = ocean_weight.shape
    present_kernel_result, present_hidden_result, present_final_result = kernel_factors, hidden_pointwise_factors, final_pointwise_factors

    def integrate_steps(tracer, forcing):
        def level_step(pieces):
            tracer_level, zonal_level, merid_level, force_level = pieces
            return scalar_step_update(tracer_level, attach_halo(tracer_level, 1), attach_halo(zonal_level, 1),
                               attach_halo(merid_level, 1), padded_land_mask, upsample_blocks(force_level))
        return lax.map(level_step, (tracer, zonal_flow_speed, meridional_flow_speed, forcing))

    for turn_index in range(2):
        blocky_heat_field = average_to_blocks(thermal_anomaly)
        blocky_salinity_sum = average_to_blocks(saltiness_anomaly)
        network_features = jnp.concatenate([blocky_heat_field, blocky_salinity_sum, blocky_zonal_flow, blocky_meridional_flow], 0)
        target = jnp.concatenate([
            average_to_blocks(zonal_flow_speed * thermal_anomaly) - blocky_zonal_flow * blocky_heat_field,
            average_to_blocks(meridional_flow_speed * thermal_anomaly) - blocky_meridional_flow * blocky_heat_field,
            average_to_blocks(zonal_flow_speed * saltiness_anomaly) - blocky_zonal_flow * blocky_salinity_sum,
            average_to_blocks(meridional_flow_speed * saltiness_anomaly) - blocky_meridional_flow * blocky_salinity_sum], 0)
        patch_rows = patches(attach_halo(network_features, 1), rows, columns)
        hidden_one, hidden_two, predicted = network(present_kernel_result, present_hidden_result, present_final_result, patch_rows)
        reformed_values = predicted.reshape(predicted.shape[0], rows, columns)
        thermal_source_term, salinity_source_term = subgrid_closure_term(attach_halo(reformed_values, 1), vertical_slabs)
        thermal_anomaly = integrate_steps(thermal_anomaly, thermal_source_term)
        saltiness_anomaly = integrate_steps(saltiness_anomaly, salinity_source_term)
        loss_scale = 2.0 / (predicted.shape[0] * ocean_area)
        misfit = predicted - target.reshape(predicted.shape[0], -1)
        back_out = loss_scale * ocean_weight.reshape(-1) * misfit
        grad_out = jnp.dot(back_out, hidden_two.T, precision=highest)
        back_two = jnp.dot(present_final_result.T, back_out, precision=highest) * (1.0 - hidden_two * hidden_two)
        grad_mix = jnp.dot(back_two, hidden_one.T, precision=highest)
        back_one = jnp.dot(present_hidden_result.T, back_two, precision=highest) * (1.0 - hidden_one * hidden_one)
        grad_conv = jnp.dot(back_one, patch_rows.T, precision=highest).reshape(present_kernel_result.shape)
        present_kernel_result = present_kernel_result - learn_rate * grad_conv
        present_hidden_result = present_hidden_result - learn_rate * grad_mix
        present_final_result = present_final_result - learn_rate * grad_out
    return thermal_anomaly, saltiness_anomaly, present_kernel_result, present_hidden_result, present_final_result
```

```python
import jax
import jax.numpy as jnp
from jax import lax
from jax.sharding import PartitionSpec as P

time_step = 0.2
diffusivity = 0.5
learn_rate = 200.0
highest = lax.Precision.HIGHEST


def with_halo(block, sides, width):
    for axis, dim in sides:
        count = lax.axis_size(axis)
        forward = [(i, i + 1) for i in range(count - 1)]
        forward.append((count - 1, 0))
        backward = [(target, source) for source, target in forward]
        low = lax.ppermute(
            lax.slice_in_dim(block, block.shape[dim] - width, None, axis=dim), axis, forward
        )
        high = lax.ppermute(lax.slice_in_dim(block, 0, width, axis=dim), axis, backward)
        block = jnp.concatenate([low, block, high], axis=dim)
    return block


def clear_rim(padded, width):
    lat_index = lax.axis_index("lat")
    lat_last = lax.axis_size("lat") - 1
    columns = jnp.arange(padded.shape[-1])
    low_rim = (columns < width) & (lat_index == 0)
    high_rim = (columns >= padded.shape[-1] - width) & (lat_index == lat_last)
    return jnp.where(low_rim | high_rim, jnp.zeros((), padded.dtype), padded)


def detailed_haloed_field(stacked):
    return clear_rim(with_halo(stacked, ((("lon", "grp"), 1), ("lat", 2)), 1), 1)


def average_to_blocks(field):
    array_extent = field.shape
    return field.reshape(
        array_extent[:-2] + (array_extent[-2] // 4, 4, array_extent[-1] // 4, 4)
    ).mean(axis=(-3, -1))


def upsample_blocks(field):
    return jnp.repeat(jnp.repeat(field, 4, axis=-2), 4, axis=-1)


def scalar_step_update(
    tracer, haloed_scalar, padded_eastward, padded_northward, padded_land_mask, forcing
):
    west_side = haloed_scalar[..., :-1, 1:-1]
    east_side = haloed_scalar[..., 1:, 1:-1]
    east_flux = (
        padded_land_mask[:-1, 1:-1]
        * padded_land_mask[1:, 1:-1]
        * (
            0.25
            * (padded_eastward[..., :-1, 1:-1] + padded_eastward[..., 1:, 1:-1])
            * (west_side + east_side)
            - diffusivity * (east_side - west_side)
        )
    )
    south_side = haloed_scalar[..., 1:-1, :-1]
    north_side = haloed_scalar[..., 1:-1, 1:]
    north_flux = (
        padded_land_mask[1:-1, :-1]
        * padded_land_mask[1:-1, 1:]
        * (
            0.25
            * (padded_northward[..., 1:-1, :-1] + padded_northward[..., 1:-1, 1:])
            * (south_side + north_side)
            - diffusivity * (north_side - south_side)
        )
    )
    tendency = (
        forcing
        - (east_flux[..., 1:, :] - east_flux[..., :-1, :])
        - (north_flux[..., 1:] - north_flux[..., :-1])
    )
    return tracer + time_step * padded_land_mask[1:-1, 1:-1] * tendency


def patches(padded, rows, columns):
    pieces = [
        padded[:, offset_x : offset_x + rows, offset_y : offset_y + columns]
        for offset_x in range(3)
        for offset_y in range(3)
    ]
    return jnp.stack(pieces, 0).reshape(9 * padded.shape[0], rows * columns)


def network(present_kernel_result, present_hidden_result, present_final_result, patch_rows):
    flat_conv = present_kernel_result.reshape(present_kernel_result.shape[0], -1)
    hidden_one = jnp.tanh(jnp.dot(flat_conv, patch_rows, precision=highest))
    hidden_two = jnp.tanh(jnp.dot(present_hidden_result, hidden_one, precision=highest))
    predicted = jnp.dot(present_final_result, hidden_two, precision=highest)
    return (hidden_one, hidden_two, predicted)


def subgrid_closure_term(haloed_prediction, vertical_slabs):
    parallel_divergence = haloed_prediction[:, 2:, 1:-1] - haloed_prediction[:, :-2, 1:-1]
    meridional_divergence = haloed_prediction[:, 1:-1, 2:] - haloed_prediction[:, 1:-1, :-2]
    thermal_source_term = -0.5 * (
        parallel_divergence[:vertical_slabs]
        + meridional_divergence[vertical_slabs : 2 * vertical_slabs]
    )
    salinity_source_term = -0.5 * (
        parallel_divergence[2 * vertical_slabs : 3 * vertical_slabs]
        + meridional_divergence[3 * vertical_slabs :]
    )
    return (thermal_source_term, salinity_source_term)


def flipped(axis, mask):
    return [(i, i ^ mask) for i in range(lax.axis_size(axis))]


def exchanged_sum(value, axis, masks):
    parts = [lax.ppermute(value, axis, flipped(axis, mask)) for mask in masks]
    if len(parts) == 1:
        return value + parts[0]
    return (value + parts[0]) + (parts[1] + parts[2])


def sum_over_devices(packed):
    half = packed.shape[0] // 2
    core = lax.axis_index("grp")
    other = lax.dynamic_slice_in_dim(packed, (1 - core) * half, half, 0)
    own = lax.dynamic_slice_in_dim(packed, core * half, half, 0)
    part = own + lax.ppermute(other, "grp", flipped("grp", 1))
    part = exchanged_sum(part, "lon", (1,))
    part = exchanged_sum(part, "lon", (2, 4, 6))
    part = exchanged_sum(part, "lon", (8, 16, 24))
    part = exchanged_sum(part, "lat", (1, 2, 3))
    back = lax.ppermute(part, "grp", flipped("grp", 1))
    first = jnp.where(core == 0, part, back)
    second = jnp.where(core == 0, back, part)
    return jnp.concatenate([first, second], 0)


def shards(
    thermal_anomaly,
    saltiness_anomaly,
    zonal_flow_speed,
    meridional_flow_speed,
    water_indicator,
    kernel_factors,
    hidden_pointwise_factors,
    final_pointwise_factors,
):
    vertical_slabs = thermal_anomaly.shape[0]
    mask_field = water_indicator.astype(jnp.float32)
    static_pad = detailed_haloed_field(
        jnp.concatenate([zonal_flow_speed, meridional_flow_speed, mask_field[None]], 0)
    )
    padded_eastward = static_pad[:vertical_slabs]
    padded_northward = static_pad[vertical_slabs : 2 * vertical_slabs]
    padded_land_mask = static_pad[2 * vertical_slabs]
    ocean_weight = average_to_blocks(mask_field)
    local_area = jnp.sum(ocean_weight)
    blocky_zonal_flow = average_to_blocks(zonal_flow_speed)
    blocky_meridional_flow = average_to_blocks(meridional_flow_speed)
    coarse_rows, coarse_columns = ocean_weight.shape
    present_kernel_result, present_hidden_result, present_final_result = (
        kernel_factors,
        hidden_pointwise_factors,
        final_pointwise_factors,
    )
    channels_out = final_pointwise_factors.shape[0]
    for turn_index in range(2):
        blocky_heat_field = average_to_blocks(thermal_anomaly)
        blocky_salinity_sum = average_to_blocks(saltiness_anomaly)
        network_features = jnp.concatenate(
            [blocky_heat_field, blocky_salinity_sum, blocky_zonal_flow, blocky_meridional_flow], 0
        )
        target = jnp.concatenate(
            [
                average_to_blocks(zonal_flow_speed * thermal_anomaly)
                - blocky_zonal_flow * blocky_heat_field,
                average_to_blocks(meridional_flow_speed * thermal_anomaly)
                - blocky_meridional_flow * blocky_heat_field,
                average_to_blocks(zonal_flow_speed * saltiness_anomaly)
                - blocky_zonal_flow * blocky_salinity_sum,
                average_to_blocks(meridional_flow_speed * saltiness_anomaly)
                - blocky_meridional_flow * blocky_salinity_sum,
            ],
            0,
        )
        input_pad = clear_rim(with_halo(network_features, ((("lon", "grp"), 1), ("lat", 2)), 1), 1)
        rows, columns = (coarse_rows, coarse_columns)
        patch_rows = patches(input_pad, rows, columns)
        hidden_one, hidden_two, predicted = network(
            present_kernel_result, present_hidden_result, present_final_result, patch_rows
        )
        reformed_values = predicted.reshape(channels_out, rows, columns)
        haloed_prediction = clear_rim(
            with_halo(reformed_values, ((("lon", "grp"), 1), ("lat", 2)), 1), 1
        )
        thermal_source_term, salinity_source_term = subgrid_closure_term(
            haloed_prediction, vertical_slabs
        )
        haloed_scalar = detailed_haloed_field(
            jnp.concatenate([thermal_anomaly, saltiness_anomaly], 0)
        )
        thermal_anomaly = scalar_step_update(
            thermal_anomaly,
            haloed_scalar[:vertical_slabs],
            padded_eastward,
            padded_northward,
            padded_land_mask,
            upsample_blocks(thermal_source_term),
        )
        saltiness_anomaly = scalar_step_update(
            saltiness_anomaly,
            haloed_scalar[vertical_slabs:],
            padded_eastward,
            padded_northward,
            padded_land_mask,
            upsample_blocks(salinity_source_term),
        )
        misfit = predicted - target.reshape(channels_out, -1)
        back_out = ocean_weight.reshape(-1) * misfit
        grad_out = jnp.dot(hidden_two, back_out.T, precision=highest)
        back_two = jnp.dot(present_final_result.T, back_out, precision=highest) * (
            1.0 - hidden_two * hidden_two
        )
        grad_mix = jnp.dot(back_two, hidden_one.T, precision=highest)
        back_one = jnp.dot(present_hidden_result.T, back_two, precision=highest) * (
            1.0 - hidden_one * hidden_one
        )
        grad_conv = jnp.dot(back_one, patch_rows.T, precision=highest)
        hidden = grad_conv.shape[0]
        area_column = jnp.full((hidden, 1), local_area, jnp.float32)
        packed = jnp.concatenate([grad_conv, grad_mix, grad_out, area_column], 1)
        used = packed.shape[1]
        packed = jnp.pad(packed, ((0, 0), (0, -used % 128)))
        total = sum_over_devices(packed)
        conv_end = grad_conv.shape[1]
        mix_end = conv_end + hidden
        step = (learn_rate * 2.0 / channels_out) / total[0, used - 1]
        present_kernel_result = present_kernel_result - step * total[:, :conv_end].reshape(
            present_kernel_result.shape
        )
        present_hidden_result = present_hidden_result - step * total[:, conv_end:mix_end]
        present_final_result = present_final_result - step * total[:, mix_end : used - 1].T
    return (
        thermal_anomaly,
        saltiness_anomaly,
        present_kernel_result,
        present_hidden_result,
        present_final_result,
    )


def solution(mesh):
    placed = (
        P(None, ("lon", "grp"), "lat"),
        P(None, ("lon", "grp"), "lat"),
        P(None, ("lon", "grp"), "lat"),
        P(None, ("lon", "grp"), "lat"),
        P(("lon", "grp"), "lat"),
        P(),
        P(),
        P(),
    )
    return jax.shard_map(
        shards,
        mesh=mesh,
        in_specs=placed,
        out_specs=(P(None, ("lon", "grp"), "lat"), P(None, ("lon", "grp"), "lat"), P(), P(), P()),
        check_vma=False,
    )
```

```python
import functools

import jax
import jax.numpy as jnp
from jax import lax
from jax.experimental import pallas as pl
from jax.experimental.pallas import tpu as pltpu
from jax.sharding import PartitionSpec as P

time_step = 0.2
diffusivity = 0.5
learn_rate = 200.0
highest = lax.Precision.HIGHEST
f32 = jnp.float32
bf16 = jnp.bfloat16

LEVELS = 12
CHANNELS = 4 * LEVELS
HIDDEN = 64
TAPS = 9 * CHANNELS
MIX_AT = 512
OUT_AT = 576
AREA_AT = 624
PACKED = 640
FINE = 512
COARSE = 128
VMEM_LIMIT = 48 * 1024 * 1024


def struct(*shape):
    return jax.ShapeDtypeStruct(shape, f32)


def call(kernel, outs, *args, scratch=(), smem=0, flops=0, bytes_accessed=0):
    specs = [pl.BlockSpec(memory_space=pltpu.SMEM)] * smem
    specs += [pl.BlockSpec(memory_space=pltpu.VMEM)] * (len(args) - smem)
    return pl.pallas_call(
        kernel,
        out_shape=outs,
        in_specs=specs,
        out_specs=[pl.BlockSpec(memory_space=pltpu.VMEM)] * len(outs),
        scratch_shapes=scratch,
        compiler_params=pltpu.CompilerParams(vmem_limit_bytes=VMEM_LIMIT),
        cost_estimate=pl.CostEstimate(
            flops=flops, bytes_accessed=bytes_accessed, transcendentals=0
        ),
    )(*args)


def exact_dot(value, selector):
    high = value.astype(bf16)
    rest = value - high.astype(f32)
    middle = rest.astype(bf16)
    low = (rest - middle.astype(f32)).astype(bf16)
    dot = functools.partial(jnp.dot, preferred_element_type=f32)
    return (dot(low, selector) + dot(middle, selector)) + dot(high, selector)


def pooling_matrix():
    fine = lax.broadcasted_iota(jnp.int32, (FINE, COARSE), 0) >> 2
    coarse = lax.broadcasted_iota(jnp.int32, (FINE, COARSE), 1)
    return jnp.where(fine == coarse, f32(1.0 / 16.0), f32(0.0)).astype(bf16)


def spreading_matrix():
    fine = lax.broadcasted_iota(jnp.int32, (COARSE, FINE), 1) >> 2
    coarse = lax.broadcasted_iota(jnp.int32, (COARSE, FINE), 0)
    return jnp.where(fine == coarse, f32(1.0), f32(0.0)).astype(bf16)


def lane_index(shape):
    return lax.broadcasted_iota(jnp.int32, shape, len(shape) - 1)


def fill_blocks(blocks, refs):
    for which, ref in enumerate(refs):
        for block in range(4):
            start = (4 * which + block) * 8 * LEVELS
            blocks[start : start + 8 * LEVELS, :] = ref[:, 128 * block : 128 * (block + 1)]


def longitude_row(blocks, which, block, lon):
    start = (4 * which + block) * 8 * LEVELS + lon
    return blocks[pl.ds(start, LEVELS, stride=8), :]


def coarsen(blocks, sums_ref, x_ref, target_ref, low_ref, high_ref):
    for row in range(2):
        for block in range(4):
            total = None
            for lon in range(4 * row, 4 * row + 4):
                t, s, u, v = (longitude_row(blocks, which, block, lon) for which in range(4))
                terms = (t, s, u, v, u * t, v * t, u * s, v * s)
                total = terms if total is None else [a + b for a, b in zip(total, terms)]
            for at, value in enumerate(total):
                start = 2 * CHANNELS * row + LEVELS * at
                sums_ref[start : start + LEVELS, 128 * block : 128 * (block + 1)] = value
    means = exact_dot(sums_ref[...], pooling_matrix())
    for row in range(2):
        x = means[2 * CHANNELS * row : 2 * CHANNELS * row + CHANNELS]
        products = means[2 * CHANNELS * row + CHANNELS : 2 * CHANNELS * (row + 1)]
        ct, cs, cu, cv = (x[LEVELS * k : LEVELS * (k + 1)] for k in range(4))
        x_ref[CHANNELS * row : CHANNELS * (row + 1), :] = x
        own = jnp.concatenate([cu * ct, cv * ct, cu * cs, cv * cs], 0)
        target_ref[CHANNELS * row : CHANNELS * (row + 1), :] = products - own
    turned = x_ref[...].T
    low_ref[...] = jnp.zeros(low_ref.shape, f32)
    high_ref[...] = jnp.zeros(high_ref.shape, f32)
    low_ref[0:1, 0 : 2 * CHANNELS] = turned[0:1]
    high_ref[0:1, 0 : 2 * CHANNELS] = turned[COARSE - 1 : COARSE]


def fine_edges(blocks, rows_of, mask_ref, columns_of, first_ref, last_ref, low_ref, high_ref):
    depth = first_ref.shape[0] // 4
    for lon, out in ((0, first_ref), (7, last_ref)):
        out[...] = jnp.zeros(out.shape, f32)
        for block in range(4):
            for which in range(rows_of):
                start = block * depth + which * LEVELS
                out[start : start + LEVELS, :] = longitude_row(blocks, which, block, lon)
            if mask_ref is not None:
                start = block * depth + rows_of * LEVELS
                out[start : start + 1, :] = mask_ref[lon : lon + 1, 128 * block : 128 * (block + 1)]
    low_ref[...] = jnp.zeros(low_ref.shape, f32)
    high_ref[...] = jnp.zeros(high_ref.shape, f32)
    for at, ref in enumerate(columns_of):
        size = ref.shape[0]
        low_ref[at : at + 1, 0:size] = ref[:, 0:128].T[0:1]
        high_ref[at : at + 1, 0:size] = ref[:, FINE - 128 : FINE].T[127:128]


def prepare_kernel(t, s, u, v, mask, x, target, weight, low, high, sums, blocks):
    fill_blocks(blocks, (t, s, u, v))
    coarsen(blocks, sums, x, target, low, high)
    m = mask[...].astype(f32)
    rows = jnp.concatenate(
        [jnp.sum(m[0:4], axis=0, keepdims=True), jnp.sum(m[4:8], axis=0, keepdims=True)]
        + [jnp.zeros((6, FINE), f32)],
        0,
    )
    weight[...] = jnp.dot(rows.astype(bf16), pooling_matrix(), preferred_element_type=f32)


def edges_kernel(t, s, u, v, mask, first, last, low, high, mask_values, blocks):
    mask_values[...] = mask[...].astype(f32)
    fill_blocks(blocks, (t, s, u))
    fine_edges(blocks, 3, mask_values, (t, s, v, mask_values), first, last, low, high)


def dot(a, b):
    return jnp.dot(a, b, precision=highest, preferred_element_type=f32)


def dot_nt(a, b):
    return lax.dot_general(
        a, b, (((1,), (1,)), ((), ())), precision=highest, preferred_element_type=f32
    )


def network_step(
    core, x, west, east, low, high, target, weight, packed, pred, pred_low, pred_high, own, other, taps, grads
):
    lanes = lane_index((CHANNELS, COARSE))
    corners = jnp.concatenate(
        [
            low[0:1, :],
            high[0:1, :],
            west[CHANNELS : CHANNELS + 1, :],
            west[CHANNELS + 8 : CHANNELS + 9, :],
            east[CHANNELS : CHANNELS + 1, :],
            east[CHANNELS + 8 : CHANNELS + 9, :],
            jnp.zeros((2, COARSE), f32),
        ],
        0,
    ).T
    rows = (
        (west[0:CHANNELS, :], CHANNELS, 2),
        (x[0:CHANNELS, :], 0, 0),
        (x[CHANNELS : 2 * CHANNELS, :], CHANNELS, 0),
        (east[0:CHANNELS, :], 0, 4),
    )
    for at, (value, start, column) in enumerate(rows):
        before = corners[start : start + CHANNELS, column : column + 1]
        after = corners[start : start + CHANNELS, column + 1 : column + 2]
        shifted = (
            jnp.where(lanes == 0, before, pltpu.roll(value, 1, 1)),
            value,
            jnp.where(lanes == COARSE - 1, after, pltpu.roll(value, COARSE - 1, 1)),
        )
        for row in range(2):
            tap = at - row
            if 0 <= tap < 3:
                for side in range(3):
                    begin = (3 * tap + side) * CHANNELS
                    taps[begin : begin + CHANNELS, COARSE * row : COARSE * (row + 1)] = shifted[side]
    kernel = packed[:, 0:TAPS]
    mix = packed[:, MIX_AT : MIX_AT + HIDDEN]
    out_turned = packed[:, OUT_AT : OUT_AT + CHANNELS]
    hidden_one = jnp.tanh(dot(kernel, taps[...]))
    hidden_two = jnp.tanh(dot(mix, hidden_one))
    predicted = dot(out_turned.T, hidden_two)
    pred[0:CHANNELS, :] = predicted[:, 0:COARSE]
    pred[CHANNELS : 2 * CHANNELS, :] = predicted[:, COARSE : 2 * COARSE]
    back_out = jnp.concatenate(
        [
            weight[row : row + 1, :]
            * (
                predicted[:, COARSE * row : COARSE * (row + 1)]
                - target[CHANNELS * row : CHANNELS * (row + 1), :]
            )
            for row in range(2)
        ],
        1,
    )
    back_two = dot(out_turned, back_out) * (1.0 - hidden_two * hidden_two)
    back_one = dot(mix.T, back_two) * (1.0 - hidden_one * hidden_one)
    grads[:, MIX_AT - 128 : PACKED] = jnp.zeros((HIDDEN, PACKED - MIX_AT + 128), f32)
    grads[:, 0:TAPS] = dot_nt(back_one, taps[...])
    grads[:, MIX_AT : MIX_AT + HIDDEN] = dot_nt(back_two, hidden_one)
    grads[:, OUT_AT : OUT_AT + CHANNELS] = dot_nt(hidden_two, back_out)
    area = jnp.sum(weight[0:2, :], axis=(0, 1), keepdims=True)
    grads[:, AREA_AT : AREA_AT + 1] = jnp.broadcast_to(area, (HIDDEN, 1))
    half = HIDDEN // 2
    own[...] = grads[pl.ds(pl.multiple_of(core[0] * half, half), half), :]
    other[...] = grads[pl.ds(pl.multiple_of((1 - core[0]) * half, half), half), :]
    turned = pred[...].T
    pred_low[...] = jnp.zeros(pred_low.shape, f32)
    pred_high[...] = jnp.zeros(pred_high.shape, f32)
    pred_low[0:1, 0 : 2 * CHANNELS] = turned[0:1]
    pred_high[0:1, 0 : 2 * CHANNELS] = turned[COARSE - 1 : COARSE]


def descended(core, packed, part, back):
    half = HIDDEN // 2
    mine, theirs = part[...], back[...]
    first = core[0] == 0
    total = jnp.concatenate(
        [jnp.where(first, mine, theirs), jnp.where(first, theirs, mine)], 0
    )
    area = total[0:1, AREA_AT : AREA_AT + 1]
    step = (learn_rate * 2.0 / CHANNELS) / area
    return packed[...] - step * total


def first_network_kernel(core, x, west, east, low, high, target, weight, packed, *rest):
    network_step(core, x, west, east, low, high, target, weight, packed, *rest)


def next_network_kernel(
    core, x, west, east, low, high, target, weight, packed, part, back, renewed, *rest
):
    renewed[...] = descended(core, packed, part, back)
    network_step(core, x, west, east, low, high, target, weight, renewed, *rest)


def last_kernel(core, packed, part, back, kernel, mix, out):
    renewed = descended(core, packed, part, back)
    kernel[...] = renewed[:, 0:TAPS]
    mix[...] = renewed[:, MIX_AT : MIX_AT + HIDDEN]
    out[...] = renewed[:, OUT_AT : OUT_AT + CHANNELS].T


def forcing(pred, west, east, low, high):
    before = (west[0:CHANNELS], pred[0:CHANNELS, :])
    after = (pred[CHANNELS : 2 * CHANNELS, :], east[0:CHANNELS])
    lanes = lane_index((CHANNELS, COARSE))
    pieces = []
    for row in range(2):
        value = pred[CHANNELS * row : CHANNELS * (row + 1), :]
        along = after[row] - before[row]
        south = jnp.where(lanes == 0, low[CHANNELS * row : CHANNELS * (row + 1)], pltpu.roll(value, 1, 1))
        north = jnp.where(
            lanes == COARSE - 1,
            high[CHANNELS * row : CHANNELS * (row + 1)],
            pltpu.roll(value, COARSE - 1, 1),
        )
        across = north - south
        for at in (0, 2 * LEVELS):
            pieces.append(-0.5 * (along[at : at + LEVELS] + across[at + LEVELS : at + 2 * LEVELS]))
            pieces.append(jnp.zeros((4, COARSE), f32))
    return exact_dot(jnp.concatenate(pieces, 0), spreading_matrix())


def advance(
    t, s, u, v, mask, pred, fixed_west, fixed_east, fixed_low, fixed_high, west, east, low, high, t_out, s_out
):
    m = mask[...].astype(f32)
    shape = (8, FINE)
    lanes = lane_index(shape)
    subs = lax.broadcasted_iota(jnp.int32, shape, 0)
    fixed_depth = 40
    depth = (west.shape[0] - CHANNELS) // 4

    def edge_row(ref, stride, at):
        return jnp.concatenate([ref[stride * k + at : stride * k + at + 1, :] for k in range(4)], 1)

    def neighbours_lon(value, row_west, row_east):
        return (
            jnp.where(subs == 0, row_west, pltpu.roll(value, 1, 0)),
            jnp.where(subs == 7, row_east, pltpu.roll(value, 7, 0)),
        )

    def neighbours_lat(value, column_low, column_high):
        return (
            jnp.where(lanes == 0, column_low, pltpu.roll(value, 1, 1)),
            jnp.where(lanes == FINE - 1, column_high, pltpu.roll(value, FINE - 1, 1)),
        )

    fixed_low_turned = fixed_low[0:8, :].T
    fixed_high_turned = fixed_high[0:8, :].T
    low_turned = jnp.concatenate([low[0:2, :], low[8:9, :], low[2:7, :]], 0).T
    high_turned = jnp.concatenate([high[0:2, :], high[8:9, :], high[2:7, :]], 0).T
    start = 4 * depth
    force = forcing(
        pred,
        west[start : start + CHANNELS, :],
        east[start : start + CHANNELS, :],
        low_turned[:, 2:3],
        high_turned[:, 2:3],
    )
    m_west, m_east = neighbours_lon(
        m, edge_row(fixed_west, fixed_depth, 3 * LEVELS), edge_row(fixed_east, fixed_depth, 3 * LEVELS)
    )
    m_low, m_high = neighbours_lat(m, fixed_low_turned[0:8, 3:4], fixed_high_turned[0:8, 3:4])
    open_west, open_east, open_low, open_high = m * m_west, m * m_east, m * m_low, m * m_high
    mix_west, mix_east = diffusivity * open_west, diffusivity * open_east
    mix_low, mix_high = diffusivity * open_low, diffusivity * open_high
    pace = time_step * m
    for level in range(LEVELS):
        at = slice(8 * level, 8 * (level + 1))
        u_here, v_here = u[at, :], v[at, :]
        u_west, u_east = neighbours_lon(
            u_here,
            edge_row(fixed_west, fixed_depth, 2 * LEVELS + level),
            edge_row(fixed_east, fixed_depth, 2 * LEVELS + level),
        )
        v_low, v_high = neighbours_lat(v_here, fixed_low_turned[at, 2:3], fixed_high_turned[at, 2:3])
        speed_west = 0.25 * (u_here + u_west) * open_west
        speed_east = 0.25 * (u_here + u_east) * open_east
        speed_low = 0.25 * (v_here + v_low) * open_low
        speed_high = 0.25 * (v_here + v_high) * open_high
        for which, (q_ref, out) in enumerate(((t, t_out), (s, s_out))):
            q = q_ref[at, :]
            q_west, q_east = neighbours_lon(
                q,
                edge_row(west, depth, LEVELS * which + level),
                edge_row(east, depth, LEVELS * which + level),
            )
            q_low, q_high = neighbours_lat(
                q, low_turned[at, which : which + 1], high_turned[at, which : which + 1]
            )
            flux_east = speed_east * (q + q_east) - mix_east * (q_east - q)
            flux_west = speed_west * (q_west + q) - mix_west * (q - q_west)
            flux_high = speed_high * (q + q_high) - mix_high * (q_high - q)
            flux_low = speed_low * (q_low + q) - mix_low * (q - q_low)
            row = 16 * which + level
            push = jnp.where(subs < 4, force[row : row + 1], force[32 + row : 33 + row])
            out[at, :] = q + pace * (push - (flux_east - flux_west) - (flux_high - flux_low))


def first_advance_kernel(*refs):
    ins, outs = refs[:10], refs[10:]
    t, s, u, v, mask, pred, west, east, low, high = ins
    t_out, s_out, x, target, low_out, high_out, first, last, fine_low, fine_high, sums, blocks = outs
    advance(t, s, u, v, mask, pred, west, east, low, high, west, east, low, high, t_out, s_out)
    fill_blocks(blocks, (t_out, s_out, u, v))
    coarsen(blocks, sums, x, target, low_out, high_out)
    fine_edges(blocks, 2, None, (t_out, s_out), first, last, fine_low, fine_high)


def next_advance_kernel(*refs):
    advance(*refs)


def ring(axis, step):
    count = 1
    for name in axis:
        count *= lax.axis_size(name)
    return [(i, (i + step) % count) for i in range(count)]


def exchange_lon(first, last):
    axis = ("lon", "grp")
    return lax.ppermute(last, axis, ring(axis, 1)), lax.ppermute(first, axis, ring(axis, -1))


def exchange_lat(low, high):
    count = lax.axis_size("lat")
    up = [(i, i + 1) for i in range(count - 1)]
    down = [(i + 1, i) for i in range(count - 1)]
    return lax.ppermute(high, "lat", up), lax.ppermute(low, "lat", down)


def flipped(axis, mask):
    return [(i, i ^ mask) for i in range(lax.axis_size(axis))]


def exchanged_sum(value, axis, masks):
    parts = [lax.ppermute(value, axis, flipped(axis, mask)) for mask in masks]
    if len(parts) == 1:
        return value + parts[0]
    return (value + parts[0]) + (parts[1] + parts[2])


def sum_over_devices(own, other):
    part = own + lax.ppermute(other, "grp", flipped("grp", 1))
    part = exchanged_sum(part, "lon", (1,))
    low = 2
    while low < lax.axis_size("lon"):
        part = exchanged_sum(part, "lon", (low, 2 * low, 3 * low))
        low *= 4
    part = exchanged_sum(part, "lat", (1, 2, 3))
    return part, lax.ppermute(part, "grp", flipped("grp", 1))


def shards(
    thermal_anomaly,
    saltiness_anomaly,
    zonal_flow_speed,
    meridional_flow_speed,
    water_indicator,
    kernel_factors,
    hidden_pointwise_factors,
    final_pointwise_factors,
):
    fields = tuple(
        value.reshape(8 * LEVELS, FINE)
        for value in (thermal_anomaly, saltiness_anomaly, zonal_flow_speed, meridional_flow_speed)
    )
    core = lax.axis_index("grp").astype(jnp.int32).reshape(1)
    packed = jnp.concatenate(
        [
            kernel_factors.reshape(HIDDEN, TAPS),
            jnp.zeros((HIDDEN, MIX_AT - TAPS), f32),
            hidden_pointwise_factors,
            final_pointwise_factors.T,
            jnp.zeros((HIDDEN, PACKED - AREA_AT), f32),
        ],
        1,
    )
    blocks = pltpu.VMEM((16 * 8 * LEVELS, 128), f32)
    sums = [pltpu.VMEM((4 * CHANNELS, FINE), f32), blocks]
    wide = struct(2 * CHANNELS, COARSE)
    tile = struct(8, 128)
    half = struct(HIDDEN // 2, PACKED)
    field = struct(8 * LEVELS, FINE)

    def input_halo(x, low, high):
        south, north = exchange_lat(low, high)
        first, last = (
            jnp.concatenate([x[CHANNELS * row : CHANNELS * (row + 1)], south, north], 0)
            for row in range(2)
        )
        west, east = exchange_lon(first, last)
        return west, east, south, north

    network_outs = [wide, tile, tile, half, half]
    network_scratch = [pltpu.VMEM((TAPS, 2 * COARSE), f32), pltpu.VMEM((HIDDEN, PACKED), f32)]

    def state_halo(pred, pred_low, pred_high, first, last, low, high):
        west, east = exchange_lon(
            jnp.concatenate([first, pred[0:CHANNELS]], 0),
            jnp.concatenate([last, pred[CHANNELS : 2 * CHANNELS]], 0),
        )
        south, north = exchange_lat(
            jnp.concatenate([low, pred_low], 0), jnp.concatenate([high, pred_high], 0)
        )
        return west, east, south, north

    x, target, weight, low, high = call(
        prepare_kernel, [wide, wide, tile, tile, tile], *fields, water_indicator, scratch=sums
    )
    edge = struct(160, 128)
    first, last, fine_low, fine_high = call(
        edges_kernel,
        [edge, edge, tile, tile],
        *fields,
        water_indicator,
        scratch=[pltpu.VMEM((8, FINE), f32), blocks],
    )
    west, east, south, north = input_halo(x, low, high)
    pred, pred_low, pred_high, own, other = call(
        first_network_kernel,
        network_outs,
        core, x, west, east, south, north, target, weight, packed,
        scratch=network_scratch,
        smem=1,
    )
    part, back = sum_over_devices(own, other)
    fixed = state_halo(pred, pred_low, pred_high, first, last, fine_low, fine_high)
    edge = struct(96, 128)
    t, s, x, target, low, high, first, last, fine_low, fine_high = call(
        first_advance_kernel,
        [field, field, wide, wide, tile, tile, edge, edge, tile, tile],
        *fields, water_indicator, pred, *fixed,
        scratch=sums,
    )
    west, east, south, north = input_halo(x, low, high)
    packed, pred, pred_low, pred_high, own, other = call(
        next_network_kernel,
        [struct(HIDDEN, PACKED)] + network_outs,
        core, x, west, east, south, north, target, weight, packed, part, back,
        scratch=network_scratch,
        smem=1,
    )
    part, back = sum_over_devices(own, other)
    moving = state_halo(pred, pred_low, pred_high, first, last, fine_low, fine_high)
    t, s = call(
        next_advance_kernel,
        [field, field],
        t, s, *fields[2:], water_indicator, pred, *fixed, *moving,
    )
    kernel, mix, out = call(
        last_kernel,
        [struct(HIDDEN, TAPS), struct(HIDDEN, HIDDEN), struct(CHANNELS, HIDDEN)],
        core, packed, part, back,
        smem=1,
    )
    return (
        t.reshape(thermal_anomaly.shape),
        s.reshape(thermal_anomaly.shape),
        kernel.reshape(kernel_factors.shape),
        mix,
        out,
    )


def solution(mesh):
    field = P(None, ("lon", "grp"), "lat")
    return jax.shard_map(
        shards,
        mesh=mesh,
        in_specs=(field, field, field, field, P(("lon", "grp"), "lat"), P(), P(), P()),
        out_specs=(field, field, P(), P(), P()),
        check_vma=False,
    )
```

```python
import functools

import jax
import jax.numpy as jnp
from jax import lax
from jax.experimental import pallas as pl
from jax.experimental.pallas import tpu as pltpu
from jax.sharding import PartitionSpec as P

time_step = 0.2
diffusivity = 0.5
learn_rate = 200.0
highest = lax.Precision.HIGHEST
f32 = jnp.float32
bf16 = jnp.bfloat16

LEVELS = 12
CHANNELS = 4 * LEVELS
HIDDEN = 64
TAPS = 9 * CHANNELS
MIX_AT = 512
OUT_AT = 576
AREA_AT = 624
PACKED = 640
COLUMNS_AT = 96
EDGE_AT = 112
FINE = 512
COARSE = 128
VMEM_LIMIT = 48 * 1024 * 1024


def struct(*shape):
    return jax.ShapeDtypeStruct(shape, f32)


def call(kernel, outs, *args, scratch=(), smem=0, remote=0, flops=0, bytes_accessed=0):
    specs = [pl.BlockSpec(memory_space=pltpu.SMEM)] * smem
    specs += [pl.BlockSpec(memory_space=pl.ANY)] * remote
    specs += [pl.BlockSpec(memory_space=pltpu.VMEM)] * (len(args) - smem - remote)
    return pl.pallas_call(
        kernel,
        out_shape=outs,
        in_specs=specs,
        out_specs=[pl.BlockSpec(memory_space=pltpu.VMEM)] * len(outs),
        scratch_shapes=scratch,
        compiler_params=pltpu.CompilerParams(vmem_limit_bytes=VMEM_LIMIT),
        cost_estimate=pl.CostEstimate(
            flops=flops, bytes_accessed=bytes_accessed, transcendentals=0
        ),
    )(*args)


def exact_dot(value, selector):
    high = value.astype(bf16)
    rest = value - high.astype(f32)
    middle = rest.astype(bf16)
    low = (rest - middle.astype(f32)).astype(bf16)
    dot = functools.partial(jnp.dot, preferred_element_type=f32)
    return (dot(low, selector) + dot(middle, selector)) + dot(high, selector)


def pooling_matrix():
    fine = lax.broadcasted_iota(jnp.int32, (FINE, COARSE), 0) >> 2
    coarse = lax.broadcasted_iota(jnp.int32, (FINE, COARSE), 1)
    return jnp.where(fine == coarse, f32(1.0 / 16.0), f32(0.0)).astype(bf16)


def spreading_matrix():
    fine = lax.broadcasted_iota(jnp.int32, (COARSE, FINE), 1) >> 2
    coarse = lax.broadcasted_iota(jnp.int32, (COARSE, FINE), 0)
    return jnp.where(fine == coarse, f32(1.0), f32(0.0)).astype(bf16)


def lane_index(shape):
    return lax.broadcasted_iota(jnp.int32, shape, len(shape) - 1)


def block_rows(which, block):
    start = (4 * which + block) * 8 * LEVELS
    return slice(start, start + 8 * LEVELS)


def fill_blocks(blocks, refs):
    for which, ref in enumerate(refs):
        for block in range(4):
            blocks[block_rows(which, block), :] = ref[:, 128 * block : 128 * (block + 1)]


def fetch(pairs, semaphore):
    copies = [
        pltpu.make_async_copy(source, target, semaphore.at[at])
        for at, (source, target) in enumerate(pairs)
    ]
    for copy in copies:
        copy.start()
    return copies


def longitude_row(blocks, which, block, lon):
    return blocks[pl.ds(block_rows(which, block).start + lon, LEVELS, stride=8), :]


def coarsen(blocks, sums_ref, x_ref, target_ref):
    for row in range(2):
        for block in range(4):
            total = None
            for lon in range(4 * row, 4 * row + 4):
                t, s, u, v = (longitude_row(blocks, which, block, lon) for which in range(4))
                terms = (t, s, u, v, u * t, v * t, u * s, v * s)
                total = terms if total is None else [a + b for a, b in zip(total, terms)]
            for at, value in enumerate(total):
                start = 2 * CHANNELS * row + LEVELS * at
                sums_ref[start : start + LEVELS, 128 * block : 128 * (block + 1)] = value
    means = exact_dot(sums_ref[...], pooling_matrix())
    for row in range(2):
        x = means[2 * CHANNELS * row : 2 * CHANNELS * row + CHANNELS]
        products = means[2 * CHANNELS * row + CHANNELS : 2 * CHANNELS * (row + 1)]
        ct, cs, cu, cv = (x[LEVELS * k : LEVELS * (k + 1)] for k in range(4))
        x_ref[CHANNELS * row : CHANNELS * (row + 1), :] = x
        own = jnp.concatenate([cu * ct, cv * ct, cu * cs, cv * cs], 0)
        target_ref[CHANNELS * row : CHANNELS * (row + 1), :] = products - own


def fill_edges(blocks, fields, column_fields, mask_ref, x_ref, first_ref, last_ref, low_ref, high_ref):
    depth = (first_ref.shape[0] - EDGE_AT) // 4
    for lon, out in ((0, first_ref), (7, last_ref)):
        out[0:COLUMNS_AT, :] = x_ref[...]
        out[COLUMNS_AT:, :] = jnp.zeros((out.shape[0] - COLUMNS_AT, COARSE), f32)
        for block in range(4):
            start = EDGE_AT + block * depth
            for which in range(fields):
                at = start + which * LEVELS
                out[at : at + LEVELS, :] = longitude_row(blocks, which, block, lon)
            if mask_ref is not None:
                at = start + fields * LEVELS
                out[at : at + 1, :] = mask_ref[lon : lon + 1, 128 * block : 128 * (block + 1)]
    turned = x_ref[...].T
    for out, block, column, inner in ((low_ref, 0, 0, 1), (high_ref, 3, 127, 126)):
        out[...] = jnp.zeros(out.shape, f32)
        for at, which in enumerate(column_fields):
            out[at : at + 1, 0 : 8 * LEVELS] = blocks[block_rows(which, block), :].T[column : column + 1]
        if mask_ref is not None:
            here = mask_ref[:, 128 * block : 128 * (block + 1)]
            out[3:4, 0:8] = here.T[column : column + 1]
        out[4:5, 0 : 2 * CHANNELS] = turned[column : column + 1]
        out[5:6, 0 : 2 * CHANNELS] = turned[inner : inner + 1]


def prepare_kernel(
    t, s, u, v, mask, x, target, weight, first, last, low, high, sums, blocks, mask_here, mask_values, semaphore
):
    pairs = [(mask, mask_here)]
    for which, ref in enumerate((t, s, u, v)):
        for block in range(4):
            pairs.append((ref.at[:, pl.ds(128 * block, 128)], blocks.at[block_rows(which, block), :]))
    copies = fetch(pairs, semaphore)
    for copy in copies:
        copy.wait()
    m = mask_here[...].astype(f32)
    mask_values[...] = m
    coarsen(blocks, sums, x, target)
    fill_edges(blocks, 3, (0, 1, 3), mask_values, x, first, last, low, high)
    rows = jnp.concatenate(
        [jnp.sum(m[0:4], axis=0, keepdims=True), jnp.sum(m[4:8], axis=0, keepdims=True)]
        + [jnp.zeros((6, FINE), f32)],
        0,
    )
    weight[...] = jnp.dot(rows.astype(bf16), pooling_matrix(), preferred_element_type=f32)


def dot(a, b):
    return jnp.dot(a, b, precision=highest, preferred_element_type=f32)


def dot_nt(a, b):
    return lax.dot_general(
        a, b, (((1,), (1,)), ((), ())), precision=highest, preferred_element_type=f32
    )


def column_matrix(low, high, west, east):
    rows = []
    for at in (4, 5):
        for ref, start in ((low, 0), (high, 0)):
            rows.append(ref[start + at : start + at + 1, :])
        for ref in (west, east):
            for start in (COLUMNS_AT, COLUMNS_AT + 8):
                rows.append(ref[start + at : start + at + 1, :])
    rows.append(jnp.zeros((4, COARSE), f32))
    return jnp.concatenate(rows, 0).T


def shifted_rows(value, before, after):
    lanes = lane_index((CHANNELS, COARSE))
    return (
        jnp.where(lanes == 0, before, pltpu.roll(value, 1, 1)),
        value,
        jnp.where(lanes == COARSE - 1, after, pltpu.roll(value, COARSE - 1, 1)),
    )


def coarse_rows(x, west, east):
    return (
        (west[0:CHANNELS, :], 0, 2),
        (west[CHANNELS : 2 * CHANNELS, :], CHANNELS, 2),
        (x[0:CHANNELS, :], 0, 0),
        (x[CHANNELS : 2 * CHANNELS, :], CHANNELS, 0),
        (east[0:CHANNELS, :], 0, 4),
        (east[CHANNELS : 2 * CHANNELS, :], CHANNELS, 4),
    )


def fill_taps(taps, rows, columns, centres):
    for at, (value, start, pair) in enumerate(rows):
        if not any(abs(at - centre) <= 1 for centre in centres):
            continue
        channels = slice(start, start + CHANNELS)
        shifted = shifted_rows(
            value, columns[channels, pair : pair + 1], columns[channels, pair + 1 : pair + 2]
        )
        for place, centre in enumerate(centres):
            tap = at - centre + 1
            if 0 <= tap < 3:
                for side in range(3):
                    begin = (3 * tap + side) * CHANNELS
                    taps[begin : begin + CHANNELS, COARSE * place : COARSE * (place + 1)] = shifted[side]


def fill_side_taps(taps, rows, columns, start_lane):
    lanes = lane_index((CHANNELS, COARSE))
    for tap in range(3):
        for side in range(3):
            out = jnp.zeros((CHANNELS, COARSE), f32)
            for row in range(2):
                value, start, pair = rows[row + tap + 1]
                channels = slice(start, start + CHANNELS)
                low = (
                    columns[channels, 6 + pair : 7 + pair],
                    columns[channels, pair : pair + 1],
                    value[:, 0:1],
                )[side]
                high = (
                    value[:, COARSE - 1 : COARSE],
                    columns[channels, pair + 1 : pair + 2],
                    columns[channels, 7 + pair : 8 + pair],
                )[side]
                out = jnp.where(lanes == row, low, out)
                out = jnp.where(lanes == 2 + row, high, out)
            begin = (3 * tap + side) * CHANNELS
            taps[begin : begin + CHANNELS, start_lane : start_lane + COARSE] = out


def network_step(
    core, x, west, east, low, high, target, weight, packed, pred, own, other, taps, grads
):
    columns = column_matrix(low, high, west, east)
    fill_taps(taps, coarse_rows(x, west, east), columns, (2, 3))
    kernel = packed[:, 0:TAPS]
    mix = packed[:, MIX_AT : MIX_AT + HIDDEN]
    out_turned = packed[:, OUT_AT : OUT_AT + CHANNELS]
    hidden_one = jnp.tanh(dot(kernel, taps[...]))
    hidden_two = jnp.tanh(dot(mix, hidden_one))
    predicted = dot(out_turned.T, hidden_two)
    pred[0:CHANNELS, :] = predicted[:, 0:COARSE]
    pred[CHANNELS : 2 * CHANNELS, :] = predicted[:, COARSE : 2 * COARSE]
    back_out = jnp.concatenate(
        [
            weight[row : row + 1, :]
            * (
                predicted[:, COARSE * row : COARSE * (row + 1)]
                - target[CHANNELS * row : CHANNELS * (row + 1), :]
            )
            for row in range(2)
        ],
        1,
    )
    back_two = dot(out_turned, back_out) * (1.0 - hidden_two * hidden_two)
    back_one = dot(mix.T, back_two) * (1.0 - hidden_one * hidden_one)
    grads[:, MIX_AT - 128 : PACKED] = jnp.zeros((HIDDEN, PACKED - MIX_AT + 128), f32)
    grads[:, 0:TAPS] = dot_nt(back_one, taps[...])
    grads[:, MIX_AT : MIX_AT + HIDDEN] = dot_nt(back_two, hidden_one)
    grads[:, OUT_AT : OUT_AT + CHANNELS] = dot_nt(hidden_two, back_out)
    area = jnp.sum(weight[0:2, :], axis=(0, 1), keepdims=True)
    grads[:, AREA_AT : AREA_AT + 1] = jnp.broadcast_to(area, (HIDDEN, 1))
    half = HIDDEN // 2
    own[...] = grads[pl.ds(pl.multiple_of(core[0] * half, half), half), :]
    other[...] = grads[pl.ds(pl.multiple_of((1 - core[0]) * half, half), half), :]


def descended(core, packed, part, back):
    half = HIDDEN // 2
    mine, theirs = part[...], back[...]
    first = core[0] == 0
    total = jnp.concatenate(
        [jnp.where(first, mine, theirs), jnp.where(first, theirs, mine)], 0
    )
    area = total[0:1, AREA_AT : AREA_AT + 1]
    step = (learn_rate * 2.0 / CHANNELS) / area
    return packed[...] - step * total


def first_network_kernel(core, x, west, east, low, high, target, weight, packed, *rest):
    network_step(core, x, west, east, low, high, target, weight, packed, *rest)


def next_network_kernel(
    core, x, west, east, low, high, target, weight, packed, part, back, renewed, *rest
):
    renewed[...] = descended(core, packed, part, back)
    network_step(core, x, west, east, low, high, target, weight, renewed, *rest)


def last_kernel(core, packed, part, back, kernel, mix, out):
    renewed = descended(core, packed, part, back)
    kernel[...] = renewed[:, 0:TAPS]
    mix[...] = renewed[:, MIX_AT : MIX_AT + HIDDEN]
    out[...] = renewed[:, OUT_AT : OUT_AT + CHANNELS].T


def forcing(place, x, pred, packed, west, east, low, high, taps):
    rows = coarse_rows(x, west, east)
    columns = column_matrix(low, high, west, east)
    fill_taps(taps, rows, columns, (1, 4))
    fill_side_taps(taps, rows, columns, 2 * COARSE)
    hidden = jnp.tanh(dot(packed[:, 0:TAPS], taps[...]))
    hidden = jnp.tanh(dot(packed[:, MIX_AT : MIX_AT + HIDDEN], hidden))
    beside = dot(packed[:, OUT_AT : OUT_AT + CHANNELS].T, hidden)
    sides = beside[:, 2 * COARSE :]
    sides_low = jnp.where(place[1] == 0, 0.0, sides)
    sides_high = jnp.where(place[2] == 0, 0.0, sides)
    before = (beside[:, 0:COARSE], pred[0:CHANNELS, :])
    after = (pred[CHANNELS : 2 * CHANNELS, :], beside[:, COARSE : 2 * COARSE])
    pieces = []
    for row in range(2):
        value = pred[CHANNELS * row : CHANNELS * (row + 1), :]
        along = after[row] - before[row]
        south, _, north = shifted_rows(value, sides_low[:, row : row + 1], sides_high[:, 2 + row : 3 + row])
        across = north - south
        for at in (0, 2 * LEVELS):
            pieces.append(-0.5 * (along[at : at + LEVELS] + across[at + LEVELS : at + 2 * LEVELS]))
            pieces.append(jnp.zeros((4, COARSE), f32))
    return exact_dot(jnp.concatenate(pieces, 0), spreading_matrix())


def advance(t, s, u, v, mask, force, fixed, moving, t_out, s_out):
    fixed_west, fixed_east, fixed_low, fixed_high = fixed
    west, east, low, high = moving
    m = mask[...].astype(f32)
    shape = (8, FINE)
    lanes = lane_index(shape)
    subs = lax.broadcasted_iota(jnp.int32, shape, 0)

    def edge_row(ref, at):
        depth = (ref.shape[0] - EDGE_AT) // 4
        starts = [EDGE_AT + depth * block + at for block in range(4)]
        return jnp.concatenate([ref[start : start + 1, :] for start in starts], 1)

    def neighbours_lon(value, row_west, row_east):
        return (
            jnp.where(subs == 0, row_west, pltpu.roll(value, 1, 0)),
            jnp.where(subs == 7, row_east, pltpu.roll(value, 7, 0)),
        )

    def neighbours_lat(value, column_low, column_high):
        return (
            jnp.where(lanes == 0, column_low, pltpu.roll(value, 1, 1)),
            jnp.where(lanes == FINE - 1, column_high, pltpu.roll(value, FINE - 1, 1)),
        )

    fixed_low_turned = fixed_low[...].T
    fixed_high_turned = fixed_high[...].T
    low_turned = low[...].T
    high_turned = high[...].T
    m_west, m_east = neighbours_lon(
        m, edge_row(fixed_west, 3 * LEVELS), edge_row(fixed_east, 3 * LEVELS)
    )
    m_low, m_high = neighbours_lat(m, fixed_low_turned[0:8, 3:4], fixed_high_turned[0:8, 3:4])
    open_west, open_east, open_low, open_high = m * m_west, m * m_east, m * m_low, m * m_high
    mix_west, mix_east = diffusivity * open_west, diffusivity * open_east
    mix_low, mix_high = diffusivity * open_low, diffusivity * open_high
    pace = time_step * m
    for level in range(LEVELS):
        at = slice(8 * level, 8 * (level + 1))
        u_here, v_here = u[at, :], v[at, :]
        u_west, u_east = neighbours_lon(
            u_here, edge_row(fixed_west, 2 * LEVELS + level), edge_row(fixed_east, 2 * LEVELS + level)
        )
        v_low, v_high = neighbours_lat(v_here, fixed_low_turned[at, 2:3], fixed_high_turned[at, 2:3])
        speed_west = 0.25 * (u_here + u_west) * open_west
        speed_east = 0.25 * (u_here + u_east) * open_east
        speed_low = 0.25 * (v_here + v_low) * open_low
        speed_high = 0.25 * (v_here + v_high) * open_high
        for which, (q_ref, out) in enumerate(((t, t_out), (s, s_out))):
            q = q_ref[at, :]
            q_west, q_east = neighbours_lon(
                q, edge_row(west, LEVELS * which + level), edge_row(east, LEVELS * which + level)
            )
            q_low, q_high = neighbours_lat(
                q, low_turned[at, which : which + 1], high_turned[at, which : which + 1]
            )
            flux_east = speed_east * (q + q_east) - mix_east * (q_east - q)
            flux_west = speed_west * (q_west + q) - mix_west * (q - q_west)
            flux_high = speed_high * (q + q_high) - mix_high * (q_high - q)
            flux_low = speed_low * (q_low + q) - mix_low * (q - q_low)
            row = 16 * which + level
            push = jnp.where(subs < 4, force[row : row + 1], force[32 + row : 33 + row])
            out[at, :] = q + pace * (push - (flux_east - flux_west) - (flux_high - flux_low))


def first_advance_kernel(place, *refs):
    t, s, u, v, mask, x, pred, packed, west, east, low, high = refs[:12]
    t_out, s_out, x_out, target, first, last, low_out, high_out = refs[12:20]
    sums, blocks, taps, t_here, s_here, u_here, v_here, semaphore = refs[20:]
    here = (t_here, s_here, u_here, v_here)
    copies = fetch(list(zip((t, s, u, v), here)), semaphore)
    halo = (west, east, low, high)
    force = forcing(place, x, pred, packed, *halo, taps)
    for copy in copies:
        copy.wait()
    advance(*here, mask, force, halo, halo, t_out, s_out)
    fill_blocks(blocks, (t_out, s_out, u_here, v_here))
    coarsen(blocks, sums, x_out, target)
    fill_edges(blocks, 2, (0, 1), None, x_out, first, last, low_out, high_out)


def next_advance_kernel(place, *refs):
    t, s, u, v, mask, x, pred, packed = refs[:8]
    fixed, moving, (t_out, s_out, taps) = refs[8:12], refs[12:16], refs[16:]
    force = forcing(place, x, pred, packed, *moving, taps)
    advance(t, s, u, v, mask, force, fixed, moving, t_out, s_out)


def ring(axis, step):
    count = 1
    for name in axis:
        count *= lax.axis_size(name)
    return [(i, (i + step) % count) for i in range(count)]


def exchange_lon(first, last):
    axis = ("lon", "grp")
    return lax.ppermute(last, axis, ring(axis, 1)), lax.ppermute(first, axis, ring(axis, -1))


def exchange_lat(low, high):
    count = lax.axis_size("lat")
    up = [(i, i + 1) for i in range(count - 1)]
    down = [(i + 1, i) for i in range(count - 1)]
    return lax.ppermute(high, "lat", up), lax.ppermute(low, "lat", down)


def flipped(axis, mask):
    return [(i, i ^ mask) for i in range(lax.axis_size(axis))]


def exchanged_sum(value, axis, masks):
    parts = [lax.ppermute(value, axis, flipped(axis, mask)) for mask in masks]
    if len(parts) == 1:
        return value + parts[0]
    return (value + parts[0]) + (parts[1] + parts[2])


def sum_over_devices(own, other):
    part = own + lax.ppermute(other, "grp", flipped("grp", 1))
    part = exchanged_sum(part, "lon", (1,))
    low = 2
    while low < lax.axis_size("lon"):
        part = exchanged_sum(part, "lon", (low, 2 * low, 3 * low))
        low *= 4
    part = exchanged_sum(part, ("lon", "lat"), (1, 6, 3))
    return part, lax.ppermute(part, "grp", flipped("grp", 1))


def shards(
    thermal_anomaly,
    saltiness_anomaly,
    zonal_flow_speed,
    meridional_flow_speed,
    water_indicator,
    kernel_factors,
    hidden_pointwise_factors,
    final_pointwise_factors,
):
    fields = tuple(
        value.reshape(8 * LEVELS, FINE)
        for value in (thermal_anomaly, saltiness_anomaly, zonal_flow_speed, meridional_flow_speed)
    )
    packed = jnp.concatenate(
        [
            kernel_factors.reshape(HIDDEN, TAPS),
            jnp.zeros((HIDDEN, MIX_AT - TAPS), f32),
            hidden_pointwise_factors,
            final_pointwise_factors.T,
            jnp.zeros((HIDDEN, PACKED - AREA_AT), f32),
        ],
        1,
    )
    blocks = pltpu.VMEM((16 * 8 * LEVELS, 128), f32)
    lat = lax.axis_index("lat")
    lat_last = lax.axis_size("lat") - 1
    place = jnp.stack(
        [lax.axis_index("grp"), (lat != 0).astype(jnp.int32), (lat != lat_last).astype(jnp.int32)]
    ).astype(jnp.int32)
    field_scratch = pltpu.VMEM((8 * LEVELS, FINE), f32)
    sums = [pltpu.VMEM((4 * CHANNELS, FINE), f32), pltpu.VMEM((16 * 8 * LEVELS, 128), f32)]
    wide = struct(2 * CHANNELS, COARSE)
    tile = struct(8, 128)
    half = struct(HIDDEN // 2, PACKED)
    field = struct(8 * LEVELS, FINE)
    network_outs = [wide, half, half]
    network_scratch = [pltpu.VMEM((TAPS, 2 * COARSE), f32), pltpu.VMEM((HIDDEN, PACKED), f32)]
    side_taps = pltpu.VMEM((TAPS, 3 * COARSE), f32)

    def halo(first, last, low, high):
        south, north = exchange_lat(low, high)
        columns = jnp.concatenate([south, north], 0)
        first = lax.dynamic_update_slice_in_dim(first, columns, COLUMNS_AT, 0)
        last = lax.dynamic_update_slice_in_dim(last, columns, COLUMNS_AT, 0)
        return *exchange_lon(first, last), south, north

    edge = struct(EDGE_AT + 160, 128)
    x, target, weight, *edges = call(
        prepare_kernel,
        [wide, wide, tile, edge, edge, tile, tile],
        *fields, water_indicator,
        scratch=sums
        + [
            pltpu.VMEM((8, FINE), jnp.int32),
            pltpu.VMEM((8, FINE), f32),
            pltpu.SemaphoreType.DMA((17,)),
        ],
        remote=5,
    )
    fixed = halo(*edges)
    pred, own, other = call(
        first_network_kernel,
        network_outs,
        place, x, *fixed, target, weight, packed,
        scratch=network_scratch,
        smem=1,
    )
    part, back = sum_over_devices(own, other)
    edge = struct(EDGE_AT + 96, 128)
    t, s, x, target, *edges = call(
        first_advance_kernel,
        [field, field, wide, wide, edge, edge, tile, tile],
        place, *fields, water_indicator, x, pred, packed, *fixed,
        scratch=sums + [side_taps] + [field_scratch] * 4 + [pltpu.SemaphoreType.DMA((4,))],
        smem=1,
        remote=4,
    )
    moving = halo(*edges)
    packed, pred, own, other = call(
        next_network_kernel,
        [struct(HIDDEN, PACKED)] + network_outs,
        place, x, *moving, target, weight, packed, part, back,
        scratch=network_scratch,
        smem=1,
    )
    part, back = sum_over_devices(own, other)
    t, s = call(
        next_advance_kernel,
        [field, field],
        place, t, s, *fields[2:], water_indicator, x, pred, packed, *fixed, *moving,
        scratch=[side_taps],
        smem=1,
    )
    kernel, mix, out = call(
        last_kernel,
        [struct(HIDDEN, TAPS), struct(HIDDEN, HIDDEN), struct(CHANNELS, HIDDEN)],
        place, packed, part, back,
        smem=1,
    )
    return (
        t.reshape(thermal_anomaly.shape),
        s.reshape(thermal_anomaly.shape),
        kernel.reshape(kernel_factors.shape),
        mix,
        out,
    )


def solution(mesh):
    field = P(None, ("lon", "grp"), "lat")
    return jax.shard_map(
        shards,
        mesh=mesh,
        in_specs=(field, field, field, field, P(("lon", "grp"), "lat"), P(), P(), P()),
        out_specs=(field, field, P(), P(), P()),
        check_vma=False,
    )
```

```python
import functools

import jax
import jax.numpy as jnp
from jax import lax
from jax.experimental import pallas as pl
from jax.experimental.pallas import tpu as pltpu
from jax.sharding import PartitionSpec as P

time_step = 0.2
diffusivity = 0.5
learn_rate = 200.0
f32 = jnp.float32
bf16 = jnp.bfloat16

LEVELS = 12
CHANNELS = 4 * LEVELS
HIDDEN = 64
TAPS = 9 * CHANNELS
MIX_AT = 512
OUT_AT = 576
AREA_AT = 624
PACKED = 640
COLUMNS_AT = 96
EDGE_AT = 112
FINE = 512
COARSE = 128
VMEM_LIMIT = 48 * 1024 * 1024


def struct(*shape):
    return jax.ShapeDtypeStruct(shape, f32)


def call(kernel, outs, *args, scratch=(), smem=0, remote=0, flops=0, bytes_accessed=0):
    first, last = smem, smem + remote
    args = [
        pltpu.with_memory_space_constraint(arg, pltpu.HBM) if first <= at < last else arg
        for at, arg in enumerate(args)
    ]
    specs = [pl.BlockSpec(memory_space=pltpu.SMEM)] * smem
    specs += [pl.BlockSpec(memory_space=pltpu.HBM)] * remote
    specs += [pl.BlockSpec(memory_space=pltpu.VMEM)] * (len(args) - smem - remote)
    return pl.pallas_call(
        kernel,
        out_shape=outs,
        in_specs=specs,
        out_specs=[pl.BlockSpec(memory_space=pltpu.VMEM)] * len(outs),
        scratch_shapes=scratch,
        compiler_params=pltpu.CompilerParams(vmem_limit_bytes=VMEM_LIMIT),
        cost_estimate=pl.CostEstimate(
            flops=flops, bytes_accessed=bytes_accessed, transcendentals=0
        ),
    )(*args)


def exact_dot(value, selector):
    high = value.astype(bf16)
    rest = value - high.astype(f32)
    middle = rest.astype(bf16)
    low = (rest - middle.astype(f32)).astype(bf16)
    dot = functools.partial(jnp.dot, preferred_element_type=f32)
    return (dot(low, selector) + dot(middle, selector)) + dot(high, selector)


def pooling_matrix():
    fine = lax.broadcasted_iota(jnp.int32, (FINE, COARSE), 0) >> 2
    coarse = lax.broadcasted_iota(jnp.int32, (FINE, COARSE), 1)
    return jnp.where(fine == coarse, f32(1.0 / 16.0), f32(0.0)).astype(bf16)


def spreading_matrix():
    fine = lax.broadcasted_iota(jnp.int32, (COARSE, FINE), 1) >> 2
    coarse = lax.broadcasted_iota(jnp.int32, (COARSE, FINE), 0)
    return jnp.where(fine == coarse, f32(1.0), f32(0.0)).astype(bf16)


def lane_index(shape):
    return lax.broadcasted_iota(jnp.int32, shape, len(shape) - 1)


def block_rows(which, block):
    start = (4 * which + block) * 8 * LEVELS
    return slice(start, start + 8 * LEVELS)


def fill_blocks(blocks, refs):
    for which, ref in enumerate(refs):
        for block in range(4):
            blocks[block_rows(which, block), :] = ref[:, 128 * block : 128 * (block + 1)]


def fetch(pairs, semaphore):
    copies = [
        pltpu.make_async_copy(source, target, semaphore.at[at])
        for at, (source, target) in enumerate(pairs)
    ]
    for copy in copies:
        copy.start()
    return copies


def longitude_row(blocks, which, block, lon):
    return blocks[pl.ds(block_rows(which, block).start + lon, LEVELS, stride=8), :]


def coarsen(blocks, sums_ref, x_ref, target_ref):
    for row in range(2):
        for block in range(4):
            total = None
            for lon in range(4 * row, 4 * row + 4):
                t, s, u, v = (longitude_row(blocks, which, block, lon) for which in range(4))
                terms = (t, s, u, v, u * t, v * t, u * s, v * s)
                total = terms if total is None else [a + b for a, b in zip(total, terms)]
            for at, value in enumerate(total):
                start = 2 * CHANNELS * row + LEVELS * at
                sums_ref[start : start + LEVELS, 128 * block : 128 * (block + 1)] = value
    means = exact_dot(sums_ref[...], pooling_matrix())
    for row in range(2):
        x = means[2 * CHANNELS * row : 2 * CHANNELS * row + CHANNELS]
        products = means[2 * CHANNELS * row + CHANNELS : 2 * CHANNELS * (row + 1)]
        ct, cs, cu, cv = (x[LEVELS * k : LEVELS * (k + 1)] for k in range(4))
        x_ref[CHANNELS * row : CHANNELS * (row + 1), :] = x
        own = jnp.concatenate([cu * ct, cv * ct, cu * cs, cv * cs], 0)
        target_ref[CHANNELS * row : CHANNELS * (row + 1), :] = products - own


class Either:
    def __init__(self, flag, one, other):
        self.flag, self.one, self.other, self.shape = flag, one, other, one.shape

    def __getitem__(self, at):
        return jnp.where(self.flag, self.one[at], self.other[at])


def sides(place, inner, outer):
    first = place[0] == 0
    return Either(first, outer, inner), Either(first, inner, outer)


def fill_edges(place, blocks, fields, column_fields, mask_ref, x_ref, inner_ref, outer_ref, near_ref, far_ref):
    core_first = place[0] == 0
    depth = (inner_ref.shape[0] - EDGE_AT) // 4
    for out in (inner_ref, outer_ref):
        out[0:COLUMNS_AT, :] = x_ref[...]
        out[COLUMNS_AT:, :] = jnp.zeros((out.shape[0] - COLUMNS_AT, COARSE), f32)

    def put(rows, first, last):
        inner_ref[rows, :] = jnp.where(core_first, last, first)
        outer_ref[rows, :] = jnp.where(core_first, first, last)

    for block in range(4):
        start = EDGE_AT + block * depth
        for which in range(fields):
            at = start + which * LEVELS
            put(
                slice(at, at + LEVELS),
                longitude_row(blocks, which, block, 0),
                longitude_row(blocks, which, block, 7),
            )
        if mask_ref is not None:
            at = start + fields * LEVELS
            lanes = slice(128 * block, 128 * (block + 1))
            put(slice(at, at + 1), mask_ref[0:1, lanes], mask_ref[7:8, lanes])
    odd = place[3] == 1
    near_ref[...] = jnp.zeros(near_ref.shape, f32)
    far_ref[...] = jnp.zeros(far_ref.shape, f32)

    def put_columns(at, low, high, low_column, high_column):
        low, high = low.T[low_column : low_column + 1], high.T[high_column : high_column + 1]
        near_ref[at : at + 1, 0 : low.shape[1]] = jnp.where(odd, low, high)
        far_ref[at : at + 1, 0 : low.shape[1]] = jnp.where(odd, high, low)

    for at, which in enumerate(column_fields):
        put_columns(at, blocks[block_rows(which, 0), :], blocks[block_rows(which, 3), :], 0, 127)
    if mask_ref is not None:
        put_columns(3, mask_ref[:, 0:128], mask_ref[:, FINE - 128 : FINE], 0, 127)
    put_columns(4, x_ref[...], x_ref[...], 0, COARSE - 1)
    put_columns(5, x_ref[...], x_ref[...], 1, COARSE - 2)


def prepare_kernel(
    place, t, s, u, v, mask, x, target, weight, mask_values, inner, outer, near, far, sums, blocks, mask_here, semaphore
):
    pairs = [(mask, mask_here)]
    for which, ref in enumerate((t, s, u, v)):
        for block in range(4):
            pairs.append((ref.at[:, pl.ds(128 * block, 128)], blocks.at[block_rows(which, block), :]))
    copies = fetch(pairs, semaphore)
    for copy in copies:
        copy.wait()
    m = mask_here[...].astype(f32)
    mask_values[...] = m
    coarsen(blocks, sums, x, target)
    fill_edges(place, blocks, 3, (0, 1, 3), mask_values, x, inner, outer, near, far)
    rows = jnp.concatenate(
        [jnp.sum(m[0:4], axis=0, keepdims=True), jnp.sum(m[4:8], axis=0, keepdims=True)]
        + [jnp.zeros((6, FINE), f32)],
        0,
    )
    weight[...] = jnp.dot(rows.astype(bf16), pooling_matrix(), preferred_element_type=f32)


def parts_of(value):
    high = value.astype(bf16)
    return high, (value - high.astype(f32)).astype(bf16)


def dot_parts(a, b, contract):
    (a_high, a_low), (b_high, b_low) = a, b
    dims = (((1,), (contract,)), ((), ()))
    dot = functools.partial(lax.dot_general, dimension_numbers=dims, preferred_element_type=f32)
    rows = a_high.shape[0]
    both = dot(jnp.concatenate([a_high, a_low], 0), b_high)
    return both[:rows] + (both[rows:] + dot(a_high, b_low))


def column_matrix(low, high, west, east):
    rows = []
    for at in (4, 5):
        for ref, start in ((low, 0), (high, 0)):
            rows.append(ref[start + at : start + at + 1, :])
        for ref in (west, east):
            for start in (COLUMNS_AT, COLUMNS_AT + 8):
                rows.append(ref[start + at : start + at + 1, :])
    rows.append(jnp.zeros((4, COARSE), f32))
    return jnp.concatenate(rows, 0).T


def shifted_rows(value, before, after):
    lanes = lane_index((CHANNELS, COARSE))
    return (
        jnp.where(lanes == 0, before, pltpu.roll(value, 1, 1)),
        value,
        jnp.where(lanes == COARSE - 1, after, pltpu.roll(value, COARSE - 1, 1)),
    )


def coarse_rows(x, west, east):
    return (
        (west[0:CHANNELS, :], 0, 2),
        (west[CHANNELS : 2 * CHANNELS, :], CHANNELS, 2),
        (x[0:CHANNELS, :], 0, 0),
        (x[CHANNELS : 2 * CHANNELS, :], CHANNELS, 0),
        (east[0:CHANNELS, :], 0, 4),
        (east[CHANNELS : 2 * CHANNELS, :], CHANNELS, 4),
    )


def fill_taps(taps, rows, columns, centres):
    for at, (value, start, pair) in enumerate(rows):
        if not any(abs(at - centre) <= 1 for centre in centres):
            continue
        channels = slice(start, start + CHANNELS)
        shifted = [
            parts_of(part)
            for part in shifted_rows(
                value, columns[channels, pair : pair + 1], columns[channels, pair + 1 : pair + 2]
            )
        ]
        for place, centre in enumerate(centres):
            tap = at - centre + 1
            if 0 <= tap < 3:
                for side in range(3):
                    begin = (3 * tap + side) * CHANNELS
                    for out, part in zip(taps, shifted[side]):
                        out[begin : begin + CHANNELS, COARSE * place : COARSE * (place + 1)] = part


def fill_side_taps(taps, rows, columns, start_lane):
    lanes = lane_index((CHANNELS, COARSE))
    for tap in range(3):
        for side in range(3):
            out = jnp.zeros((CHANNELS, COARSE), f32)
            for row in range(2):
                value, start, pair = rows[row + tap + 1]
                channels = slice(start, start + CHANNELS)
                low = (
                    columns[channels, 6 + pair : 7 + pair],
                    columns[channels, pair : pair + 1],
                    value[:, 0:1],
                )[side]
                high = (
                    value[:, COARSE - 1 : COARSE],
                    columns[channels, pair + 1 : pair + 2],
                    columns[channels, 7 + pair : 8 + pair],
                )[side]
                out = jnp.where(lanes == row, low, out)
                out = jnp.where(lanes == 2 + row, high, out)
            begin = (3 * tap + side) * CHANNELS
            for ref, part in zip(taps, parts_of(out)):
                ref[begin : begin + CHANNELS, start_lane : start_lane + COARSE] = part


def network_step(
    place, x, inner, outer, low, high, target, weight, packed, pred, own, other, taps_high, taps_low, grads
):
    west, east = sides(place, inner, outer)
    columns = column_matrix(low, high, west, east)
    fill_taps((taps_high, taps_low), coarse_rows(x, west, east), columns, (2, 3))
    taps = taps_high[...], taps_low[...]
    kernel = parts_of(packed[:, 0:TAPS])
    mix = packed[:, MIX_AT : MIX_AT + HIDDEN]
    out_turned = packed[:, OUT_AT : OUT_AT + CHANNELS]
    hidden_one = jnp.tanh(dot_parts(kernel, taps, 0))
    one = parts_of(hidden_one)
    hidden_two = jnp.tanh(dot_parts(parts_of(mix), one, 0))
    two = parts_of(hidden_two)
    predicted = dot_parts(parts_of(out_turned.T), two, 0)
    pred[0:CHANNELS, :] = predicted[:, 0:COARSE]
    pred[CHANNELS : 2 * CHANNELS, :] = predicted[:, COARSE : 2 * COARSE]
    back_out = parts_of(
        jnp.concatenate(
            [
                weight[row : row + 1, :]
                * (
                    predicted[:, COARSE * row : COARSE * (row + 1)]
                    - target[CHANNELS * row : CHANNELS * (row + 1), :]
                )
                for row in range(2)
            ],
            1,
        )
    )
    back_two = parts_of(
        dot_parts(parts_of(out_turned), back_out, 0) * (1.0 - hidden_two * hidden_two)
    )
    back_one = parts_of(
        dot_parts(parts_of(mix.T), back_two, 0) * (1.0 - hidden_one * hidden_one)
    )
    grads[:, MIX_AT - 128 : PACKED] = jnp.zeros((HIDDEN, PACKED - MIX_AT + 128), f32)
    grads[:, 0:TAPS] = dot_parts(back_one, taps, 1)
    grads[:, MIX_AT : MIX_AT + HIDDEN] = dot_parts(back_two, one, 1)
    grads[:, OUT_AT : OUT_AT + CHANNELS] = dot_parts(two, back_out, 1)
    area = jnp.sum(weight[0:2, :], axis=(0, 1), keepdims=True)
    grads[:, AREA_AT : AREA_AT + 1] = jnp.broadcast_to(area, (HIDDEN, 1))
    half = HIDDEN // 2
    for core, out in ((place[0], own), (1 - place[0], other)):
        rows = pl.ds(pl.multiple_of(core * half, half), half)
        for block in range(PACKED // 128):
            out[half * block : half * (block + 1), :] = grads[rows, 128 * block : 128 * (block + 1)]


def descended(place, packed, part, back):
    half = HIDDEN // 2
    first = place[0] == 0
    blocks = []
    for block in range(PACKED // 128):
        mine, theirs = (ref[half * block : half * (block + 1), :] for ref in (part, back))
        blocks.append(
            jnp.concatenate([jnp.where(first, mine, theirs), jnp.where(first, theirs, mine)], 0)
        )
    area = blocks[AREA_AT // 128][0:1, AREA_AT % 128 : AREA_AT % 128 + 1]
    step = (learn_rate * 2.0 / CHANNELS) / area
    return packed[...] - step * jnp.concatenate(blocks, 1)


def next_network_kernel(
    place, x, inner, outer, low, high, target, weight, packed, part, back, renewed, *rest
):
    renewed[...] = descended(place, packed, part, back)
    network_step(place, x, inner, outer, low, high, target, weight, renewed, *rest)


def last_kernel(place, packed, part, back, kernel, mix, out):
    renewed = descended(place, packed, part, back)
    kernel[...] = renewed[:, 0:TAPS].T
    mix[...] = renewed[:, MIX_AT : MIX_AT + HIDDEN]
    out[...] = renewed[:, OUT_AT : OUT_AT + CHANNELS].T


def forcing(place, x, pred, packed, west, east, low, high, taps):
    rows = coarse_rows(x, west, east)
    columns = column_matrix(low, high, west, east)
    fill_taps(taps, rows, columns, (1, 4))
    fill_side_taps(taps, rows, columns, 2 * COARSE)
    inputs = tuple(ref[...] for ref in taps)
    hidden = jnp.tanh(dot_parts(parts_of(packed[:, 0:TAPS]), inputs, 0))
    hidden = jnp.tanh(
        dot_parts(parts_of(packed[:, MIX_AT : MIX_AT + HIDDEN]), parts_of(hidden), 0)
    )
    beside = dot_parts(
        parts_of(packed[:, OUT_AT : OUT_AT + CHANNELS].T), parts_of(hidden), 0
    )
    sides = beside[:, 2 * COARSE :]
    sides_low = jnp.where(place[1] == 0, 0.0, sides)
    sides_high = jnp.where(place[2] == 0, 0.0, sides)
    before = (beside[:, 0:COARSE], pred[0:CHANNELS, :])
    after = (pred[CHANNELS : 2 * CHANNELS, :], beside[:, COARSE : 2 * COARSE])
    pieces = []
    for row in range(2):
        value = pred[CHANNELS * row : CHANNELS * (row + 1), :]
        along = after[row] - before[row]
        south, _, north = shifted_rows(value, sides_low[:, row : row + 1], sides_high[:, 2 + row : 3 + row])
        across = north - south
        for at in (0, 2 * LEVELS):
            pieces.append(-0.5 * (along[at : at + LEVELS] + across[at + LEVELS : at + 2 * LEVELS]))
            pieces.append(jnp.zeros((4, COARSE), f32))
    return exact_dot(jnp.concatenate(pieces, 0), spreading_matrix())


def advance(t, s, u, v, mask, force, fixed, moving, t_out, s_out):
    fixed_west, fixed_east, fixed_low, fixed_high = fixed
    west, east, low, high = moving
    m = mask[...]
    shape = (8, FINE)
    lanes = lane_index(shape)
    subs = lax.broadcasted_iota(jnp.int32, shape, 0)

    def edge_row(ref, at):
        depth = (ref.shape[0] - EDGE_AT) // 4
        starts = [EDGE_AT + depth * block + at for block in range(4)]
        return jnp.concatenate([ref[start : start + 1, :] for start in starts], 1)

    def neighbours_lon(value, row_west, row_east):
        return (
            jnp.where(subs == 0, row_west, pltpu.roll(value, 1, 0)),
            jnp.where(subs == 7, row_east, pltpu.roll(value, 7, 0)),
        )

    def neighbours_lat(value, column_low, column_high):
        return (
            jnp.where(lanes == 0, column_low, pltpu.roll(value, 1, 1)),
            jnp.where(lanes == FINE - 1, column_high, pltpu.roll(value, FINE - 1, 1)),
        )

    fixed_low_turned = fixed_low[...].T
    fixed_high_turned = fixed_high[...].T
    low_turned = low[...].T
    high_turned = high[...].T
    m_west, m_east = neighbours_lon(
        m, edge_row(fixed_west, 3 * LEVELS), edge_row(fixed_east, 3 * LEVELS)
    )
    m_low, m_high = neighbours_lat(m, fixed_low_turned[0:8, 3:4], fixed_high_turned[0:8, 3:4])
    open_west, open_east, open_low, open_high = m * m_west, m * m_east, m * m_low, m * m_high
    mix_west, mix_east = diffusivity * open_west, diffusivity * open_east
    mix_low, mix_high = diffusivity * open_low, diffusivity * open_high
    pace = time_step * m
    for level in range(LEVELS):
        at = slice(8 * level, 8 * (level + 1))
        u_here, v_here = u[at, :], v[at, :]
        u_west, u_east = neighbours_lon(
            u_here, edge_row(fixed_west, 2 * LEVELS + level), edge_row(fixed_east, 2 * LEVELS + level)
        )
        v_low, v_high = neighbours_lat(v_here, fixed_low_turned[at, 2:3], fixed_high_turned[at, 2:3])
        speed_west = 0.25 * (u_here + u_west) * open_west
        speed_east = 0.25 * (u_here + u_east) * open_east
        speed_low = 0.25 * (v_here + v_low) * open_low
        speed_high = 0.25 * (v_here + v_high) * open_high
        for which, (q_ref, out) in enumerate(((t, t_out), (s, s_out))):
            q = q_ref[at, :]
            q_west, q_east = neighbours_lon(
                q, edge_row(west, LEVELS * which + level), edge_row(east, LEVELS * which + level)
            )
            q_low, q_high = neighbours_lat(
                q, low_turned[at, which : which + 1], high_turned[at, which : which + 1]
            )
            flux_east = speed_east * (q + q_east) - mix_east * (q_east - q)
            flux_west = speed_west * (q_west + q) - mix_west * (q - q_west)
            flux_high = speed_high * (q + q_high) - mix_high * (q_high - q)
            flux_low = speed_low * (q_low + q) - mix_low * (q - q_low)
            row = 16 * which + level
            push = jnp.where(subs < 4, force[row : row + 1], force[32 + row : 33 + row])
            out[at, :] = q + pace * (push - (flux_east - flux_west) - (flux_high - flux_low))


def first_advance_kernel(place, *refs):
    t, s, u, v, mask, x, pred, packed, inner, outer, low, high = refs[:12]
    t_out, s_out, x_out, target, inner_out, outer_out, near, far = refs[12:20]
    sums, blocks, *taps = refs[20:24]
    t_here, s_here, u_here, v_here, semaphore = refs[24:]
    here = (t_here, s_here, u_here, v_here)
    copies = fetch(list(zip((t, s, u, v), here)), semaphore)
    halo = (*sides(place, inner, outer), low, high)
    force = forcing(place, x, pred, packed, *halo, taps)
    for copy in copies:
        copy.wait()
    advance(*here, mask, force, halo, halo, t_out, s_out)
    fill_blocks(blocks, (t_out, s_out, u_here, v_here))
    coarsen(blocks, sums, x_out, target)
    fill_edges(place, blocks, 2, (0, 1), None, x_out, inner_out, outer_out, near, far)


def next_advance_kernel(place, *refs):
    t, s, u, v, mask, x, pred, packed = refs[:8]
    fixed, moving, (t_out, s_out, *taps) = refs[8:12], refs[12:16], refs[16:]
    fixed = (*sides(place, *fixed[:2]), *fixed[2:])
    moving = (*sides(place, *moving[:2]), *moving[2:])
    force = forcing(place, x, pred, packed, *moving, taps)
    advance(t, s, u, v, mask, force, fixed, moving, t_out, s_out)


def swap_lon(inner, outer):
    axis = ("lon", "grp")
    count = lax.axis_size("lon") * lax.axis_size("grp")
    chips = [(i, (i + (1 if i % 2 else -1)) % count) for i in range(count)]
    outer = lax.ppermute(outer, axis, chips)
    return lax.ppermute(inner, "grp", flipped("grp", 1)), outer


def swap_lat(near, far):
    last = lax.axis_size("lat") - 1
    beyond = [(i, i ^ 3) for i in range(1, last)]
    return lax.ppermute(near, "lat", flipped("lat", 1)), lax.ppermute(far, "lat", beyond)


def south_north(near, far):
    lat = lax.axis_index("lat")
    odd = lat % 2 == 1
    south, north = jnp.where(odd, near, far), jnp.where(odd, far, near)
    south = jnp.where(lat == 0, 0.0, south)
    return south, jnp.where(lat == lax.axis_size("lat") - 1, 0.0, north)


def halo(inner, outer, near, far):
    south, north = south_north(near, far)
    columns = jnp.concatenate([south, north], 0)
    inner = lax.dynamic_update_slice_in_dim(inner, columns, COLUMNS_AT, 0)
    outer = lax.dynamic_update_slice_in_dim(outer, columns, COLUMNS_AT, 0)
    return *swap_lon(inner, outer), south, north


def flipped(axis, mask):
    return [(i, i ^ mask) for i in range(lax.axis_size(axis))]


def from_chip(value, mask):
    count = lax.axis_size("lon") * lax.axis_size("lat")
    return lax.ppermute(value, ("lon", "lat"), [(i, i ^ mask) for i in range(count)])


def sum_over_devices(own, other, beside):
    rows = own.shape[0]
    part = own + lax.ppermute(other, "grp", flipped("grp", 1))
    part = part + from_chip(part, 4)
    part, riders, extra = beside(part)
    near = from_chip(jnp.concatenate([part, *riders[:1]], 0), 1)
    cross = from_chip(part, 6)
    far = from_chip(jnp.concatenate([part, *riders[1:]], 0), 3)
    part = (part + near[:rows]) + (cross + far[:rows])
    extra = extra(near[rows:], far[rows:])
    if lax.axis_size("lon") > 2:
        for bit in (8, 32):
            one, two, three = (from_chip(part, bit * step) for step in (1, 2, 3))
            part = (part + one) + (two + three)
    return part, lax.ppermute(part, "grp", flipped("grp", 1)), extra


def shards(
    thermal_anomaly,
    saltiness_anomaly,
    zonal_flow_speed,
    meridional_flow_speed,
    water_indicator,
    kernel_factors,
    hidden_pointwise_factors,
    final_pointwise_factors,
):
    fields = tuple(
        value.reshape(8 * LEVELS, FINE)
        for value in (thermal_anomaly, saltiness_anomaly, zonal_flow_speed, meridional_flow_speed)
    )
    packed = jnp.concatenate(
        [
            kernel_factors.reshape(HIDDEN, TAPS),
            jnp.zeros((HIDDEN, MIX_AT - TAPS), f32),
            hidden_pointwise_factors,
            final_pointwise_factors.T,
            jnp.zeros((HIDDEN, PACKED - AREA_AT), f32),
        ],
        1,
    )
    blocks = pltpu.VMEM((16 * 8 * LEVELS, 128), f32)
    lat = lax.axis_index("lat")
    lat_last = lax.axis_size("lat") - 1
    place = jnp.stack(
        [lax.axis_index("grp"), (lat != 0).astype(jnp.int32), (lat != lat_last).astype(jnp.int32), lat % 2]
    ).astype(jnp.int32)
    field_scratch = pltpu.VMEM((8 * LEVELS, FINE), f32)
    sums = [pltpu.VMEM((4 * CHANNELS, FINE), f32), pltpu.VMEM((16 * 8 * LEVELS, 128), f32)]
    wide = struct(2 * CHANNELS, COARSE)
    tile = struct(8, 128)
    half = struct(HIDDEN // 2 * PACKED // 128, 128)
    field = struct(8 * LEVELS, FINE)
    network_outs = [wide, half, half]
    network_scratch = [pltpu.VMEM((TAPS, 2 * COARSE), bf16)] * 2 + [pltpu.VMEM((HIDDEN, PACKED), f32)]
    side_taps = [pltpu.VMEM((TAPS, 3 * COARSE), bf16)] * 2

    edge = struct(EDGE_AT + 160, 128)
    x, target, weight, mask, *edges = call(
        prepare_kernel,
        [wide, wide, tile, struct(8, FINE), edge, edge, tile, tile],
        place, *fields, water_indicator,
        scratch=sums
        + [
            pltpu.VMEM((8, FINE), jnp.int32),
            pltpu.SemaphoreType.DMA((17,)),
        ],
        smem=1,
        remote=5,
    )
    fixed = halo(*edges[:2], *swap_lat(*edges[2:]))
    pred, own, other = call(
        network_step,
        network_outs,
        place, x, *fixed, target, weight, packed,
        scratch=network_scratch,
        smem=1,
    )
    edge = struct(EDGE_AT + 96, 128)

    def first_advance(part):
        t, s, x_next, target_next, *edges = call(
            first_advance_kernel,
            [field, field, wide, wide, edge, edge, tile, tile],
            place, *fields, mask, x, pred, packed, *fixed,
            scratch=sums + side_taps + [field_scratch] * 4 + [pltpu.SemaphoreType.DMA((4,))],
            smem=1,
            remote=4,
        )
        inner, outer, *riders = edges
        state = t, s, x_next, target_next
        return part, riders, lambda near, far: (*state, halo(inner, outer, near, far))

    part, back, (t, s, x, target, moving) = sum_over_devices(own, other, first_advance)
    packed, pred, own, other = call(
        next_network_kernel,
        [struct(HIDDEN, PACKED)] + network_outs,
        place, x, *moving, target, weight, packed, part, back,
        scratch=network_scratch,
        smem=1,
    )

    def next_advance(part):
        fields_next = call(
            next_advance_kernel,
            [field, field],
            place, t, s, *fields[2:], mask, x, pred, packed, *fixed, *moving,
            scratch=side_taps,
            smem=1,
        )
        part, *fields_next = lax.optimization_barrier((part, *fields_next))
        return part, [], lambda near, far: fields_next

    part, back, (t, s) = sum_over_devices(own, other, next_advance)
    kernel, mix, out = call(
        last_kernel,
        [struct(TAPS, HIDDEN), struct(HIDDEN, HIDDEN), struct(CHANNELS, HIDDEN)],
        place, packed, part, back,
        smem=1,
    )
    return (
        t.reshape(thermal_anomaly.shape),
        s.reshape(thermal_anomaly.shape),
        kernel.T.reshape(kernel_factors.shape),
        mix,
        out,
    )


def solution(mesh):
    field = P(None, ("lon", "grp"), "lat")
    return jax.shard_map(
        shards,
        mesh=mesh,
        in_specs=(field, field, field, field, P(("lon", "grp"), "lat"), P(), P(), P()),
        out_specs=(field, field, P(), P(), P()),
        check_vma=False,
    )
```

```python
import functools

import jax
import jax.numpy as jnp
from jax import lax
from jax.experimental import pallas as pl
from jax.experimental.pallas import tpu as pltpu
from jax.sharding import PartitionSpec as P

time_step = 0.2
diffusivity = 0.5
learn_rate = 200.0
f32 = jnp.float32
bf16 = jnp.bfloat16

LEVELS = 12
CHANNELS = 4 * LEVELS
HIDDEN = 64
TAPS = 9 * CHANNELS
MIX_AT = 512
OUT_AT = 576
AREA_AT = 624
PACKED = 640
FINE = 512
COARSE = 128
VMEM_LIMIT = 48 * 1024 * 1024


def struct(*shape):
    return jax.ShapeDtypeStruct(shape, f32)


def call(kernel, outs, *args, scratch=(), remote=0, flops=0, bytes_accessed=0):
    args = [
        pltpu.with_memory_space_constraint(arg, pltpu.HBM) if at < remote else arg
        for at, arg in enumerate(args)
    ]
    specs = []
    specs += [pl.BlockSpec(memory_space=pltpu.HBM)] * remote
    specs += [pl.BlockSpec(memory_space=pltpu.VMEM)] * (len(args) - remote)
    return pl.pallas_call(
        kernel,
        out_shape=outs,
        in_specs=specs,
        out_specs=[pl.BlockSpec(memory_space=pltpu.VMEM)] * len(outs),
        scratch_shapes=scratch,
        compiler_params=pltpu.CompilerParams(vmem_limit_bytes=VMEM_LIMIT),
        cost_estimate=pl.CostEstimate(
            flops=flops, bytes_accessed=bytes_accessed, transcendentals=0
        ),
    )(*args)


def exact_dot(value, selector):
    high = value.astype(bf16)
    rest = value - high.astype(f32)
    middle = rest.astype(bf16)
    low = (rest - middle.astype(f32)).astype(bf16)
    dot = functools.partial(jnp.dot, preferred_element_type=f32)
    return (dot(low, selector) + dot(middle, selector)) + dot(high, selector)


def pooling_matrix():
    fine = lax.broadcasted_iota(jnp.int32, (FINE, COARSE), 0) >> 2
    coarse = lax.broadcasted_iota(jnp.int32, (FINE, COARSE), 1)
    return jnp.where(fine == coarse, f32(1.0 / 16.0), f32(0.0)).astype(bf16)


def spreading_matrix():
    fine = lax.broadcasted_iota(jnp.int32, (COARSE, FINE), 1) >> 2
    coarse = lax.broadcasted_iota(jnp.int32, (COARSE, FINE), 0)
    return jnp.where(fine == coarse, f32(1.0), f32(0.0)).astype(bf16)


def lane_index(shape):
    return lax.broadcasted_iota(jnp.int32, shape, len(shape) - 1)


def block_rows(which, block):
    start = (4 * which + block) * 8 * LEVELS
    return slice(start, start + 8 * LEVELS)


def fill_blocks(blocks, refs):
    for which, ref in enumerate(refs):
        for block in range(4):
            blocks[block_rows(which, block), :] = ref[:, 128 * block : 128 * (block + 1)]


def fetch(pairs, semaphore):
    copies = [
        pltpu.make_async_copy(source, target, semaphore.at[at])
        for at, (source, target) in enumerate(pairs)
    ]
    for copy in copies:
        copy.start()
    return copies


def longitude_row(blocks, which, block, lon):
    return blocks[pl.ds(block_rows(which, block).start + lon, LEVELS, stride=8), :]


def coarsen(blocks, sums_ref, x_ref, target_ref):
    for row in range(2):
        for block in range(4):
            total = None
            for lon in range(4 * row, 4 * row + 4):
                t, s, u, v = (longitude_row(blocks, which, block, lon) for which in range(4))
                terms = (t, s, u, v, u * t, v * t, u * s, v * s)
                total = terms if total is None else [a + b for a, b in zip(total, terms)]
            for at, value in enumerate(total):
                start = 2 * CHANNELS * row + LEVELS * at
                sums_ref[start : start + LEVELS, 128 * block : 128 * (block + 1)] = value
    means = exact_dot(sums_ref[...], pooling_matrix())
    for row in range(2):
        x = means[2 * CHANNELS * row : 2 * CHANNELS * row + CHANNELS]
        products = means[2 * CHANNELS * row + CHANNELS : 2 * CHANNELS * (row + 1)]
        ct, cs, cu, cv = (x[LEVELS * k : LEVELS * (k + 1)] for k in range(4))
        x_ref[CHANNELS * row : CHANNELS * (row + 1), :] = x
        own = jnp.concatenate([cu * ct, cv * ct, cu * cs, cv * cs], 0)
        target_ref[CHANNELS * row : CHANNELS * (row + 1), :] = products - own


class Either:
    def __init__(self, flag, one, other):
        self.flag, self.one, self.other, self.shape = flag, one, other, one.shape

    def __getitem__(self, at):
        return jnp.where(self.flag, self.one[at], self.other[at])


def sides(inner, outer):
    first = lax.axis_index("grp") == 0
    return Either(first, outer, inner), Either(first, inner, outer)


def edge_layout(ref):
    first = 2 * CHANNELS
    return first, (ref.shape[0] - first) // 4


def fill_edges(blocks, fields, mask_ref, x_ref, inner_ref, outer_ref):
    core_first = lax.axis_index("grp") == 0
    first_row, depth = edge_layout(inner_ref)
    for out in (inner_ref, outer_ref):
        out[0:first_row, :] = x_ref[...]
        out[first_row:, :] = jnp.zeros((out.shape[0] - first_row, COARSE), f32)

    def put(rows, first, last):
        inner_ref[rows, :] = jnp.where(core_first, last, first)
        outer_ref[rows, :] = jnp.where(core_first, first, last)

    for block in range(4):
        start = first_row + block * depth
        for which in range(fields):
            at = start + which * LEVELS
            put(
                slice(at, at + LEVELS),
                longitude_row(blocks, which, block, 0),
                longitude_row(blocks, which, block, 7),
            )
        if mask_ref is not None:
            at = start + fields * LEVELS
            lanes = slice(128 * block, 128 * (block + 1))
            put(slice(at, at + 1), mask_ref[0:1, lanes], mask_ref[7:8, lanes])


def put_columns(near_ref, far_ref, at, low, high):
    odd = lax.axis_index("lat") % 2 == 1
    near_ref[at : at + 1, 0 : low.shape[1]] = jnp.where(odd, low, high)
    far_ref[at : at + 1, 0 : low.shape[1]] = jnp.where(odd, high, low)


def fill_columns(blocks, column_fields, mask_ref, near_ref, far_ref):
    near_ref[...] = jnp.zeros(near_ref.shape, f32)
    far_ref[...] = jnp.zeros(far_ref.shape, f32)
    for at, which in enumerate(column_fields):
        low, high = (blocks[block_rows(which, block), :].T for block in (0, 3))
        put_columns(near_ref, far_ref, at, low[0:1], high[127:128])
    if mask_ref is not None:
        low, high = mask_ref[:, 0:128].T[0:1], mask_ref[:, FINE - 128 : FINE].T[127:128]
        put_columns(near_ref, far_ref, 3, low, high)


def columns_kernel(x, x_inner, x_outer, near_fine, far_fine, near, far):
    for fine, out in ((near_fine, near), (far_fine, far)):
        out[0:8, :] = fine[...]
        out[8:16, :] = jnp.zeros((8, COARSE), f32)
    rows = slice(0, 2 * CHANNELS)
    for at, ref in enumerate((x, *sides(x_inner, x_outer))):
        turned = ref[rows, :].T
        put_columns(near, far, 8 + 2 * at, turned[0:1], turned[127:128])
        put_columns(near, far, 9 + 2 * at, turned[1:2], turned[126:127])


def block_copies(refs, blocks):
    return [
        (ref.at[:, pl.ds(128 * block, 128)], blocks.at[block_rows(which, block), :])
        for which, ref in enumerate(refs)
        for block in range(4)
    ]


def prepare_kernel(
    t, s, u, v, mask, x, target, weight, mask_values, inner, outer, sums, blocks, mask_here, semaphore
):
    copies = fetch([(mask, mask_here)] + block_copies((t, s, u, v), blocks), semaphore)
    for copy in copies:
        copy.wait()
    m = mask_here[...].astype(f32)
    mask_values[...] = m
    coarsen(blocks, sums, x, target)
    fill_edges(blocks, 3, mask_values, x, inner, outer)
    rows = jnp.concatenate(
        [jnp.sum(m[0:4], axis=0, keepdims=True), jnp.sum(m[4:8], axis=0, keepdims=True)]
        + [jnp.zeros((6, FINE), f32)],
        0,
    )
    weight[...] = jnp.dot(rows.astype(bf16), pooling_matrix(), preferred_element_type=f32)


def fine_columns_kernel(t, s, v, mask, near, far, blocks, semaphore):
    for copy in fetch(block_copies((t, s, v), blocks), semaphore):
        copy.wait()
    fill_columns(blocks, (0, 1, 2), mask, near, far)


def parts_of(value):
    high = value.astype(bf16)
    return high, (value - high.astype(f32)).astype(bf16)


def dot_parts(a, b, contract):
    (a_high, a_low), (b_high, b_low) = a, b
    dims = (((1,), (contract,)), ((), ()))
    dot = functools.partial(lax.dot_general, dimension_numbers=dims, preferred_element_type=f32)
    rows = a_high.shape[0]
    both = dot(jnp.concatenate([a_high, a_low], 0), b_high)
    return both[:rows] + (both[rows:] + dot(a_high, b_low))


def column_matrix(low, high):
    rows = []
    for at in (8, 9):
        for side in range(3):
            rows += [ref[at + 2 * side : at + 2 * side + 1, :] for ref in (low, high)]
    rows.append(jnp.zeros((4, COARSE), f32))
    return jnp.concatenate(rows, 0).T


def shifted_rows(value, before, after):
    lanes = lane_index((CHANNELS, COARSE))
    return (
        jnp.where(lanes == 0, before, pltpu.roll(value, 1, 1)),
        value,
        jnp.where(lanes == COARSE - 1, after, pltpu.roll(value, COARSE - 1, 1)),
    )


def coarse_rows(x, west, east):
    return (
        (west[0:CHANNELS, :], 0, 2),
        (west[CHANNELS : 2 * CHANNELS, :], CHANNELS, 2),
        (x[0:CHANNELS, :], 0, 0),
        (x[CHANNELS : 2 * CHANNELS, :], CHANNELS, 0),
        (east[0:CHANNELS, :], 0, 4),
        (east[CHANNELS : 2 * CHANNELS, :], CHANNELS, 4),
    )


def fill_taps(taps, rows, columns, centres):
    for at, (value, start, pair) in enumerate(rows):
        if not any(abs(at - centre) <= 1 for centre in centres):
            continue
        channels = slice(start, start + CHANNELS)
        shifted = [
            parts_of(part)
            for part in shifted_rows(
                value, columns[channels, pair : pair + 1], columns[channels, pair + 1 : pair + 2]
            )
        ]
        for place, centre in enumerate(centres):
            tap = at - centre + 1
            if 0 <= tap < 3:
                for side in range(3):
                    begin = (3 * tap + side) * CHANNELS
                    for out, part in zip(taps, shifted[side]):
                        out[begin : begin + CHANNELS, COARSE * place : COARSE * (place + 1)] = part


def fill_side_taps(taps, rows, columns, start_lane):
    lanes = lane_index((CHANNELS, COARSE))
    for tap in range(3):
        for side in range(3):
            out = jnp.zeros((CHANNELS, COARSE), f32)
            for row in range(2):
                value, start, pair = rows[row + tap + 1]
                channels = slice(start, start + CHANNELS)
                low = (
                    columns[channels, 6 + pair : 7 + pair],
                    columns[channels, pair : pair + 1],
                    value[:, 0:1],
                )[side]
                high = (
                    value[:, COARSE - 1 : COARSE],
                    columns[channels, pair + 1 : pair + 2],
                    columns[channels, 7 + pair : 8 + pair],
                )[side]
                out = jnp.where(lanes == row, low, out)
                out = jnp.where(lanes == 2 + row, high, out)
            begin = (3 * tap + side) * CHANNELS
            for ref, part in zip(taps, parts_of(out)):
                ref[begin : begin + CHANNELS, start_lane : start_lane + COARSE] = part


def network_step(
    x, inner, outer, low, high, target, weight, packed, pred, own, other, taps_high, taps_low, grads
):
    west, east = sides(inner, outer)
    columns = column_matrix(low, high)
    fill_taps((taps_high, taps_low), coarse_rows(x, west, east), columns, (2, 3))
    taps = taps_high[...], taps_low[...]
    kernel = parts_of(packed[:, 0:TAPS])
    mix = packed[:, MIX_AT : MIX_AT + HIDDEN]
    out_turned = packed[:, OUT_AT : OUT_AT + CHANNELS]
    hidden_one = jnp.tanh(dot_parts(kernel, taps, 0))
    one = parts_of(hidden_one)
    hidden_two = jnp.tanh(dot_parts(parts_of(mix), one, 0))
    two = parts_of(hidden_two)
    predicted = dot_parts(parts_of(out_turned.T), two, 0)
    pred[0:CHANNELS, :] = predicted[:, 0:COARSE]
    pred[CHANNELS : 2 * CHANNELS, :] = predicted[:, COARSE : 2 * COARSE]
    back_out = parts_of(
        jnp.concatenate(
            [
                weight[row : row + 1, :]
                * (
                    predicted[:, COARSE * row : COARSE * (row + 1)]
                    - target[CHANNELS * row : CHANNELS * (row + 1), :]
                )
                for row in range(2)
            ],
            1,
        )
    )
    back_two = parts_of(
        dot_parts(parts_of(out_turned), back_out, 0) * (1.0 - hidden_two * hidden_two)
    )
    back_one = parts_of(
        dot_parts(parts_of(mix.T), back_two, 0) * (1.0 - hidden_one * hidden_one)
    )
    grads[:, MIX_AT - 128 : PACKED] = jnp.zeros((HIDDEN, PACKED - MIX_AT + 128), f32)
    grads[:, 0:TAPS] = dot_parts(back_one, taps, 1)
    grads[:, MIX_AT : MIX_AT + HIDDEN] = dot_parts(back_two, one, 1)
    grads[:, OUT_AT : OUT_AT + CHANNELS] = dot_parts(two, back_out, 1)
    area = jnp.sum(weight[0:2, :], axis=(0, 1), keepdims=True)
    grads[:, AREA_AT : AREA_AT + 1] = jnp.broadcast_to(area, (HIDDEN, 1))
    half = HIDDEN // 2
    here = lax.axis_index("grp")
    for core, out in ((here, own), (1 - here, other)):
        rows = pl.ds(pl.multiple_of(core * half, half), half)
        for block in range(PACKED // 128):
            out[half * block : half * (block + 1), :] = grads[rows, 128 * block : 128 * (block + 1)]


def descended(packed, part, back):
    half = HIDDEN // 2
    first = lax.axis_index("grp") == 0
    blocks = []
    for block in range(PACKED // 128):
        mine, theirs = (ref[half * block : half * (block + 1), :] for ref in (part, back))
        blocks.append(
            jnp.concatenate([jnp.where(first, mine, theirs), jnp.where(first, theirs, mine)], 0)
        )
    area = blocks[AREA_AT // 128][0:1, AREA_AT % 128 : AREA_AT % 128 + 1]
    step = (learn_rate * 2.0 / CHANNELS) / area
    return packed[...] - step * jnp.concatenate(blocks, 1)


def next_network_kernel(*refs):
    *ins, packed, part, back, renewed = refs[:11]
    renewed[...] = descended(packed, part, back)
    network_step(*ins, renewed, *refs[11:])


def last_kernel(packed, part, back, kernel, mix, out):
    renewed = descended(packed, part, back)
    kernel[...] = renewed[:, 0:TAPS].T
    mix[...] = renewed[:, MIX_AT : MIX_AT + HIDDEN]
    out[...] = renewed[:, OUT_AT : OUT_AT + CHANNELS].T


def forcing(x, pred, packed, halo, taps):
    west, east, low, high = halo
    rows = coarse_rows(x, west, east)
    columns = column_matrix(low, high)
    fill_taps(taps, rows, columns, (1, 4))
    fill_side_taps(taps, rows, columns, 2 * COARSE)
    inputs = tuple(ref[...] for ref in taps)
    hidden = jnp.tanh(dot_parts(parts_of(packed[:, 0:TAPS]), inputs, 0))
    hidden = jnp.tanh(
        dot_parts(parts_of(packed[:, MIX_AT : MIX_AT + HIDDEN]), parts_of(hidden), 0)
    )
    beside = dot_parts(
        parts_of(packed[:, OUT_AT : OUT_AT + CHANNELS].T), parts_of(hidden), 0
    )
    sides = beside[:, 2 * COARSE :]
    lat = lax.axis_index("lat")
    sides_low = jnp.where(lat == 0, 0.0, sides)
    sides_high = jnp.where(lat == lax.axis_size("lat") - 1, 0.0, sides)
    before = (beside[:, 0:COARSE], pred[0:CHANNELS, :])
    after = (pred[CHANNELS : 2 * CHANNELS, :], beside[:, COARSE : 2 * COARSE])
    pieces = []
    for row in range(2):
        value = pred[CHANNELS * row : CHANNELS * (row + 1), :]
        along = after[row] - before[row]
        south, _, north = shifted_rows(value, sides_low[:, row : row + 1], sides_high[:, 2 + row : 3 + row])
        across = north - south
        for at in (0, 2 * LEVELS):
            pieces.append(-0.5 * (along[at : at + LEVELS] + across[at + LEVELS : at + 2 * LEVELS]))
            pieces.append(jnp.zeros((4, COARSE), f32))
    return exact_dot(jnp.concatenate(pieces, 0), spreading_matrix())


def advance(t, s, u, v, mask, force, fixed, moving, t_out, s_out):
    fixed_west, fixed_east, fixed_low, fixed_high = fixed
    west, east, low, high = moving
    m = mask[...]
    shape = (8, FINE)
    lanes = lane_index(shape)
    subs = lax.broadcasted_iota(jnp.int32, shape, 0)

    def edge_row(ref, at):
        first, depth = edge_layout(ref)
        starts = [first + depth * block + at for block in range(4)]
        return jnp.concatenate([ref[start : start + 1, :] for start in starts], 1)

    def neighbours_lon(value, row_west, row_east):
        return (
            jnp.where(subs == 0, row_west, pltpu.roll(value, 1, 0)),
            jnp.where(subs == 7, row_east, pltpu.roll(value, 7, 0)),
        )

    def neighbours_lat(value, column_low, column_high):
        return (
            jnp.where(lanes == 0, column_low, pltpu.roll(value, 1, 1)),
            jnp.where(lanes == FINE - 1, column_high, pltpu.roll(value, FINE - 1, 1)),
        )

    fixed_low_turned = fixed_low[...].T
    fixed_high_turned = fixed_high[...].T
    low_turned = low[...].T
    high_turned = high[...].T
    m_west, m_east = neighbours_lon(
        m, edge_row(fixed_west, 3 * LEVELS), edge_row(fixed_east, 3 * LEVELS)
    )
    m_low, m_high = neighbours_lat(m, fixed_low_turned[0:8, 3:4], fixed_high_turned[0:8, 3:4])
    open_west, open_east, open_low, open_high = m * m_west, m * m_east, m * m_low, m * m_high
    mix_west, mix_east = diffusivity * open_west, diffusivity * open_east
    mix_low, mix_high = diffusivity * open_low, diffusivity * open_high
    pace = time_step * m
    for level in range(LEVELS):
        at = slice(8 * level, 8 * (level + 1))
        u_here, v_here = u[at, :], v[at, :]
        u_west, u_east = neighbours_lon(
            u_here, edge_row(fixed_west, 2 * LEVELS + level), edge_row(fixed_east, 2 * LEVELS + level)
        )
        v_low, v_high = neighbours_lat(v_here, fixed_low_turned[at, 2:3], fixed_high_turned[at, 2:3])
        speed_west = 0.25 * (u_here + u_west) * open_west
        speed_east = 0.25 * (u_here + u_east) * open_east
        speed_low = 0.25 * (v_here + v_low) * open_low
        speed_high = 0.25 * (v_here + v_high) * open_high
        for which, (q_ref, out) in enumerate(((t, t_out), (s, s_out))):
            q = q_ref[at, :]
            q_west, q_east = neighbours_lon(
                q, edge_row(west, LEVELS * which + level), edge_row(east, LEVELS * which + level)
            )
            q_low, q_high = neighbours_lat(
                q, low_turned[at, which : which + 1], high_turned[at, which : which + 1]
            )
            flux_east = speed_east * (q + q_east) - mix_east * (q_east - q)
            flux_west = speed_west * (q_west + q) - mix_west * (q - q_west)
            flux_high = speed_high * (q + q_high) - mix_high * (q_high - q)
            flux_low = speed_low * (q_low + q) - mix_low * (q - q_low)
            row = 16 * which + level
            push = jnp.where(subs < 4, force[row : row + 1], force[32 + row : 33 + row])
            out[at, :] = q + pace * (push - (flux_east - flux_west) - (flux_high - flux_low))


def around(inner, outer, low, high):
    return (*sides(inner, outer), low, high)


def first_advance_kernel(*refs):
    t, s, u, v, mask, x, pred, packed = refs[:8]
    halo = around(*refs[8:12])
    t_out, s_out, x_out, target, inner, outer, near, far = refs[12:20]
    sums, blocks, *taps = refs[20:24]
    t_here, s_here, u_here, v_here, semaphore = refs[24:]
    here = (t_here, s_here, u_here, v_here)
    copies = fetch(list(zip((t, s, u, v), here)), semaphore)
    force = forcing(x, pred, packed, halo, taps)
    for copy in copies:
        copy.wait()
    advance(*here, mask, force, halo, halo, t_out, s_out)
    fill_blocks(blocks, (t_out, s_out, u_here, v_here))
    coarsen(blocks, sums, x_out, target)
    fill_edges(blocks, 2, None, x_out, inner, outer)
    fill_columns(blocks, (0, 1), None, near, far)


def next_advance_kernel(*refs):
    t, s, u, v, mask, x, pred, packed = refs[:8]
    fixed, moving = around(*refs[8:12]), around(*refs[12:16])
    t_out, s_out, *taps = refs[16:]
    force = forcing(x, pred, packed, moving, taps)
    advance(t, s, u, v, mask, force, fixed, moving, t_out, s_out)


def swap_lon(inner, outer):
    axis = ("lon", "grp")
    count = lax.axis_size("lon") * lax.axis_size("grp")
    chips = [(i, (i + (1 if i % 2 else -1)) % count) for i in range(count)]
    outer = lax.ppermute(outer, axis, chips)
    return lax.ppermute(inner, "grp", flipped("grp", 1)), outer


def swap_lat(near, far):
    last = lax.axis_size("lat") - 1
    beyond = [(i, i ^ 3) for i in range(1, last)]
    return lax.ppermute(near, "lat", flipped("lat", 1)), lax.ppermute(far, "lat", beyond)


def south_north(near, far):
    lat = lax.axis_index("lat")
    odd = lat % 2 == 1
    south, north = jnp.where(odd, near, far), jnp.where(odd, far, near)
    south = jnp.where(lat == 0, 0.0, south)
    return south, jnp.where(lat == lax.axis_size("lat") - 1, 0.0, north)


def flipped(axis, mask):
    return [(i, i ^ mask) for i in range(lax.axis_size(axis))]


def from_chip(value, mask):
    count = lax.axis_size("lon") * lax.axis_size("lat")
    return lax.ppermute(value, ("lon", "lat"), [(i, i ^ mask) for i in range(count)])


def sum_of_four(part, bit):
    if lax.axis_size("lon") * lax.axis_size("lat") <= 2 * bit:
        return part
    one, two, three = (from_chip(part, bit * step) for step in (1, 2, 3))
    return (part + one) + (two + three)


def sum_over_devices(own, other, after_pair, riders):
    rows = own.shape[0]
    part = own + lax.ppermute(other, "grp", flipped("grp", 1))
    part = after_pair(part + from_chip(part, 4))
    for bit in (8, 32):
        part = sum_of_four(part, bit)
    near, far = riders()
    near = from_chip(jnp.concatenate([part, *near], 0), 1)
    cross = from_chip(part, 6)
    far = from_chip(jnp.concatenate([part, *far], 0), 3)
    part = (part + near[:rows]) + (cross + far[:rows])
    back = lax.ppermute(part, "grp", flipped("grp", 1))
    return part, back, (near[rows:], far[rows:])


def shards(
    thermal_anomaly,
    saltiness_anomaly,
    zonal_flow_speed,
    meridional_flow_speed,
    water_indicator,
    kernel_factors,
    hidden_pointwise_factors,
    final_pointwise_factors,
):
    fields = tuple(
        value.reshape(8 * LEVELS, FINE)
        for value in (thermal_anomaly, saltiness_anomaly, zonal_flow_speed, meridional_flow_speed)
    )
    packed = jnp.concatenate(
        [
            kernel_factors.reshape(HIDDEN, TAPS),
            jnp.zeros((HIDDEN, MIX_AT - TAPS), f32),
            hidden_pointwise_factors,
            final_pointwise_factors.T,
            jnp.zeros((HIDDEN, PACKED - AREA_AT), f32),
        ],
        1,
    )
    blocks = pltpu.VMEM((16 * 8 * LEVELS, 128), f32)
    field_scratch = pltpu.VMEM((8 * LEVELS, FINE), f32)
    sums = [pltpu.VMEM((4 * CHANNELS, FINE), f32), pltpu.VMEM((16 * 8 * LEVELS, 128), f32)]
    wide = struct(2 * CHANNELS, COARSE)
    tile = struct(8, 128)
    half = struct(HIDDEN // 2 * PACKED // 128, 128)
    field = struct(8 * LEVELS, FINE)
    network_outs = [wide, half, half]
    network_scratch = [pltpu.VMEM((TAPS, 2 * COARSE), bf16)] * 2 + [pltpu.VMEM((HIDDEN, PACKED), f32)]
    side_taps = [pltpu.VMEM((TAPS, 3 * COARSE), bf16)] * 2

    edge = struct(2 * CHANNELS + 160, 128)
    x, target, weight, mask, inner, outer = call(
        prepare_kernel,
        [wide, wide, tile, struct(8, FINE), edge, edge],
        *fields, water_indicator,
        scratch=sums + [pltpu.VMEM((8, FINE), jnp.int32), pltpu.SemaphoreType.DMA((17,))],
        remote=5,
    )
    near, far = call(
        fine_columns_kernel,
        [tile, tile],
        *fields[:2], fields[3], mask,
        scratch=[sums[1], pltpu.SemaphoreType.DMA((12,))],
        remote=3,
    )

    def columns(x, inner, outer, near, far):
        return call(columns_kernel, [struct(16, 128)] * 2, x, inner, outer, near, far)

    inner, outer = swap_lon(inner, outer)
    south, north = south_north(*swap_lat(*columns(x, inner, outer, near, far)))
    pred, own, other = call(
        network_step,
        network_outs,
        x, inner, outer, south, north, target, weight, packed,
        scratch=network_scratch,
    )
    edge = struct(2 * CHANNELS + 96, 128)
    later = {}

    fixed = inner, outer, south, north

    def first_advance(part):
        t, s, x_next, target, inner, outer, near, far = call(
            first_advance_kernel,
            [field, field, wide, wide, edge, edge, tile, tile],
            *fields, mask, x, pred, packed, *fixed,
            scratch=sums + side_taps + [field_scratch] * 4 + [pltpu.SemaphoreType.DMA((4,))],
            remote=4,
        )
        part, inner, outer = lax.optimization_barrier((part, inner, outer))
        later["state"] = t, s, x_next, target
        later["beside"] = swap_lon(inner, outer)
        later["columns"] = near, far
        return part

    def first_riders():
        x_next = later["state"][2]
        near, far = columns(x_next, *later["beside"], *later["columns"])
        return [near], [far]

    part, back, received = sum_over_devices(own, other, first_advance, first_riders)
    moving = *later["beside"], *south_north(*received)
    t, s, x, target = later["state"]
    packed, pred, own, other = call(
        next_network_kernel,
        [struct(HIDDEN, PACKED)] + network_outs,
        x, *moving, target, weight, packed, part, back,
        scratch=network_scratch,
    )

    def next_advance(part):
        fields_next = call(
            next_advance_kernel,
            [field, field],
            t, s, *fields[2:], mask, x, pred, packed, *fixed, *moving,
            scratch=side_taps,
        )
        part, *later["fields"] = lax.optimization_barrier((part, *fields_next))
        return part

    part, back, _ = sum_over_devices(own, other, next_advance, lambda: ([], []))
    t, s = later["fields"]
    kernel, mix, out = call(
        last_kernel,
        [struct(TAPS, HIDDEN), struct(HIDDEN, HIDDEN), struct(CHANNELS, HIDDEN)],
        packed, part, back,
    )
    return (
        t.reshape(thermal_anomaly.shape),
        s.reshape(thermal_anomaly.shape),
        kernel.T.reshape(kernel_factors.shape),
        mix,
        out,
    )


def solution(mesh):
    field = P(None, ("lon", "grp"), "lat")
    return jax.shard_map(
        shards,
        mesh=mesh,
        in_specs=(field, field, field, field, P(("lon", "grp"), "lat"), P(), P(), P()),
        out_specs=(field, field, P(), P(), P()),
        check_vma=False,
    )
```

```python
import functools

import jax
import jax.numpy as jnp
from jax import lax
from jax.experimental import pallas as pl
from jax.experimental.pallas import tpu as pltpu
from jax.sharding import PartitionSpec as P

time_step = 0.2
diffusivity = 0.5
learn_rate = 200.0
f32 = jnp.float32
bf16 = jnp.bfloat16

LEVELS = 12
CHANNELS = 4 * LEVELS
HIDDEN = 64
TAPS = 9 * CHANNELS
MIX_AT = 432
OUT_AT = 496
REST_AT = 512
USED = 544
PACKED = 640
HALF = HIDDEN // 2
SUMMED = 4 * HALF + 8
FINE = 512
COARSE = 128
VMEM_LIMIT = 48 * 1024 * 1024


def struct(*shape):
    return jax.ShapeDtypeStruct(shape, f32)


def call(kernel, outs, *args, scratch=(), remote=0, flops=0, bytes_accessed=0):
    args = [
        pltpu.with_memory_space_constraint(arg, pltpu.HBM) if at < remote else arg
        for at, arg in enumerate(args)
    ]
    specs = []
    specs += [pl.BlockSpec(memory_space=pltpu.HBM)] * remote
    specs += [pl.BlockSpec(memory_space=pltpu.VMEM)] * (len(args) - remote)
    return pl.pallas_call(
        kernel,
        out_shape=outs,
        in_specs=specs,
        out_specs=[pl.BlockSpec(memory_space=pltpu.VMEM)] * len(outs),
        scratch_shapes=scratch,
        compiler_params=pltpu.CompilerParams(vmem_limit_bytes=VMEM_LIMIT),
        cost_estimate=pl.CostEstimate(
            flops=flops, bytes_accessed=bytes_accessed, transcendentals=0
        ),
    )(*args)


def exact_dot(value, selector):
    high = value.astype(bf16)
    rest = value - high.astype(f32)
    middle = rest.astype(bf16)
    low = (rest - middle.astype(f32)).astype(bf16)
    dot = functools.partial(jnp.dot, preferred_element_type=f32)
    return (dot(low, selector) + dot(middle, selector)) + dot(high, selector)


def pooling_matrix():
    fine = lax.broadcasted_iota(jnp.int32, (FINE, COARSE), 0) >> 2
    coarse = lax.broadcasted_iota(jnp.int32, (FINE, COARSE), 1)
    return jnp.where(fine == coarse, f32(1.0 / 16.0), f32(0.0)).astype(bf16)


def spreading_matrix():
    fine = lax.broadcasted_iota(jnp.int32, (COARSE, FINE), 1) >> 2
    coarse = lax.broadcasted_iota(jnp.int32, (COARSE, FINE), 0)
    return jnp.where(fine == coarse, f32(1.0), f32(0.0)).astype(bf16)


def lane_index(shape):
    return lax.broadcasted_iota(jnp.int32, shape, len(shape) - 1)


def block_rows(which, block):
    start = (4 * which + block) * 8 * LEVELS
    return slice(start, start + 8 * LEVELS)


def fill_blocks(blocks, refs):
    for which, ref in enumerate(refs):
        for block in range(4):
            blocks[block_rows(which, block), :] = ref[:, 128 * block : 128 * (block + 1)]


def fetch(pairs, semaphore):
    copies = [
        pltpu.make_async_copy(source, target, semaphore.at[at])
        for at, (source, target) in enumerate(pairs)
    ]
    for copy in copies:
        copy.start()
    return copies


def longitude_row(blocks, which, block, lon):
    return blocks[pl.ds(block_rows(which, block).start + lon, LEVELS, stride=8), :]


def coarsen(blocks, sums_ref, x_ref, target_ref):
    for row in range(2):
        for block in range(4):
            total = None
            for lon in range(4 * row, 4 * row + 4):
                t, s, u, v = (longitude_row(blocks, which, block, lon) for which in range(4))
                terms = (t, s, u, v, u * t, v * t, u * s, v * s)
                total = terms if total is None else [a + b for a, b in zip(total, terms)]
            for at, value in enumerate(total):
                start = 2 * CHANNELS * row + LEVELS * at
                sums_ref[start : start + LEVELS, 128 * block : 128 * (block + 1)] = value
    means = exact_dot(sums_ref[...], pooling_matrix())
    for row in range(2):
        x = means[2 * CHANNELS * row : 2 * CHANNELS * row + CHANNELS]
        products = means[2 * CHANNELS * row + CHANNELS : 2 * CHANNELS * (row + 1)]
        ct, cs, cu, cv = (x[LEVELS * k : LEVELS * (k + 1)] for k in range(4))
        x_ref[CHANNELS * row : CHANNELS * (row + 1), :] = x
        own = jnp.concatenate([cu * ct, cv * ct, cu * cs, cv * cs], 0)
        target_ref[CHANNELS * row : CHANNELS * (row + 1), :] = products - own


class Either:
    def __init__(self, flag, one, other):
        self.flag, self.one, self.other, self.shape = flag, one, other, one.shape

    def __getitem__(self, at):
        return jnp.where(self.flag, self.one[at], self.other[at])


def sides(inner, outer):
    first = lax.axis_index("grp") == 0
    return Either(first, outer, inner), Either(first, inner, outer)


def edge_layout(ref):
    first = 2 * CHANNELS
    return first, (ref.shape[0] - first) // 4


def fill_edges(blocks, fields, mask_ref, x_ref, inner_ref, outer_ref):
    core_first = lax.axis_index("grp") == 0
    first_row, depth = edge_layout(inner_ref)
    for out in (inner_ref, outer_ref):
        out[0:first_row, :] = x_ref[...]
        out[first_row:, :] = jnp.zeros((out.shape[0] - first_row, COARSE), f32)

    def put(rows, first, last):
        inner_ref[rows, :] = jnp.where(core_first, last, first)
        outer_ref[rows, :] = jnp.where(core_first, first, last)

    for block in range(4):
        start = first_row + block * depth
        for which in range(fields):
            at = start + which * LEVELS
            put(
                slice(at, at + LEVELS),
                longitude_row(blocks, which, block, 0),
                longitude_row(blocks, which, block, 7),
            )
        if mask_ref is not None:
            at = start + fields * LEVELS
            lanes = slice(128 * block, 128 * (block + 1))
            put(slice(at, at + 1), mask_ref[0:1, lanes], mask_ref[7:8, lanes])


def put_columns(near_ref, far_ref, at, low, high):
    odd = lax.axis_index("lat") % 2 == 1
    near_ref[at : at + 1, 0 : low.shape[1]] = jnp.where(odd, low, high)
    far_ref[at : at + 1, 0 : low.shape[1]] = jnp.where(odd, high, low)


def fill_columns(blocks, column_fields, mask_ref, near_ref, far_ref):
    near_ref[...] = jnp.zeros(near_ref.shape, f32)
    far_ref[...] = jnp.zeros(far_ref.shape, f32)
    for at, which in enumerate(column_fields):
        low, high = (blocks[block_rows(which, block), :].T for block in (0, 3))
        put_columns(near_ref, far_ref, at, low[0:1], high[127:128])
    if mask_ref is not None:
        low, high = mask_ref[:, 0:128].T[0:1], mask_ref[:, FINE - 128 : FINE].T[127:128]
        put_columns(near_ref, far_ref, 3, low, high)


def columns_kernel(x, x_inner, x_outer, near_fine, far_fine, near, far):
    for fine, out in ((near_fine, near), (far_fine, far)):
        out[0:8, :] = fine[...]
        out[8:16, :] = jnp.zeros((8, COARSE), f32)
    rows = slice(0, 2 * CHANNELS)
    for at, ref in enumerate((x, *sides(x_inner, x_outer))):
        turned = ref[rows, :].T
        put_columns(near, far, 8 + 2 * at, turned[0:1], turned[127:128])
        put_columns(near, far, 9 + 2 * at, turned[1:2], turned[126:127])


def block_copies(refs, blocks):
    return [
        (ref.at[:, pl.ds(128 * block, 128)], blocks.at[block_rows(which, block), :])
        for which, ref in enumerate(refs)
        for block in range(4)
    ]


def prepare_kernel(
    t, s, u, v, mask, x, target, weight, mask_values, inner, outer, sums, blocks, mask_here, semaphore
):
    copies = fetch([(mask, mask_here)] + block_copies((t, s, u, v), blocks), semaphore)
    for copy in copies:
        copy.wait()
    m = mask_here[...].astype(f32)
    mask_values[...] = m
    coarsen(blocks, sums, x, target)
    fill_edges(blocks, 3, mask_values, x, inner, outer)
    rows = jnp.concatenate(
        [jnp.sum(m[0:4], axis=0, keepdims=True), jnp.sum(m[4:8], axis=0, keepdims=True)]
        + [jnp.zeros((6, FINE), f32)],
        0,
    )
    weight[...] = jnp.dot(rows.astype(bf16), pooling_matrix(), preferred_element_type=f32)


def fine_columns_kernel(t, s, v, mask, near, far, blocks, semaphore):
    for copy in fetch(block_copies((t, s, v), blocks), semaphore):
        copy.wait()
    fill_columns(blocks, (0, 1, 2), mask, near, far)


def parts_of(value):
    high = value.astype(bf16)
    return high, (value - high.astype(f32)).astype(bf16)


def dot_parts(a, b, contract):
    (a_high, a_low), (b_high, b_low) = a, b
    dims = (((1,), (contract,)), ((), ()))
    dot = functools.partial(lax.dot_general, dimension_numbers=dims, preferred_element_type=f32)
    rows = a_high.shape[0]
    both = dot(jnp.concatenate([a_high, a_low], 0), b_high)
    return both[:rows] + (both[rows:] + dot(a_high, b_low))


def column_matrix(low, high):
    rows = []
    for at in (8, 9):
        for side in range(3):
            rows += [ref[at + 2 * side : at + 2 * side + 1, :] for ref in (low, high)]
    rows.append(jnp.zeros((4, COARSE), f32))
    return jnp.concatenate(rows, 0).T


def shifted_rows(value, before, after):
    lanes = lane_index((CHANNELS, COARSE))
    return (
        jnp.where(lanes == 0, before, pltpu.roll(value, 1, 1)),
        value,
        jnp.where(lanes == COARSE - 1, after, pltpu.roll(value, COARSE - 1, 1)),
    )


def coarse_rows(x, west, east):
    return (
        (west[0:CHANNELS, :], 0, 2),
        (west[CHANNELS : 2 * CHANNELS, :], CHANNELS, 2),
        (x[0:CHANNELS, :], 0, 0),
        (x[CHANNELS : 2 * CHANNELS, :], CHANNELS, 0),
        (east[0:CHANNELS, :], 0, 4),
        (east[CHANNELS : 2 * CHANNELS, :], CHANNELS, 4),
    )


def fill_taps(taps, rows, columns, centres):
    for at, (value, start, pair) in enumerate(rows):
        if not any(abs(at - centre) <= 1 for centre in centres):
            continue
        channels = slice(start, start + CHANNELS)
        shifted = [
            parts_of(part)
            for part in shifted_rows(
                value, columns[channels, pair : pair + 1], columns[channels, pair + 1 : pair + 2]
            )
        ]
        for place, centre in enumerate(centres):
            tap = at - centre + 1
            if 0 <= tap < 3:
                for side in range(3):
                    begin = (3 * tap + side) * CHANNELS
                    for out, part in zip(taps, shifted[side]):
                        out[begin : begin + CHANNELS, COARSE * place : COARSE * (place + 1)] = part


def fill_side_taps(taps, rows, columns, start_lane):
    lanes = lane_index((CHANNELS, COARSE))
    for tap in range(3):
        for side in range(3):
            out = jnp.zeros((CHANNELS, COARSE), f32)
            for row in range(2):
                value, start, pair = rows[row + tap + 1]
                channels = slice(start, start + CHANNELS)
                low = (
                    columns[channels, 6 + pair : 7 + pair],
                    columns[channels, pair : pair + 1],
                    value[:, 0:1],
                )[side]
                high = (
                    value[:, COARSE - 1 : COARSE],
                    columns[channels, pair + 1 : pair + 2],
                    columns[channels, 7 + pair : 8 + pair],
                )[side]
                out = jnp.where(lanes == row, low, out)
                out = jnp.where(lanes == 2 + row, high, out)
            begin = (3 * tap + side) * CHANNELS
            for ref, part in zip(taps, parts_of(out)):
                ref[begin : begin + CHANNELS, start_lane : start_lane + COARSE] = part


def network_step(
    x, inner, outer, low, high, target, weight, packed, pred, own, other, taps_high, taps_low, grads
):
    west, east = sides(inner, outer)
    columns = column_matrix(low, high)
    fill_taps((taps_high, taps_low), coarse_rows(x, west, east), columns, (2, 3))
    taps = taps_high[...], taps_low[...]
    kernel = parts_of(packed[:, 0:TAPS])
    mix = packed[:, MIX_AT : MIX_AT + HIDDEN]
    out_turned = packed[:, OUT_AT : OUT_AT + CHANNELS]
    hidden_one = jnp.tanh(dot_parts(kernel, taps, 0))
    one = parts_of(hidden_one)
    hidden_two = jnp.tanh(dot_parts(parts_of(mix), one, 0))
    two = parts_of(hidden_two)
    predicted = dot_parts(parts_of(out_turned.T), two, 0)
    pred[0:CHANNELS, :] = predicted[:, 0:COARSE]
    pred[CHANNELS : 2 * CHANNELS, :] = predicted[:, COARSE : 2 * COARSE]
    back_out = parts_of(
        jnp.concatenate(
            [
                weight[row : row + 1, :]
                * (
                    predicted[:, COARSE * row : COARSE * (row + 1)]
                    - target[CHANNELS * row : CHANNELS * (row + 1), :]
                )
                for row in range(2)
            ],
            1,
        )
    )
    back_two = parts_of(
        dot_parts(parts_of(out_turned), back_out, 0) * (1.0 - hidden_two * hidden_two)
    )
    back_one = parts_of(
        dot_parts(parts_of(mix.T), back_two, 0) * (1.0 - hidden_one * hidden_one)
    )
    grads[:, 0:TAPS] = dot_parts(back_one, taps, 1)
    grads[:, MIX_AT : MIX_AT + HIDDEN] = dot_parts(back_two, one, 1)
    grads[:, OUT_AT : OUT_AT + CHANNELS] = dot_parts(two, back_out, 1)
    here = lax.axis_index("grp")
    for core, out in ((here, own), (1 - here, other)):
        start = core * HALF
        rows = pl.ds(pl.multiple_of(start, HALF), HALF)
        for block in range(4):
            out[HALF * block : HALF * (block + 1), :] = grads[rows, 128 * block : 128 * (block + 1)]
        for part in range(4):
            rows = pl.ds(pl.multiple_of(start + 8 * part, 8), 8)
            out[4 * HALF : SUMMED, 32 * part : 32 * (part + 1)] = grads[rows, REST_AT:USED]
        if out.shape[0] > SUMMED:
            area = jnp.sum(weight[0:2, :], axis=(0, 1), keepdims=True)
            out[SUMMED:, :] = jnp.broadcast_to(area, (8, 128))


def descended(packed, part, back, with_area):
    first = lax.axis_index("grp") == 0

    def whole(mine, theirs):
        return jnp.concatenate([jnp.where(first, mine, theirs), jnp.where(first, theirs, mine)], 0)

    blocks = []
    for block in range(4):
        rows = slice(HALF * block, HALF * (block + 1))
        blocks.append(whole(part[rows, :], back[rows, :]))
    rest = [
        jnp.concatenate([ref[4 * HALF : SUMMED, 32 * at : 32 * (at + 1)] for at in range(4)], 0)
        for ref in (part, back)
    ]
    blocks += [whole(*rest), jnp.zeros((HIDDEN, PACKED - USED), f32)]
    step = (learn_rate * 2.0 / CHANNELS) / with_area[SUMMED : SUMMED + 1, 0:1]
    return packed[...] - step * jnp.concatenate(blocks, 1)


def next_network_kernel(*refs):
    *ins, packed, part, back, renewed = refs[:11]
    renewed[...] = descended(packed, part, back, part)
    network_step(*ins, renewed, *refs[11:])


def last_kernel(packed, part, back, with_area, kernel, mix, out):
    renewed = descended(packed, part, back, with_area)
    kernel[...] = renewed[:, 0:TAPS].T
    mix[...] = renewed[:, MIX_AT : MIX_AT + HIDDEN]
    out[...] = renewed[:, OUT_AT : OUT_AT + CHANNELS].T


def forcing(x, pred, packed, halo, taps):
    west, east, low, high = halo
    rows = coarse_rows(x, west, east)
    columns = column_matrix(low, high)
    fill_taps(taps, rows, columns, (1, 4))
    fill_side_taps(taps, rows, columns, 2 * COARSE)
    inputs = tuple(ref[...] for ref in taps)
    hidden = jnp.tanh(dot_parts(parts_of(packed[:, 0:TAPS]), inputs, 0))
    hidden = jnp.tanh(
        dot_parts(parts_of(packed[:, MIX_AT : MIX_AT + HIDDEN]), parts_of(hidden), 0)
    )
    beside = dot_parts(
        parts_of(packed[:, OUT_AT : OUT_AT + CHANNELS].T), parts_of(hidden), 0
    )
    sides = beside[:, 2 * COARSE :]
    lat = lax.axis_index("lat")
    sides_low = jnp.where(lat == 0, 0.0, sides)
    sides_high = jnp.where(lat == lax.axis_size("lat") - 1, 0.0, sides)
    before = (beside[:, 0:COARSE], pred[0:CHANNELS, :])
    after = (pred[CHANNELS : 2 * CHANNELS, :], beside[:, COARSE : 2 * COARSE])
    pieces = []
    for row in range(2):
        value = pred[CHANNELS * row : CHANNELS * (row + 1), :]
        along = after[row] - before[row]
        south, _, north = shifted_rows(value, sides_low[:, row : row + 1], sides_high[:, 2 + row : 3 + row])
        across = north - south
        for at in (0, 2 * LEVELS):
            pieces.append(-0.5 * (along[at : at + LEVELS] + across[at + LEVELS : at + 2 * LEVELS]))
            pieces.append(jnp.zeros((4, COARSE), f32))
    return exact_dot(jnp.concatenate(pieces, 0), spreading_matrix())


def advance(t, s, u, v, mask, force, fixed, moving, t_out, s_out):
    fixed_west, fixed_east, fixed_low, fixed_high = fixed
    west, east, low, high = moving
    m = mask[...]
    shape = (8, FINE)
    lanes = lane_index(shape)
    subs = lax.broadcasted_iota(jnp.int32, shape, 0)

    def edge_row(ref, at):
        first, depth = edge_layout(ref)
        starts = [first + depth * block + at for block in range(4)]
        return jnp.concatenate([ref[start : start + 1, :] for start in starts], 1)

    def neighbours_lon(value, row_west, row_east):
        return (
            jnp.where(subs == 0, row_west, pltpu.roll(value, 1, 0)),
            jnp.where(subs == 7, row_east, pltpu.roll(value, 7, 0)),
        )

    def neighbours_lat(value, column_low, column_high):
        return (
            jnp.where(lanes == 0, column_low, pltpu.roll(value, 1, 1)),
            jnp.where(lanes == FINE - 1, column_high, pltpu.roll(value, FINE - 1, 1)),
        )

    fixed_low_turned = fixed_low[...].T
    fixed_high_turned = fixed_high[...].T
    low_turned = low[...].T
    high_turned = high[...].T
    m_west, m_east = neighbours_lon(
        m, edge_row(fixed_west, 3 * LEVELS), edge_row(fixed_east, 3 * LEVELS)
    )
    m_low, m_high = neighbours_lat(m, fixed_low_turned[0:8, 3:4], fixed_high_turned[0:8, 3:4])
    open_west, open_east, open_low, open_high = m * m_west, m * m_east, m * m_low, m * m_high
    mix_west, mix_east = diffusivity * open_west, diffusivity * open_east
    mix_low, mix_high = diffusivity * open_low, diffusivity * open_high
    pace = time_step * m
    for level in range(LEVELS):
        at = slice(8 * level, 8 * (level + 1))
        u_here, v_here = u[at, :], v[at, :]
        u_west, u_east = neighbours_lon(
            u_here, edge_row(fixed_west, 2 * LEVELS + level), edge_row(fixed_east, 2 * LEVELS + level)
        )
        v_low, v_high = neighbours_lat(v_here, fixed_low_turned[at, 2:3], fixed_high_turned[at, 2:3])
        speed_west = 0.25 * (u_here + u_west) * open_west
        speed_east = 0.25 * (u_here + u_east) * open_east
        speed_low = 0.25 * (v_here + v_low) * open_low
        speed_high = 0.25 * (v_here + v_high) * open_high
        for which, (q_ref, out) in enumerate(((t, t_out), (s, s_out))):
            q = q_ref[at, :]
            q_west, q_east = neighbours_lon(
                q, edge_row(west, LEVELS * which + level), edge_row(east, LEVELS * which + level)
            )
            q_low, q_high = neighbours_lat(
                q, low_turned[at, which : which + 1], high_turned[at, which : which + 1]
            )
            flux_east = speed_east * (q + q_east) - mix_east * (q_east - q)
            flux_west = speed_west * (q_west + q) - mix_west * (q - q_west)
            flux_high = speed_high * (q + q_high) - mix_high * (q_high - q)
            flux_low = speed_low * (q_low + q) - mix_low * (q - q_low)
            row = 16 * which + level
            push = jnp.where(subs < 4, force[row : row + 1], force[32 + row : 33 + row])
            out[at, :] = q + pace * (push - (flux_east - flux_west) - (flux_high - flux_low))


def around(inner, outer, low, high):
    return (*sides(inner, outer), low, high)


def first_advance_kernel(*refs):
    t, s, u, v, mask, x, pred, packed = refs[:8]
    halo = around(*refs[8:12])
    t_out, s_out, x_out, target, inner, outer, near, far = refs[12:20]
    sums, blocks, *taps = refs[20:24]
    t_here, s_here, u_here, v_here, semaphore = refs[24:]
    here = (t_here, s_here, u_here, v_here)
    copies = fetch(list(zip((t, s, u, v), here)), semaphore)
    force = forcing(x, pred, packed, halo, taps)
    for copy in copies:
        copy.wait()
    advance(*here, mask, force, halo, halo, t_out, s_out)
    fill_blocks(blocks, (t_out, s_out, u_here, v_here))
    coarsen(blocks, sums, x_out, target)
    fill_edges(blocks, 2, None, x_out, inner, outer)
    fill_columns(blocks, (0, 1), None, near, far)


def next_advance_kernel(*refs):
    t, s, u, v, mask, x, pred, packed = refs[:8]
    fixed, moving = around(*refs[8:12]), around(*refs[12:16])
    t_out, s_out, *taps = refs[16:]
    force = forcing(x, pred, packed, moving, taps)
    advance(t, s, u, v, mask, force, fixed, moving, t_out, s_out)


def swap_lon(inner, outer):
    axis = ("lon", "grp")
    count = lax.axis_size("lon") * lax.axis_size("grp")
    chips = [(i, (i + (1 if i % 2 else -1)) % count) for i in range(count)]
    outer = lax.ppermute(outer, axis, chips)
    return lax.ppermute(inner, "grp", flipped("grp", 1)), outer


def swap_lat(near, far):
    last = lax.axis_size("lat") - 1
    beyond = [(i, i ^ 3) for i in range(1, last)]
    return lax.ppermute(near, "lat", flipped("lat", 1)), lax.ppermute(far, "lat", beyond)


def south_north(near, far):
    lat = lax.axis_index("lat")
    odd = lat % 2 == 1
    south, north = jnp.where(odd, near, far), jnp.where(odd, far, near)
    south = jnp.where(lat == 0, 0.0, south)
    return south, jnp.where(lat == lax.axis_size("lat") - 1, 0.0, north)


def flipped(axis, mask):
    return [(i, i ^ mask) for i in range(lax.axis_size(axis))]


def from_chip(value, mask):
    count = lax.axis_size("lon") * lax.axis_size("lat")
    return lax.ppermute(value, ("lon", "lat"), [(i, i ^ mask) for i in range(count)])


def sum_of_four(part, bit):
    if lax.axis_size("lon") * lax.axis_size("lat") <= 2 * bit:
        return part
    one, two, three = (from_chip(part, bit * step) for step in (1, 2, 3))
    return (part + one) + (two + three)


def sum_over_devices(own, other, after_pair, riders):
    rows = own.shape[0]
    part = own + lax.ppermute(other, "grp", flipped("grp", 1))
    part = after_pair(part + from_chip(part, 4))
    for bit in (8, 32):
        part = sum_of_four(part, bit)
    near, far = riders()
    near = from_chip(jnp.concatenate([part, *near], 0), 1)
    cross = from_chip(part, 6)
    far = from_chip(jnp.concatenate([part, *far], 0), 3)
    part = (part + near[:rows]) + (cross + far[:rows])
    back = lax.ppermute(part, "grp", flipped("grp", 1))
    return part, back, (near[rows:], far[rows:])


def shards(
    thermal_anomaly,
    saltiness_anomaly,
    zonal_flow_speed,
    meridional_flow_speed,
    water_indicator,
    kernel_factors,
    hidden_pointwise_factors,
    final_pointwise_factors,
):
    fields = tuple(
        value.reshape(8 * LEVELS, FINE)
        for value in (thermal_anomaly, saltiness_anomaly, zonal_flow_speed, meridional_flow_speed)
    )
    packed = jnp.concatenate(
        [
            kernel_factors.reshape(HIDDEN, TAPS),
            hidden_pointwise_factors,
            final_pointwise_factors.T,
            jnp.zeros((HIDDEN, PACKED - USED), f32),
        ],
        1,
    )
    blocks = pltpu.VMEM((16 * 8 * LEVELS, 128), f32)
    field_scratch = pltpu.VMEM((8 * LEVELS, FINE), f32)
    sums = [pltpu.VMEM((4 * CHANNELS, FINE), f32), pltpu.VMEM((16 * 8 * LEVELS, 128), f32)]
    wide = struct(2 * CHANNELS, COARSE)
    tile = struct(8, 128)
    with_area, without = struct(SUMMED + 8, 128), struct(SUMMED, 128)
    field = struct(8 * LEVELS, FINE)
    network_scratch = [pltpu.VMEM((TAPS, 2 * COARSE), bf16)] * 2 + [pltpu.VMEM((HIDDEN, PACKED), f32)]
    side_taps = [pltpu.VMEM((TAPS, 3 * COARSE), bf16)] * 2

    edge = struct(2 * CHANNELS + 160, 128)
    x, target, weight, mask, inner, outer = call(
        prepare_kernel,
        [wide, wide, tile, struct(8, FINE), edge, edge],
        *fields, water_indicator,
        scratch=sums + [pltpu.VMEM((8, FINE), jnp.int32), pltpu.SemaphoreType.DMA((17,))],
        remote=5,
    )
    near, far = call(
        fine_columns_kernel,
        [tile, tile],
        *fields[:2], fields[3], mask,
        scratch=[sums[1], pltpu.SemaphoreType.DMA((12,))],
        remote=3,
    )

    def columns(x, inner, outer, near, far):
        return call(columns_kernel, [struct(16, 128)] * 2, x, inner, outer, near, far)

    (inner, outer), packed = lax.optimization_barrier((swap_lon(inner, outer), packed))
    south, north = south_north(*swap_lat(*columns(x, inner, outer, near, far)))
    pred, own, other = call(
        network_step,
        [wide, with_area, with_area],
        x, inner, outer, south, north, target, weight, packed,
        scratch=network_scratch,
    )
    edge = struct(2 * CHANNELS + 96, 128)
    later = {}

    fixed = inner, outer, south, north

    def first_advance(part):
        t, s, x_next, target, inner, outer, near, far = call(
            first_advance_kernel,
            [field, field, wide, wide, edge, edge, tile, tile],
            *fields, mask, x, pred, packed, *fixed,
            scratch=sums + side_taps + [field_scratch] * 4 + [pltpu.SemaphoreType.DMA((4,))],
            remote=4,
        )
        part, inner, outer = lax.optimization_barrier((part, inner, outer))
        later["state"] = t, s, x_next, target
        later["beside"] = swap_lon(inner, outer)
        later["columns"] = near, far
        return part

    def first_riders():
        x_next = later["state"][2]
        near, far = columns(x_next, *later["beside"], *later["columns"])
        return [near], [far]

    part, back, received = sum_over_devices(own, other, first_advance, first_riders)
    moving = *later["beside"], *south_north(*received)
    t, s, x, target = later["state"]
    packed, pred, own, other = call(
        next_network_kernel,
        [struct(HIDDEN, PACKED), wide, without, without],
        x, *moving, target, weight, packed, part, back,
        scratch=network_scratch,
    )

    def next_advance(part):
        fields_next = call(
            next_advance_kernel,
            [field, field],
            t, s, *fields[2:], mask, x, pred, packed, *fixed, *moving,
            scratch=side_taps,
        )
        part, *later["fields"] = lax.optimization_barrier((part, *fields_next))
        return part

    first_part = part
    part = own + lax.ppermute(other, "grp", flipped("grp", 1))
    part = next_advance(part + from_chip(part, 3))
    for bit in (8, 32):
        part = sum_of_four(part, bit)
    one, two, three = (from_chip(part, mask) for mask in (4, 1, 5))
    part = (part + one) + (two + three)
    back = lax.ppermute(part, "grp", flipped("grp", 1))
    t, s = later["fields"]
    kernel, mix, out = call(
        last_kernel,
        [struct(TAPS, HIDDEN), struct(HIDDEN, HIDDEN), struct(CHANNELS, HIDDEN)],
        packed, part, back, first_part,
    )
    return (
        t.reshape(thermal_anomaly.shape),
        s.reshape(thermal_anomaly.shape),
        kernel.T.reshape(kernel_factors.shape),
        mix,
        out,
    )


def solution(mesh):
    field = P(None, ("lon", "grp"), "lat")
    return jax.shard_map(
        shards,
        mesh=mesh,
        in_specs=(field, field, field, field, P(("lon", "grp"), "lat"), P(), P(), P()),
        out_specs=(field, field, P(), P(), P()),
        check_vma=False,
    )
```

```python
import functools

import jax
import jax.numpy as jnp
from jax import lax
from jax.experimental import pallas as pl
from jax.experimental.pallas import tpu as pltpu
from jax.sharding import PartitionSpec as P

time_step = 0.2
diffusivity = 0.5
learn_rate = 200.0
f32 = jnp.float32
bf16 = jnp.bfloat16

LEVELS = 12
CHANNELS = 4 * LEVELS
HIDDEN = 64
TAPS = 9 * CHANNELS
MIX_AT = 432
OUT_AT = 496
REST_AT = 512
USED = 544
PACKED = 640
HALF = HIDDEN // 2
SUMMED = 4 * HALF + 8
FINE = 512
COARSE = 128
VMEM_LIMIT = 48 * 1024 * 1024


def struct(*shape):
    return jax.ShapeDtypeStruct(shape, f32)


def call(kernel, outs, *args, scratch=(), remote=0, flops=0, bytes_accessed=0):
    args = [
        pltpu.with_memory_space_constraint(arg, pltpu.HBM) if at < remote else arg
        for at, arg in enumerate(args)
    ]
    specs = []
    specs += [pl.BlockSpec(memory_space=pltpu.HBM)] * remote
    specs += [pl.BlockSpec(memory_space=pltpu.VMEM)] * (len(args) - remote)
    return pl.pallas_call(
        kernel,
        out_shape=outs,
        in_specs=specs,
        out_specs=[pl.BlockSpec(memory_space=pltpu.VMEM)] * len(outs),
        scratch_shapes=scratch,
        compiler_params=pltpu.CompilerParams(vmem_limit_bytes=VMEM_LIMIT),
        cost_estimate=pl.CostEstimate(
            flops=flops, bytes_accessed=bytes_accessed, transcendentals=0
        ),
    )(*args)


def exact_dot(value, selector):
    high = value.astype(bf16)
    rest = value - high.astype(f32)
    middle = rest.astype(bf16)
    low = (rest - middle.astype(f32)).astype(bf16)
    dot = functools.partial(jnp.dot, preferred_element_type=f32)
    return (dot(low, selector) + dot(middle, selector)) + dot(high, selector)


def pooling_matrix():
    fine = lax.broadcasted_iota(jnp.int32, (FINE, COARSE), 0) >> 2
    coarse = lax.broadcasted_iota(jnp.int32, (FINE, COARSE), 1)
    return jnp.where(fine == coarse, f32(1.0 / 16.0), f32(0.0)).astype(bf16)


def spreading_matrix():
    fine = lax.broadcasted_iota(jnp.int32, (COARSE, FINE), 1) >> 2
    coarse = lax.broadcasted_iota(jnp.int32, (COARSE, FINE), 0)
    return jnp.where(fine == coarse, f32(1.0), f32(0.0)).astype(bf16)


def lane_index(shape):
    return lax.broadcasted_iota(jnp.int32, shape, len(shape) - 1)


def block_rows(which, block):
    start = (4 * which + block) * 8 * LEVELS
    return slice(start, start + 8 * LEVELS)


def fill_blocks(blocks, refs):
    for which, ref in enumerate(refs):
        for block in range(4):
            blocks[block_rows(which, block), :] = ref[:, 128 * block : 128 * (block + 1)]


def fetch(pairs, semaphore):
    copies = [
        pltpu.make_async_copy(source, target, semaphore.at[at])
        for at, (source, target) in enumerate(pairs)
    ]
    for copy in copies:
        copy.start()
    return copies


def longitude_row(blocks, which, block, lon):
    return blocks[pl.ds(block_rows(which, block).start + lon, LEVELS, stride=8), :]


def coarsen(blocks, sums_ref, x_ref, target_ref):
    for row in range(2):
        for block in range(4):
            total = None
            for lon in range(4 * row, 4 * row + 4):
                t, s, u, v = (longitude_row(blocks, which, block, lon) for which in range(4))
                terms = (t, s, u, v, u * t, v * t, u * s, v * s)
                total = terms if total is None else [a + b for a, b in zip(total, terms)]
            for at, value in enumerate(total):
                start = 2 * CHANNELS * row + LEVELS * at
                sums_ref[start : start + LEVELS, 128 * block : 128 * (block + 1)] = value
    means = exact_dot(sums_ref[...], pooling_matrix())
    for row in range(2):
        x = means[2 * CHANNELS * row : 2 * CHANNELS * row + CHANNELS]
        products = means[2 * CHANNELS * row + CHANNELS : 2 * CHANNELS * (row + 1)]
        ct, cs, cu, cv = (x[LEVELS * k : LEVELS * (k + 1)] for k in range(4))
        x_ref[CHANNELS * row : CHANNELS * (row + 1), :] = x
        own = jnp.concatenate([cu * ct, cv * ct, cu * cs, cv * cs], 0)
        target_ref[CHANNELS * row : CHANNELS * (row + 1), :] = products - own


class Either:
    def __init__(self, flag, one, other):
        self.flag, self.one, self.other, self.shape = flag, one, other, one.shape

    def __getitem__(self, at):
        return jnp.where(self.flag, self.one[at], self.other[at])


def sides(inner, outer):
    first = lax.axis_index("grp") == 0
    return Either(first, outer, inner), Either(first, inner, outer)


def edge_layout(ref):
    first = 2 * CHANNELS
    return first, (ref.shape[0] - first) // 4


def fill_edges(blocks, fields, mask_ref, x_ref, inner_ref, outer_ref):
    core_first = lax.axis_index("grp") == 0
    first_row, depth = edge_layout(inner_ref)
    for out in (inner_ref, outer_ref):
        out[0:first_row, :] = x_ref[...]
        out[first_row:, :] = jnp.zeros((out.shape[0] - first_row, COARSE), f32)

    def put(rows, first, last):
        inner_ref[rows, :] = jnp.where(core_first, last, first)
        outer_ref[rows, :] = jnp.where(core_first, first, last)

    for block in range(4):
        start = first_row + block * depth
        for which in range(fields):
            at = start + which * LEVELS
            put(
                slice(at, at + LEVELS),
                longitude_row(blocks, which, block, 0),
                longitude_row(blocks, which, block, 7),
            )
        if mask_ref is not None:
            at = start + fields * LEVELS
            lanes = slice(128 * block, 128 * (block + 1))
            put(slice(at, at + 1), mask_ref[0:1, lanes], mask_ref[7:8, lanes])


def put_columns(near_ref, far_ref, at, low, high):
    odd = lax.axis_index("lat") % 2 == 1
    near_ref[at : at + 1, 0 : low.shape[1]] = jnp.where(odd, low, high)
    far_ref[at : at + 1, 0 : low.shape[1]] = jnp.where(odd, high, low)


def fill_columns(blocks, column_fields, mask_ref, near_ref, far_ref):
    near_ref[...] = jnp.zeros(near_ref.shape, f32)
    far_ref[...] = jnp.zeros(far_ref.shape, f32)
    for at, which in enumerate(column_fields):
        low, high = (blocks[block_rows(which, block), :].T for block in (0, 3))
        put_columns(near_ref, far_ref, at, low[0:1], high[127:128])
    if mask_ref is not None:
        low, high = mask_ref[:, 0:128].T[0:1], mask_ref[:, FINE - 128 : FINE].T[127:128]
        put_columns(near_ref, far_ref, 3, low, high)


def columns_kernel(x, x_inner, x_outer, near_fine, far_fine, near, far):
    for fine, out in ((near_fine, near), (far_fine, far)):
        out[0:8, :] = fine[...]
        out[8:16, :] = jnp.zeros((8, COARSE), f32)
    rows = slice(0, 2 * CHANNELS)
    for at, ref in enumerate((x, *sides(x_inner, x_outer))):
        turned = ref[rows, :].T
        put_columns(near, far, 8 + 2 * at, turned[0:1], turned[127:128])
        put_columns(near, far, 9 + 2 * at, turned[1:2], turned[126:127])


def block_copies(refs, blocks):
    return [
        (ref.at[:, pl.ds(128 * block, 128)], blocks.at[block_rows(which, block), :])
        for which, ref in enumerate(refs)
        for block in range(4)
    ]


def prepare_kernel(
    t, s, u, v, mask, x, target, weight, mask_values, inner, outer, sums, blocks, mask_here, semaphore
):
    copies = fetch([(mask, mask_here)] + block_copies((t, s, u, v), blocks), semaphore)
    for copy in copies:
        copy.wait()
    m = mask_here[...].astype(f32)
    mask_values[...] = m
    coarsen(blocks, sums, x, target)
    fill_edges(blocks, 3, mask_values, x, inner, outer)
    rows = jnp.concatenate(
        [jnp.sum(m[0:4], axis=0, keepdims=True), jnp.sum(m[4:8], axis=0, keepdims=True)]
        + [jnp.zeros((6, FINE), f32)],
        0,
    )
    weight[...] = jnp.dot(rows.astype(bf16), pooling_matrix(), preferred_element_type=f32)


def fine_columns_kernel(t, s, v, mask, near, far, blocks, semaphore):
    for copy in fetch(block_copies((t, s, v), blocks), semaphore):
        copy.wait()
    fill_columns(blocks, (0, 1, 2), mask, near, far)


def parts_of(value):
    high = value.astype(bf16)
    return high, (value - high.astype(f32)).astype(bf16)


def dot_parts(a, b, contract):
    (a_high, a_low), (b_high, b_low) = a, b
    dims = (((1,), (contract,)), ((), ()))
    dot = functools.partial(lax.dot_general, dimension_numbers=dims, preferred_element_type=f32)
    rows = a_high.shape[0]
    both = dot(jnp.concatenate([a_high, a_low], 0), b_high)
    return both[:rows] + (both[rows:] + dot(a_high, b_low))


def column_matrix(low, high):
    rows = []
    for at in (8, 9):
        for side in range(3):
            rows += [ref[at + 2 * side : at + 2 * side + 1, :] for ref in (low, high)]
    rows.append(jnp.zeros((4, COARSE), f32))
    return jnp.concatenate(rows, 0).T


def shifted_rows(value, before, after):
    lanes = lane_index((CHANNELS, COARSE))
    return (
        jnp.where(lanes == 0, before, pltpu.roll(value, 1, 1)),
        value,
        jnp.where(lanes == COARSE - 1, after, pltpu.roll(value, COARSE - 1, 1)),
    )


def coarse_rows(x, west, east):
    return (
        (west[0:CHANNELS, :], 0, 2),
        (west[CHANNELS : 2 * CHANNELS, :], CHANNELS, 2),
        (x[0:CHANNELS, :], 0, 0),
        (x[CHANNELS : 2 * CHANNELS, :], CHANNELS, 0),
        (east[0:CHANNELS, :], 0, 4),
        (east[CHANNELS : 2 * CHANNELS, :], CHANNELS, 4),
    )


def fill_taps(taps, rows, columns, centres):
    for at, (value, start, pair) in enumerate(rows):
        if not any(abs(at - centre) <= 1 for centre in centres):
            continue
        channels = slice(start, start + CHANNELS)
        shifted = [
            parts_of(part)
            for part in shifted_rows(
                value, columns[channels, pair : pair + 1], columns[channels, pair + 1 : pair + 2]
            )
        ]
        for place, centre in enumerate(centres):
            tap = at - centre + 1
            if 0 <= tap < 3:
                for side in range(3):
                    begin = (3 * tap + side) * CHANNELS
                    for out, part in zip(taps, shifted[side]):
                        out[begin : begin + CHANNELS, COARSE * place : COARSE * (place + 1)] = part


def fill_side_taps(taps, rows, columns, start_lane):
    lanes = lane_index((CHANNELS, COARSE))
    for tap in range(3):
        for side in range(3):
            out = jnp.zeros((CHANNELS, COARSE), f32)
            for row in range(2):
                value, start, pair = rows[row + tap + 1]
                channels = slice(start, start + CHANNELS)
                low = (
                    columns[channels, 6 + pair : 7 + pair],
                    columns[channels, pair : pair + 1],
                    value[:, 0:1],
                )[side]
                high = (
                    value[:, COARSE - 1 : COARSE],
                    columns[channels, pair + 1 : pair + 2],
                    columns[channels, 7 + pair : 8 + pair],
                )[side]
                out = jnp.where(lanes == row, low, out)
                out = jnp.where(lanes == 2 + row, high, out)
            begin = (3 * tap + side) * CHANNELS
            for ref, part in zip(taps, parts_of(out)):
                ref[begin : begin + CHANNELS, start_lane : start_lane + COARSE] = part


def network_step(
    x, inner, outer, low, high, target, weight, packed, pred, own, other, taps_high, taps_low, grads
):
    west, east = sides(inner, outer)
    columns = column_matrix(low, high)
    fill_taps((taps_high, taps_low), coarse_rows(x, west, east), columns, (2, 3))
    taps = taps_high[...], taps_low[...]
    kernel = parts_of(packed[:, 0:TAPS])
    mix = packed[:, MIX_AT : MIX_AT + HIDDEN]
    out_turned = packed[:, OUT_AT : OUT_AT + CHANNELS]
    hidden_one = jnp.tanh(dot_parts(kernel, taps, 0))
    one = parts_of(hidden_one)
    hidden_two = jnp.tanh(dot_parts(parts_of(mix), one, 0))
    two = parts_of(hidden_two)
    predicted = dot_parts(parts_of(out_turned.T), two, 0)
    pred[0:CHANNELS, :] = predicted[:, 0:COARSE]
    pred[CHANNELS : 2 * CHANNELS, :] = predicted[:, COARSE : 2 * COARSE]
    back_out = parts_of(
        jnp.concatenate(
            [
                weight[row : row + 1, :]
                * (
                    predicted[:, COARSE * row : COARSE * (row + 1)]
                    - target[CHANNELS * row : CHANNELS * (row + 1), :]
                )
                for row in range(2)
            ],
            1,
        )
    )
    back_two = parts_of(
        dot_parts(parts_of(out_turned), back_out, 0) * (1.0 - hidden_two * hidden_two)
    )
    back_one = parts_of(
        dot_parts(parts_of(mix.T), back_two, 0) * (1.0 - hidden_one * hidden_one)
    )
    grads[:, 0:TAPS] = dot_parts(back_one, taps, 1)
    grads[:, MIX_AT : MIX_AT + HIDDEN] = dot_parts(back_two, one, 1)
    grads[:, OUT_AT : OUT_AT + CHANNELS] = dot_parts(two, back_out, 1)
    here = lax.axis_index("grp")
    for core, out in ((here, own), (1 - here, other)):
        start = core * HALF
        rows = pl.ds(pl.multiple_of(start, HALF), HALF)
        for block in range(4):
            out[HALF * block : HALF * (block + 1), :] = grads[rows, 128 * block : 128 * (block + 1)]
        for part in range(4):
            rows = pl.ds(pl.multiple_of(start + 8 * part, 8), 8)
            out[4 * HALF : SUMMED, 32 * part : 32 * (part + 1)] = grads[rows, REST_AT:USED]
        if out.shape[0] > SUMMED:
            area = jnp.sum(weight[0:2, :], axis=(0, 1), keepdims=True)
            out[SUMMED:, :] = jnp.broadcast_to(area, (8, 128))


def descended(packed, part, back, with_area):
    first = lax.axis_index("grp") == 0

    def whole(mine, theirs):
        return jnp.concatenate([jnp.where(first, mine, theirs), jnp.where(first, theirs, mine)], 0)

    blocks = []
    for block in range(4):
        rows = slice(HALF * block, HALF * (block + 1))
        blocks.append(whole(part[rows, :], back[rows, :]))
    rest = [
        jnp.concatenate([ref[4 * HALF : SUMMED, 32 * at : 32 * (at + 1)] for at in range(4)], 0)
        for ref in (part, back)
    ]
    blocks += [whole(*rest), jnp.zeros((HIDDEN, PACKED - USED), f32)]
    step = (learn_rate * 2.0 / CHANNELS) / with_area[SUMMED : SUMMED + 1, 0:1]
    return packed[...] - step * jnp.concatenate(blocks, 1)


def next_network_kernel(*refs):
    *ins, packed, part, back, renewed = refs[:11]
    renewed[...] = descended(packed, part, back, part)
    network_step(*ins, renewed, *refs[11:])


def last_kernel(packed, part, back, with_area, kernel, mix, out):
    renewed = descended(packed, part, back, with_area)
    kernel[...] = renewed[:, 0:TAPS].T
    mix[...] = renewed[:, MIX_AT : MIX_AT + HIDDEN]
    out[...] = renewed[:, OUT_AT : OUT_AT + CHANNELS].T


def forcing(x, pred, packed, halo, taps):
    west, east, low, high = halo
    rows = coarse_rows(x, west, east)
    columns = column_matrix(low, high)
    fill_taps(taps, rows, columns, (1, 4))
    fill_side_taps(taps, rows, columns, 2 * COARSE)
    inputs = tuple(ref[...] for ref in taps)
    hidden = jnp.tanh(dot_parts(parts_of(packed[:, 0:TAPS]), inputs, 0))
    hidden = jnp.tanh(
        dot_parts(parts_of(packed[:, MIX_AT : MIX_AT + HIDDEN]), parts_of(hidden), 0)
    )
    beside = dot_parts(
        parts_of(packed[:, OUT_AT : OUT_AT + CHANNELS].T), parts_of(hidden), 0
    )
    sides = beside[:, 2 * COARSE :]
    lat = lax.axis_index("lat")
    sides_low = jnp.where(lat == 0, 0.0, sides)
    sides_high = jnp.where(lat == lax.axis_size("lat") - 1, 0.0, sides)
    before = (beside[:, 0:COARSE], pred[0:CHANNELS, :])
    after = (pred[CHANNELS : 2 * CHANNELS, :], beside[:, COARSE : 2 * COARSE])
    pieces = []
    for row in range(2):
        value = pred[CHANNELS * row : CHANNELS * (row + 1), :]
        along = after[row] - before[row]
        south, _, north = shifted_rows(value, sides_low[:, row : row + 1], sides_high[:, 2 + row : 3 + row])
        across = north - south
        for at in (0, 2 * LEVELS):
            pieces.append(-0.5 * (along[at : at + LEVELS] + across[at + LEVELS : at + 2 * LEVELS]))
            pieces.append(jnp.zeros((4, COARSE), f32))
    return exact_dot(jnp.concatenate(pieces, 0), spreading_matrix())


def advance(t, s, u, v, mask, force, fixed, moving, t_out, s_out):
    fixed_west, fixed_east, fixed_low, fixed_high = fixed
    west, east, low, high = moving
    m = mask[...]
    shape = (8, FINE)
    lanes = lane_index(shape)
    subs = lax.broadcasted_iota(jnp.int32, shape, 0)

    def edge_row(ref, at):
        first, depth = edge_layout(ref)
        starts = [first + depth * block + at for block in range(4)]
        return jnp.concatenate([ref[start : start + 1, :] for start in starts], 1)

    def neighbours_lon(value, row_west, row_east):
        return (
            jnp.where(subs == 0, row_west, pltpu.roll(value, 1, 0)),
            jnp.where(subs == 7, row_east, pltpu.roll(value, 7, 0)),
        )

    def neighbours_lat(value, column_low, column_high):
        return (
            jnp.where(lanes == 0, column_low, pltpu.roll(value, 1, 1)),
            jnp.where(lanes == FINE - 1, column_high, pltpu.roll(value, FINE - 1, 1)),
        )

    fixed_low_turned = fixed_low[...].T
    fixed_high_turned = fixed_high[...].T
    low_turned = low[...].T
    high_turned = high[...].T
    m_west, m_east = neighbours_lon(
        m, edge_row(fixed_west, 3 * LEVELS), edge_row(fixed_east, 3 * LEVELS)
    )
    m_low, m_high = neighbours_lat(m, fixed_low_turned[0:8, 3:4], fixed_high_turned[0:8, 3:4])
    open_west, open_east, open_low, open_high = m * m_west, m * m_east, m * m_low, m * m_high
    mix_west, mix_east = diffusivity * open_west, diffusivity * open_east
    mix_low, mix_high = diffusivity * open_low, diffusivity * open_high
    pace = time_step * m
    for level in range(LEVELS):
        at = slice(8 * level, 8 * (level + 1))
        u_here, v_here = u[at, :], v[at, :]
        u_west, u_east = neighbours_lon(
            u_here, edge_row(fixed_west, 2 * LEVELS + level), edge_row(fixed_east, 2 * LEVELS + level)
        )
        v_low, v_high = neighbours_lat(v_here, fixed_low_turned[at, 2:3], fixed_high_turned[at, 2:3])
        speed_west = 0.25 * (u_here + u_west) * open_west
        speed_east = 0.25 * (u_here + u_east) * open_east
        speed_low = 0.25 * (v_here + v_low) * open_low
        speed_high = 0.25 * (v_here + v_high) * open_high
        for which, (q_ref, out) in enumerate(((t, t_out), (s, s_out))):
            q = q_ref[at, :]
            q_west, q_east = neighbours_lon(
                q, edge_row(west, LEVELS * which + level), edge_row(east, LEVELS * which + level)
            )
            q_low, q_high = neighbours_lat(
                q, low_turned[at, which : which + 1], high_turned[at, which : which + 1]
            )
            flux_east = speed_east * (q + q_east) - mix_east * (q_east - q)
            flux_west = speed_west * (q_west + q) - mix_west * (q - q_west)
            flux_high = speed_high * (q + q_high) - mix_high * (q_high - q)
            flux_low = speed_low * (q_low + q) - mix_low * (q - q_low)
            row = 16 * which + level
            push = jnp.where(subs < 4, force[row : row + 1], force[32 + row : 33 + row])
            out[at, :] = q + pace * (push - (flux_east - flux_west) - (flux_high - flux_low))


def around(inner, outer, low, high):
    return (*sides(inner, outer), low, high)


def first_advance_kernel(*refs):
    t, s, u, v, mask, x, pred, packed = refs[:8]
    halo = around(*refs[8:12])
    t_out, s_out, x_out, target, inner, outer, near, far = refs[12:20]
    sums, blocks, *taps = refs[20:24]
    t_here, s_here, u_here, v_here, semaphore = refs[24:]
    here = (t_here, s_here, u_here, v_here)
    copies = fetch(list(zip((t, s, u, v), here)), semaphore)
    force = forcing(x, pred, packed, halo, taps)
    for copy in copies:
        copy.wait()
    advance(*here, mask, force, halo, halo, t_out, s_out)
    fill_blocks(blocks, (t_out, s_out, u_here, v_here))
    coarsen(blocks, sums, x_out, target)
    fill_edges(blocks, 2, None, x_out, inner, outer)
    fill_columns(blocks, (0, 1), None, near, far)


def next_advance_kernel(*refs):
    t, s, u, v, mask, x, pred, packed = refs[:8]
    fixed, moving = around(*refs[8:12]), around(*refs[12:16])
    t_out, s_out, *taps = refs[16:]
    force = forcing(x, pred, packed, moving, taps)
    advance(t, s, u, v, mask, force, fixed, moving, t_out, s_out)


def swap_lon(inner, outer):
    axis = ("lon", "grp")
    count = lax.axis_size("lon") * lax.axis_size("grp")
    chips = [(i, (i + (1 if i % 2 else -1)) % count) for i in range(count)]
    outer = lax.ppermute(outer, axis, chips)
    return lax.ppermute(inner, "grp", flipped("grp", 1)), outer


def swap_lat(near, far):
    last = lax.axis_size("lat") - 1
    beyond = [(i, i ^ 3) for i in range(1, last)]
    return lax.ppermute(near, "lat", flipped("lat", 1)), lax.ppermute(far, "lat", beyond)


def south_north(near, far):
    lat = lax.axis_index("lat")
    odd = lat % 2 == 1
    south, north = jnp.where(odd, near, far), jnp.where(odd, far, near)
    south = jnp.where(lat == 0, 0.0, south)
    return south, jnp.where(lat == lax.axis_size("lat") - 1, 0.0, north)


def flipped(axis, mask):
    return [(i, i ^ mask) for i in range(lax.axis_size(axis))]


def from_chip(value, mask):
    count = lax.axis_size("lon") * lax.axis_size("lat")
    return lax.ppermute(value, ("lon", "lat"), [(i, i ^ mask) for i in range(count)])


def sum_of_four(part, bit):
    if lax.axis_size("lon") * lax.axis_size("lat") <= 2 * bit:
        return part
    one, two, three = (from_chip(part, bit * step) for step in (1, 2, 3))
    return (part + one) + (two + three)


def sum_over_devices(own, other, after_pair, riders):
    rows = own.shape[0]
    part = own + lax.ppermute(other, "grp", flipped("grp", 1))
    part = after_pair(part + from_chip(part, 4))
    for bit in (8, 32):
        part = sum_of_four(part, bit)
    near, far = riders()
    near = from_chip(jnp.concatenate([part, *near], 0), 1)
    cross = from_chip(part, 6)
    far = from_chip(jnp.concatenate([part, *far], 0), 3)
    part = (part + near[:rows]) + (cross + far[:rows])
    back = lax.ppermute(part, "grp", flipped("grp", 1))
    return part, back, (near[rows:], far[rows:])


def shards(
    thermal_anomaly,
    saltiness_anomaly,
    zonal_flow_speed,
    meridional_flow_speed,
    water_indicator,
    kernel_factors,
    hidden_pointwise_factors,
    final_pointwise_factors,
):
    fields = tuple(
        value.reshape(8 * LEVELS, FINE)
        for value in (thermal_anomaly, saltiness_anomaly, zonal_flow_speed, meridional_flow_speed)
    )
    packed = jnp.concatenate(
        [
            kernel_factors.reshape(HIDDEN, TAPS),
            hidden_pointwise_factors,
            final_pointwise_factors.T,
            jnp.zeros((HIDDEN, PACKED - USED), f32),
        ],
        1,
    )
    blocks = pltpu.VMEM((16 * 8 * LEVELS, 128), f32)
    field_scratch = pltpu.VMEM((8 * LEVELS, FINE), f32)
    sums = [pltpu.VMEM((4 * CHANNELS, FINE), f32), pltpu.VMEM((16 * 8 * LEVELS, 128), f32)]
    wide = struct(2 * CHANNELS, COARSE)
    tile = struct(8, 128)
    with_area, without = struct(SUMMED + 8, 128), struct(SUMMED, 128)
    field = struct(8 * LEVELS, FINE)
    network_scratch = [pltpu.VMEM((TAPS, 2 * COARSE), bf16)] * 2 + [pltpu.VMEM((HIDDEN, PACKED), f32)]
    side_taps = [pltpu.VMEM((TAPS, 3 * COARSE), bf16)] * 2

    edge = struct(2 * CHANNELS + 160, 128)
    x, target, weight, mask, inner, outer = call(
        prepare_kernel,
        [wide, wide, tile, struct(8, FINE), edge, edge],
        *fields, water_indicator,
        scratch=sums + [pltpu.VMEM((8, FINE), jnp.int32), pltpu.SemaphoreType.DMA((17,))],
        remote=5,
    )
    near, far = call(
        fine_columns_kernel,
        [tile, tile],
        *fields[:2], fields[3], mask,
        scratch=[sums[1], pltpu.SemaphoreType.DMA((12,))],
        remote=3,
    )

    def columns(x, inner, outer, near, far):
        return call(columns_kernel, [struct(16, 128)] * 2, x, inner, outer, near, far)

    (inner, outer), packed = lax.optimization_barrier((swap_lon(inner, outer), packed))
    south, north = south_north(*swap_lat(*columns(x, inner, outer, near, far)))
    pred, own, other = call(
        network_step,
        [wide, with_area, with_area],
        x, inner, outer, south, north, target, weight, packed,
        scratch=network_scratch,
    )
    edge = struct(2 * CHANNELS + 96, 128)
    later = {}

    fixed = inner, outer, south, north

    def first_advance(part):
        t, s, x_next, target, inner, outer, near, far = call(
            first_advance_kernel,
            [field, field, wide, wide, edge, edge, tile, tile],
            *fields, mask, x, pred, packed, *fixed,
            scratch=sums + side_taps + [field_scratch] * 4 + [pltpu.SemaphoreType.DMA((4,))],
            remote=4,
        )
        part, inner, outer = lax.optimization_barrier((part, inner, outer))
        later["state"] = t, s, x_next, target
        later["beside"] = swap_lon(inner, outer)
        later["columns"] = near, far
        return part

    def first_riders():
        x_next = later["state"][2]
        near, far = columns(x_next, *later["beside"], *later["columns"])
        return [near], [far]

    part, back, received = sum_over_devices(own, other, first_advance, first_riders)
    moving = *later["beside"], *south_north(*received)
    t, s, x, target = later["state"]
    packed, pred, own, other = call(
        next_network_kernel,
        [struct(HIDDEN, PACKED), wide, without, without],
        x, *moving, target, weight, packed, part, back,
        scratch=network_scratch,
    )

    def next_advance(part):
        fields_next = call(
            next_advance_kernel,
            [field, field],
            t, s, *fields[2:], mask, x, pred, packed, *fixed, *moving,
            scratch=side_taps,
        )
        part, *later["fields"] = lax.optimization_barrier((part, *fields_next))
        return part

    first_part = part
    part = own + lax.ppermute(other, "grp", flipped("grp", 1))
    part = sum_of_four(part, 32)
    part = next_advance(sum_of_four(part, 8))
    one, two, three = (from_chip(part, mask) for mask in (4, 1, 5))
    part = (part + one) + (two + three)
    part = part + from_chip(part, 3)
    back = lax.ppermute(part, "grp", flipped("grp", 1))
    t, s = later["fields"]
    kernel, mix, out = call(
        last_kernel,
        [struct(TAPS, HIDDEN), struct(HIDDEN, HIDDEN), struct(CHANNELS, HIDDEN)],
        packed, part, back, first_part,
    )
    return (
        t.reshape(thermal_anomaly.shape),
        s.reshape(thermal_anomaly.shape),
        kernel.T.reshape(kernel_factors.shape),
        mix,
        out,
    )


def solution(mesh):
    field = P(None, ("lon", "grp"), "lat")
    return jax.shard_map(
        shards,
        mesh=mesh,
        in_specs=(field, field, field, field, P(("lon", "grp"), "lat"), P(), P(), P()),
        out_specs=(field, field, P(), P(), P()),
        check_vma=False,
    )
```

```python
import functools

import jax
import jax.numpy as jnp
from jax import lax
from jax.experimental import pallas as pl
from jax.experimental.pallas import tpu as pltpu
from jax.sharding import PartitionSpec as P

time_step = 0.2
diffusivity = 0.5
learn_rate = 200.0
f32 = jnp.float32
bf16 = jnp.bfloat16

LEVELS = 12
CHANNELS = 4 * LEVELS
HIDDEN = 64
TAPS = 9 * CHANNELS
MIX_AT = 432
OUT_AT = 496
REST_AT = 512
USED = 544
PACKED = 640
HALF = HIDDEN // 2
SUMMED = 4 * HALF + 8
FINE = 512
COARSE = 128
VMEM_LIMIT = 48 * 1024 * 1024


def struct(*shape):
    return jax.ShapeDtypeStruct(shape, f32)


def call(kernel, outs, *args, scratch=(), remote=0, flops=0, bytes_accessed=0):
    args = [
        pltpu.with_memory_space_constraint(arg, pltpu.HBM) if at < remote else arg
        for at, arg in enumerate(args)
    ]
    specs = []
    specs += [pl.BlockSpec(memory_space=pltpu.HBM)] * remote
    specs += [pl.BlockSpec(memory_space=pltpu.VMEM)] * (len(args) - remote)
    return pl.pallas_call(
        kernel,
        out_shape=outs,
        in_specs=specs,
        out_specs=[pl.BlockSpec(memory_space=pltpu.VMEM)] * len(outs),
        scratch_shapes=scratch,
        compiler_params=pltpu.CompilerParams(vmem_limit_bytes=VMEM_LIMIT),
        cost_estimate=pl.CostEstimate(
            flops=flops, bytes_accessed=bytes_accessed, transcendentals=0
        ),
    )(*args)


def exact_dot(value, selector):
    high = value.astype(bf16)
    rest = value - high.astype(f32)
    middle = rest.astype(bf16)
    low = (rest - middle.astype(f32)).astype(bf16)
    dot = functools.partial(jnp.dot, preferred_element_type=f32)
    return (dot(low, selector) + dot(middle, selector)) + dot(high, selector)


def pooling_matrix():
    fine = lax.broadcasted_iota(jnp.int32, (FINE, COARSE), 0) >> 2
    coarse = lax.broadcasted_iota(jnp.int32, (FINE, COARSE), 1)
    return jnp.where(fine == coarse, f32(1.0 / 16.0), f32(0.0)).astype(bf16)


def spreading_matrix():
    fine = lax.broadcasted_iota(jnp.int32, (COARSE, FINE), 1) >> 2
    coarse = lax.broadcasted_iota(jnp.int32, (COARSE, FINE), 0)
    return jnp.where(fine == coarse, f32(1.0), f32(0.0)).astype(bf16)


def lane_index(shape):
    return lax.broadcasted_iota(jnp.int32, shape, len(shape) - 1)


def block_rows(which, block):
    start = (4 * which + block) * 8 * LEVELS
    return slice(start, start + 8 * LEVELS)


def fill_blocks(blocks, refs):
    for which, ref in enumerate(refs):
        for block in range(4):
            blocks[block_rows(which, block), :] = ref[:, 128 * block : 128 * (block + 1)]


def fetch(pairs, semaphore):
    copies = [
        pltpu.make_async_copy(source, target, semaphore.at[at])
        for at, (source, target) in enumerate(pairs)
    ]
    for copy in copies:
        copy.start()
    return copies


def longitude_row(blocks, which, block, lon):
    return blocks[pl.ds(block_rows(which, block).start + lon, LEVELS, stride=8), :]


def coarsen(blocks, sums_ref, x_ref, target_ref):
    for row in range(2):
        for block in range(4):
            total = None
            for lon in range(4 * row, 4 * row + 4):
                t, s, u, v = (longitude_row(blocks, which, block, lon) for which in range(4))
                terms = (t, s, u, v, u * t, v * t, u * s, v * s)
                total = terms if total is None else [a + b for a, b in zip(total, terms)]
            for at, value in enumerate(total):
                start = 2 * CHANNELS * row + LEVELS * at
                sums_ref[start : start + LEVELS, 128 * block : 128 * (block + 1)] = value
    means = exact_dot(sums_ref[...], pooling_matrix())
    for row in range(2):
        x = means[2 * CHANNELS * row : 2 * CHANNELS * row + CHANNELS]
        products = means[2 * CHANNELS * row + CHANNELS : 2 * CHANNELS * (row + 1)]
        ct, cs, cu, cv = (x[LEVELS * k : LEVELS * (k + 1)] for k in range(4))
        x_ref[CHANNELS * row : CHANNELS * (row + 1), :] = x
        own = jnp.concatenate([cu * ct, cv * ct, cu * cs, cv * cs], 0)
        target_ref[CHANNELS * row : CHANNELS * (row + 1), :] = products - own


class Either:
    def __init__(self, flag, one, other):
        self.flag, self.one, self.other, self.shape = flag, one, other, one.shape

    def __getitem__(self, at):
        return jnp.where(self.flag, self.one[at], self.other[at])


def sides(inner, outer):
    first = lax.axis_index("grp") == 0
    return Either(first, outer, inner), Either(first, inner, outer)


def edge_layout(ref):
    first = 2 * CHANNELS
    return first, (ref.shape[0] - first) // 4


def fill_edges(blocks, fields, mask_ref, x_ref, inner_ref, outer_ref):
    core_first = lax.axis_index("grp") == 0
    first_row, depth = edge_layout(inner_ref)
    for out in (inner_ref, outer_ref):
        out[0:first_row, :] = x_ref[...]
        out[first_row:, :] = jnp.zeros((out.shape[0] - first_row, COARSE), f32)

    def put(rows, first, last):
        inner_ref[rows, :] = jnp.where(core_first, last, first)
        outer_ref[rows, :] = jnp.where(core_first, first, last)

    for block in range(4):
        start = first_row + block * depth
        for which in range(fields):
            at = start + which * LEVELS
            put(
                slice(at, at + LEVELS),
                longitude_row(blocks, which, block, 0),
                longitude_row(blocks, which, block, 7),
            )
        if mask_ref is not None:
            at = start + fields * LEVELS
            lanes = slice(128 * block, 128 * (block + 1))
            put(slice(at, at + 1), mask_ref[0:1, lanes], mask_ref[7:8, lanes])


def put_columns(near_ref, far_ref, at, low, high):
    odd = lax.axis_index("lat") % 2 == 1
    near_ref[at : at + 1, 0 : low.shape[1]] = jnp.where(odd, low, high)
    far_ref[at : at + 1, 0 : low.shape[1]] = jnp.where(odd, high, low)


def fill_columns(blocks, column_fields, mask_ref, near_ref, far_ref):
    near_ref[...] = jnp.zeros(near_ref.shape, f32)
    far_ref[...] = jnp.zeros(far_ref.shape, f32)
    for at, which in enumerate(column_fields):
        low, high = (blocks[block_rows(which, block), :].T for block in (0, 3))
        put_columns(near_ref, far_ref, at, low[0:1], high[127:128])
    if mask_ref is not None:
        low, high = mask_ref[:, 0:128].T[0:1], mask_ref[:, FINE - 128 : FINE].T[127:128]
        put_columns(near_ref, far_ref, 3, low, high)


def columns_kernel(x, x_inner, x_outer, near_fine, far_fine, near, far):
    for fine, out in ((near_fine, near), (far_fine, far)):
        out[0:8, :] = fine[...]
        out[8:16, :] = jnp.zeros((8, COARSE), f32)
    rows = slice(0, 2 * CHANNELS)
    for at, ref in enumerate((x, *sides(x_inner, x_outer))):
        turned = ref[rows, :].T
        put_columns(near, far, 8 + 2 * at, turned[0:1], turned[127:128])
        put_columns(near, far, 9 + 2 * at, turned[1:2], turned[126:127])


def block_copies(refs, blocks):
    return [
        (ref.at[:, pl.ds(128 * block, 128)], blocks.at[block_rows(which, block), :])
        for which, ref in enumerate(refs)
        for block in range(4)
    ]


def prepare_kernel(
    t, s, u, v, mask, x, target, weight, mask_values, inner, outer, sums, blocks, mask_here, semaphore
):
    copies = fetch([(mask, mask_here)] + block_copies((t, s, u, v), blocks), semaphore)
    for copy in copies:
        copy.wait()
    m = mask_here[...].astype(f32)
    mask_values[...] = m
    coarsen(blocks, sums, x, target)
    fill_edges(blocks, 3, mask_values, x, inner, outer)
    rows = jnp.concatenate(
        [jnp.sum(m[0:4], axis=0, keepdims=True), jnp.sum(m[4:8], axis=0, keepdims=True)]
        + [jnp.zeros((6, FINE), f32)],
        0,
    )
    weight[...] = jnp.dot(rows.astype(bf16), pooling_matrix(), preferred_element_type=f32)


def fine_columns_kernel(t, s, v, mask, near, far, blocks, semaphore):
    for copy in fetch(block_copies((t, s, v), blocks), semaphore):
        copy.wait()
    fill_columns(blocks, (0, 1, 2), mask, near, far)


def parts_of(value):
    high = value.astype(bf16)
    return high, (value - high.astype(f32)).astype(bf16)


def dot_parts(a, b, contract):
    (a_high, a_low), (b_high, b_low) = a, b
    dims = (((1,), (contract,)), ((), ()))
    dot = functools.partial(lax.dot_general, dimension_numbers=dims, preferred_element_type=f32)
    rows = a_high.shape[0]
    both = dot(jnp.concatenate([a_high, a_low], 0), b_high)
    return both[:rows] + (both[rows:] + dot(a_high, b_low))


def column_matrix(low, high):
    rows = []
    for at in (8, 9):
        for side in range(3):
            rows += [ref[at + 2 * side : at + 2 * side + 1, :] for ref in (low, high)]
    rows.append(jnp.zeros((4, COARSE), f32))
    return jnp.concatenate(rows, 0).T


def shifted_rows(value, before, after):
    lanes = lane_index((CHANNELS, COARSE))
    return (
        jnp.where(lanes == 0, before, pltpu.roll(value, 1, 1)),
        value,
        jnp.where(lanes == COARSE - 1, after, pltpu.roll(value, COARSE - 1, 1)),
    )


def coarse_rows(x, west, east):
    return (
        (west[0:CHANNELS, :], 0, 2),
        (west[CHANNELS : 2 * CHANNELS, :], CHANNELS, 2),
        (x[0:CHANNELS, :], 0, 0),
        (x[CHANNELS : 2 * CHANNELS, :], CHANNELS, 0),
        (east[0:CHANNELS, :], 0, 4),
        (east[CHANNELS : 2 * CHANNELS, :], CHANNELS, 4),
    )


def fill_taps(taps, rows, columns, centres):
    for at, (value, start, pair) in enumerate(rows):
        if not any(abs(at - centre) <= 1 for centre in centres):
            continue
        channels = slice(start, start + CHANNELS)
        shifted = [
            parts_of(part)
            for part in shifted_rows(
                value, columns[channels, pair : pair + 1], columns[channels, pair + 1 : pair + 2]
            )
        ]
        for place, centre in enumerate(centres):
            tap = at - centre + 1
            if 0 <= tap < 3:
                for side in range(3):
                    begin = (3 * tap + side) * CHANNELS
                    for out, part in zip(taps, shifted[side]):
                        out[begin : begin + CHANNELS, COARSE * place : COARSE * (place + 1)] = part


def fill_side_taps(taps, rows, columns, start_lane):
    lanes = lane_index((CHANNELS, COARSE))
    for tap in range(3):
        for side in range(3):
            out = jnp.zeros((CHANNELS, COARSE), f32)
            for row in range(2):
                value, start, pair = rows[row + tap + 1]
                channels = slice(start, start + CHANNELS)
                low = (
                    columns[channels, 6 + pair : 7 + pair],
                    columns[channels, pair : pair + 1],
                    value[:, 0:1],
                )[side]
                high = (
                    value[:, COARSE - 1 : COARSE],
                    columns[channels, pair + 1 : pair + 2],
                    columns[channels, 7 + pair : 8 + pair],
                )[side]
                out = jnp.where(lanes == row, low, out)
                out = jnp.where(lanes == 2 + row, high, out)
            begin = (3 * tap + side) * CHANNELS
            for ref, part in zip(taps, parts_of(out)):
                ref[begin : begin + CHANNELS, start_lane : start_lane + COARSE] = part


def network_step(
    x, inner, outer, low, high, target, weight, packed, pred, own, other, taps_high, taps_low, grads
):
    west, east = sides(inner, outer)
    columns = column_matrix(low, high)
    fill_taps((taps_high, taps_low), coarse_rows(x, west, east), columns, (2, 3))
    taps = taps_high[...], taps_low[...]
    kernel = parts_of(packed[:, 0:TAPS])
    mix = packed[:, MIX_AT : MIX_AT + HIDDEN]
    out_turned = packed[:, OUT_AT : OUT_AT + CHANNELS]
    hidden_one = jnp.tanh(dot_parts(kernel, taps, 0))
    one = parts_of(hidden_one)
    hidden_two = jnp.tanh(dot_parts(parts_of(mix), one, 0))
    two = parts_of(hidden_two)
    predicted = dot_parts(parts_of(out_turned.T), two, 0)
    pred[0:CHANNELS, :] = predicted[:, 0:COARSE]
    pred[CHANNELS : 2 * CHANNELS, :] = predicted[:, COARSE : 2 * COARSE]
    back_out = parts_of(
        jnp.concatenate(
            [
                weight[row : row + 1, :]
                * (
                    predicted[:, COARSE * row : COARSE * (row + 1)]
                    - target[CHANNELS * row : CHANNELS * (row + 1), :]
                )
                for row in range(2)
            ],
            1,
        )
    )
    back_two = parts_of(
        dot_parts(parts_of(out_turned), back_out, 0) * (1.0 - hidden_two * hidden_two)
    )
    back_one = parts_of(
        dot_parts(parts_of(mix.T), back_two, 0) * (1.0 - hidden_one * hidden_one)
    )
    grads[:, 0:TAPS] = dot_parts(back_one, taps, 1)
    grads[:, MIX_AT : MIX_AT + HIDDEN] = dot_parts(back_two, one, 1)
    grads[:, OUT_AT : OUT_AT + CHANNELS] = dot_parts(two, back_out, 1)
    here = lax.axis_index("grp")
    for core, out in ((here, own), (1 - here, other)):
        start = core * HALF
        rows = pl.ds(pl.multiple_of(start, HALF), HALF)
        for block in range(4):
            out[HALF * block : HALF * (block + 1), :] = grads[rows, 128 * block : 128 * (block + 1)]
        for part in range(4):
            rows = pl.ds(pl.multiple_of(start + 8 * part, 8), 8)
            out[4 * HALF : SUMMED, 32 * part : 32 * (part + 1)] = grads[rows, REST_AT:USED]
        if out.shape[0] > SUMMED:
            area = jnp.sum(weight[0:2, :], axis=(0, 1), keepdims=True)
            out[SUMMED:, :] = jnp.broadcast_to(area, (8, 128))


def descended(packed, part, back, with_area):
    first = lax.axis_index("grp") == 0

    def whole(mine, theirs):
        return jnp.concatenate([jnp.where(first, mine, theirs), jnp.where(first, theirs, mine)], 0)

    blocks = []
    for block in range(4):
        rows = slice(HALF * block, HALF * (block + 1))
        blocks.append(whole(part[rows, :], back[rows, :]))
    rest = [
        jnp.concatenate([ref[4 * HALF : SUMMED, 32 * at : 32 * (at + 1)] for at in range(4)], 0)
        for ref in (part, back)
    ]
    blocks += [whole(*rest), jnp.zeros((HIDDEN, PACKED - USED), f32)]
    step = (learn_rate * 2.0 / CHANNELS) / with_area[SUMMED : SUMMED + 1, 0:1]
    return packed[...] - step * jnp.concatenate(blocks, 1)


def next_network_kernel(*refs):
    *ins, packed, part, back, renewed = refs[:11]
    renewed[...] = descended(packed, part, back, part)
    network_step(*ins, renewed, *refs[11:])


def last_kernel(packed, part, back, with_area, kernel, mix, out):
    renewed = descended(packed, part, back, with_area)
    kernel[...] = renewed[:, 0:TAPS].T
    mix[...] = renewed[:, MIX_AT : MIX_AT + HIDDEN]
    out[...] = renewed[:, OUT_AT : OUT_AT + CHANNELS].T


def forcing(x, pred, packed, halo, taps):
    west, east, low, high = halo
    rows = coarse_rows(x, west, east)
    columns = column_matrix(low, high)
    fill_taps(taps, rows, columns, (1, 4))
    fill_side_taps(taps, rows, columns, 2 * COARSE)
    inputs = tuple(ref[...] for ref in taps)
    hidden = jnp.tanh(dot_parts(parts_of(packed[:, 0:TAPS]), inputs, 0))
    hidden = jnp.tanh(
        dot_parts(parts_of(packed[:, MIX_AT : MIX_AT + HIDDEN]), parts_of(hidden), 0)
    )
    beside = dot_parts(
        parts_of(packed[:, OUT_AT : OUT_AT + CHANNELS].T), parts_of(hidden), 0
    )
    sides = beside[:, 2 * COARSE :]
    lat = lax.axis_index("lat")
    sides_low = jnp.where(lat == 0, 0.0, sides)
    sides_high = jnp.where(lat == lax.axis_size("lat") - 1, 0.0, sides)
    before = (beside[:, 0:COARSE], pred[0:CHANNELS, :])
    after = (pred[CHANNELS : 2 * CHANNELS, :], beside[:, COARSE : 2 * COARSE])
    pieces = []
    for row in range(2):
        value = pred[CHANNELS * row : CHANNELS * (row + 1), :]
        along = after[row] - before[row]
        south, _, north = shifted_rows(value, sides_low[:, row : row + 1], sides_high[:, 2 + row : 3 + row])
        across = north - south
        for at in (0, 2 * LEVELS):
            pieces.append(-0.5 * (along[at : at + LEVELS] + across[at + LEVELS : at + 2 * LEVELS]))
            pieces.append(jnp.zeros((4, COARSE), f32))
    return exact_dot(jnp.concatenate(pieces, 0), spreading_matrix())


def advance(t, s, u, v, mask, force, fixed, moving, t_out, s_out):
    fixed_west, fixed_east, fixed_low, fixed_high = fixed
    west, east, low, high = moving
    m = mask[...]
    shape = (8, FINE)
    lanes = lane_index(shape)
    subs = lax.broadcasted_iota(jnp.int32, shape, 0)

    def edge_row(ref, at):
        first, depth = edge_layout(ref)
        starts = [first + depth * block + at for block in range(4)]
        return jnp.concatenate([ref[start : start + 1, :] for start in starts], 1)

    def neighbours_lon(value, row_west, row_east):
        return (
            jnp.where(subs == 0, row_west, pltpu.roll(value, 1, 0)),
            jnp.where(subs == 7, row_east, pltpu.roll(value, 7, 0)),
        )

    def neighbours_lat(value, column_low, column_high):
        return (
            jnp.where(lanes == 0, column_low, pltpu.roll(value, 1, 1)),
            jnp.where(lanes == FINE - 1, column_high, pltpu.roll(value, FINE - 1, 1)),
        )

    fixed_low_turned = fixed_low[...].T
    fixed_high_turned = fixed_high[...].T
    low_turned = low[...].T
    high_turned = high[...].T
    m_west, m_east = neighbours_lon(
        m, edge_row(fixed_west, 3 * LEVELS), edge_row(fixed_east, 3 * LEVELS)
    )
    m_low, m_high = neighbours_lat(m, fixed_low_turned[0:8, 3:4], fixed_high_turned[0:8, 3:4])
    open_west, open_east, open_low, open_high = m * m_west, m * m_east, m * m_low, m * m_high
    mix_west, mix_east = diffusivity * open_west, diffusivity * open_east
    mix_low, mix_high = diffusivity * open_low, diffusivity * open_high
    pace = time_step * m
    for level in range(LEVELS):
        at = slice(8 * level, 8 * (level + 1))
        u_here, v_here = u[at, :], v[at, :]
        u_west, u_east = neighbours_lon(
            u_here, edge_row(fixed_west, 2 * LEVELS + level), edge_row(fixed_east, 2 * LEVELS + level)
        )
        v_low, v_high = neighbours_lat(v_here, fixed_low_turned[at, 2:3], fixed_high_turned[at, 2:3])
        speed_west = 0.25 * (u_here + u_west) * open_west
        speed_east = 0.25 * (u_here + u_east) * open_east
        speed_low = 0.25 * (v_here + v_low) * open_low
        speed_high = 0.25 * (v_here + v_high) * open_high
        for which, (q_ref, out) in enumerate(((t, t_out), (s, s_out))):
            q = q_ref[at, :]
            q_west, q_east = neighbours_lon(
                q, edge_row(west, LEVELS * which + level), edge_row(east, LEVELS * which + level)
            )
            q_low, q_high = neighbours_lat(
                q, low_turned[at, which : which + 1], high_turned[at, which : which + 1]
            )
            flux_east = speed_east * (q + q_east) - mix_east * (q_east - q)
            flux_west = speed_west * (q_west + q) - mix_west * (q - q_west)
            flux_high = speed_high * (q + q_high) - mix_high * (q_high - q)
            flux_low = speed_low * (q_low + q) - mix_low * (q - q_low)
            row = 16 * which + level
            push = jnp.where(subs < 4, force[row : row + 1], force[32 + row : 33 + row])
            out[at, :] = q + pace * (push - (flux_east - flux_west) - (flux_high - flux_low))


def around(inner, outer, low, high):
    return (*sides(inner, outer), low, high)


def first_advance_kernel(*refs):
    t, s, u, v, mask, x, pred, packed = refs[:8]
    halo = around(*refs[8:12])
    t_out, s_out, x_out, target, inner, outer, near, far = refs[12:20]
    sums, blocks, *taps = refs[20:24]
    t_here, s_here, u_here, v_here, semaphore = refs[24:]
    here = (t_here, s_here, u_here, v_here)
    copies = fetch(list(zip((t, s, u, v), here)), semaphore)
    force = forcing(x, pred, packed, halo, taps)
    for copy in copies:
        copy.wait()
    advance(*here, mask, force, halo, halo, t_out, s_out)
    fill_blocks(blocks, (t_out, s_out, u_here, v_here))
    coarsen(blocks, sums, x_out, target)
    fill_edges(blocks, 2, None, x_out, inner, outer)
    fill_columns(blocks, (0, 1), None, near, far)


def next_advance_kernel(*refs):
    t, s, u, v, mask, x, pred, packed = refs[:8]
    fixed, moving = around(*refs[8:12]), around(*refs[12:16])
    t_out, s_out, *taps = refs[16:]
    force = forcing(x, pred, packed, moving, taps)
    advance(t, s, u, v, mask, force, fixed, moving, t_out, s_out)


def swap_lon(inner, outer):
    axis = ("lon", "grp")
    count = lax.axis_size("lon") * lax.axis_size("grp")
    chips = [(i, (i + (1 if i % 2 else -1)) % count) for i in range(count)]
    outer = lax.ppermute(outer, axis, chips)
    return lax.ppermute(inner, "grp", flipped("grp", 1)), outer


def swap_lat(near, far):
    last = lax.axis_size("lat") - 1
    beyond = [(i, i ^ 3) for i in range(1, last)]
    return lax.ppermute(near, "lat", flipped("lat", 1)), lax.ppermute(far, "lat", beyond)


def south_north(near, far):
    lat = lax.axis_index("lat")
    odd = lat % 2 == 1
    south, north = jnp.where(odd, near, far), jnp.where(odd, far, near)
    south = jnp.where(lat == 0, 0.0, south)
    return south, jnp.where(lat == lax.axis_size("lat") - 1, 0.0, north)


def flipped(axis, mask):
    return [(i, i ^ mask) for i in range(lax.axis_size(axis))]


def from_chip(value, mask):
    count = lax.axis_size("lon") * lax.axis_size("lat")
    return lax.ppermute(value, ("lon", "lat"), [(i, i ^ mask) for i in range(count)])


def sum_of_four(part, bit):
    if lax.axis_size("lon") * lax.axis_size("lat") <= 2 * bit:
        return part
    one, two, three = (from_chip(part, bit * step) for step in (1, 2, 3))
    return (part + one) + (two + three)


def sum_over_devices(own, other, after_pair, riders):
    rows = own.shape[0]
    part = own + lax.ppermute(other, "grp", flipped("grp", 1))
    part = after_pair(part + from_chip(part, 4))
    for bit in (8, 32):
        part = sum_of_four(part, bit)
    near, far = riders()
    near = from_chip(jnp.concatenate([part, *near], 0), 1)
    cross = from_chip(part, 6)
    far = from_chip(jnp.concatenate([part, *far], 0), 3)
    part = (part + near[:rows]) + (cross + far[:rows])
    back = lax.ppermute(part, "grp", flipped("grp", 1))
    return part, back, (near[rows:], far[rows:])


def shards(
    thermal_anomaly,
    saltiness_anomaly,
    zonal_flow_speed,
    meridional_flow_speed,
    water_indicator,
    kernel_factors,
    hidden_pointwise_factors,
    final_pointwise_factors,
):
    fields = tuple(
        value.reshape(8 * LEVELS, FINE)
        for value in (thermal_anomaly, saltiness_anomaly, zonal_flow_speed, meridional_flow_speed)
    )
    packed = jnp.concatenate(
        [
            kernel_factors.reshape(HIDDEN, TAPS),
            hidden_pointwise_factors,
            final_pointwise_factors.T,
            jnp.zeros((HIDDEN, PACKED - USED), f32),
        ],
        1,
    )
    blocks = pltpu.VMEM((16 * 8 * LEVELS, 128), f32)
    field_scratch = pltpu.VMEM((8 * LEVELS, FINE), f32)
    sums = [pltpu.VMEM((4 * CHANNELS, FINE), f32), pltpu.VMEM((16 * 8 * LEVELS + 64, 128), f32)]
    wide = struct(2 * CHANNELS, COARSE)
    tile = struct(8, 128)
    with_area, without = struct(SUMMED + 8, 128), struct(SUMMED, 128)
    field = struct(8 * LEVELS, FINE)
    network_scratch = [pltpu.VMEM((TAPS, 2 * COARSE), bf16)] * 2 + [pltpu.VMEM((HIDDEN, PACKED), f32)]
    side_taps = [pltpu.VMEM((TAPS, 3 * COARSE), bf16)] * 2

    edge = struct(2 * CHANNELS + 160, 128)
    x, target, weight, mask, inner, outer = call(
        prepare_kernel,
        [wide, wide, tile, struct(8, FINE), edge, edge],
        *fields, water_indicator,
        scratch=sums + [pltpu.VMEM((8, FINE), jnp.int32), pltpu.SemaphoreType.DMA((17,))],
        remote=5,
    )
    near, far = call(
        fine_columns_kernel,
        [tile, tile],
        *fields[:2], fields[3], mask,
        scratch=[sums[1], pltpu.SemaphoreType.DMA((12,))],
        remote=3,
    )

    def columns(x, inner, outer, near, far):
        return call(columns_kernel, [struct(16, 128)] * 2, x, inner, outer, near, far)

    (inner, outer), packed = lax.optimization_barrier((swap_lon(inner, outer), packed))
    south, north = south_north(*swap_lat(*columns(x, inner, outer, near, far)))
    pred, own, other = call(
        network_step,
        [wide, with_area, with_area],
        x, inner, outer, south, north, target, weight, packed,
        scratch=network_scratch,
    )
    edge = struct(2 * CHANNELS + 96, 128)
    later = {}

    fixed = inner, outer, south, north

    def first_advance(part):
        t, s, x_next, target, inner, outer, near, far = call(
            first_advance_kernel,
            [field, field, wide, wide, edge, edge, tile, tile],
            *fields, mask, x, pred, packed, *fixed,
            scratch=sums + side_taps + [field_scratch] * 4 + [pltpu.SemaphoreType.DMA((4,))],
            remote=4,
        )
        part, inner, outer = lax.optimization_barrier((part, inner, outer))
        later["state"] = t, s, x_next, target
        later["beside"] = swap_lon(inner, outer)
        later["columns"] = near, far
        return part

    def first_riders():
        x_next = later["state"][2]
        near, far = columns(x_next, *later["beside"], *later["columns"])
        return [near], [far]

    part, back, received = sum_over_devices(own, other, first_advance, first_riders)
    moving = *later["beside"], *south_north(*received)
    t, s, x, target = later["state"]
    packed, pred, own, other = call(
        next_network_kernel,
        [struct(HIDDEN, PACKED), wide, without, without],
        x, *moving, target, weight, packed, part, back,
        scratch=network_scratch,
    )

    def next_advance(part):
        fields_next = call(
            next_advance_kernel,
            [field, field],
            t, s, *fields[2:], mask, x, pred, packed, *fixed, *moving,
            scratch=side_taps,
        )
        part, *later["fields"] = lax.optimization_barrier((part, *fields_next))
        return part

    first_part = part
    part = own + lax.ppermute(other, "grp", flipped("grp", 1))
    part = sum_of_four(part, 32)
    part = next_advance(sum_of_four(part, 8))
    one, two, three = (from_chip(part, mask) for mask in (4, 1, 5))
    part = (part + one) + (two + three)
    part = part + from_chip(part, 3)
    back = lax.ppermute(part, "grp", flipped("grp", 1))
    t, s = later["fields"]
    kernel, mix, out = call(
        last_kernel,
        [struct(TAPS, HIDDEN), struct(HIDDEN, HIDDEN), struct(CHANNELS, HIDDEN)],
        packed, part, back, first_part,
    )
    return (
        t.reshape(thermal_anomaly.shape),
        s.reshape(thermal_anomaly.shape),
        kernel.T.reshape(kernel_factors.shape),
        mix,
        out,
    )


def solution(mesh):
    field = P(None, ("lon", "grp"), "lat")
    return jax.shard_map(
        shards,
        mesh=mesh,
        in_specs=(field, field, field, field, P(("lon", "grp"), "lat"), P(), P(), P()),
        out_specs=(field, field, P(), P(), P()),
        check_vma=False,
    )
```
